32 devices in a mesh: dp: 16 (over z, y, x), tensor: 2 (over core).
Axes of the slice: x: 2, y: 2, z: 4, core: 2. Of those that a mesh axis runs over, the one named last changes fastest.
Arguments:
- decoder_input: bfloat16 [16, 1024, 768], P('dp'), may hold values from -6 to 6
- encoder_output: bfloat16 [16, 512, 768], P('dp'), may hold values from -6 to 6
- cotangent: bfloat16 [16, 1024, 768], P('dp'), may hold values from -6 to 6
- target_length: int32 [16], P('dp'), may hold values from 128 to 1024, as said below
- source_length: int32 [16], P('dp'), may hold values from 128 to 512, as said below
- identifier_tags: int32 [16, 1024], P('dp'), may hold values 0 or 1
- distance_bucket: int32 [1024], replicated, may hold values from 0 to 31, as said below
- self_gain: float32 [768], replicated, may hold values from 0.5 to 1.5
- self_query: bfloat16 [768, 768], P(None, 'tensor'), may hold values from -0.0546875 to 0.0546875
- self_attention_key: bfloat16 [768, 768], P(None, 'tensor'), may hold values from -0.21875 to 0.21875
- self_value: bfloat16 [768, 768], P(None, 'tensor'), may hold values from -0.21875 to 0.21875
- self_output: bfloat16 [768, 768], P('tensor'), may hold values from -1.25 to 1.25
- position_table: float32 [32, 12], P(None, 'tensor'), may hold values from -4 to 4
- cross_gain: float32 [768], replicated, may hold values from 0.5 to 1.5
- cross_query: bfloat16 [768, 768], P(None, 'tensor'), may hold values from -0.0546875 to 0.0546875
- cross_key: bfloat16 [768, 768], P(None, 'tensor'), may hold values from -0.21875 to 0.21875
- cross_value: bfloat16 [768, 768], P(None, 'tensor'), may hold values from -0.21875 to 0.21875
- cross_output: bfloat16 [768, 768], P('tensor'), may hold values from -1.25 to 1.25
- hidden_gain: float32 [768], replicated, may hold values from 0.5 to 1.5
- hidden_in: bfloat16 [768, 3072], P(None, 'tensor'), may hold values from -0.21875 to 0.21875
- hidden_out: bfloat16 [3072, 768], P('tensor'), may hold values from -0.109375 to 0.109375
Outputs:
- layer_out: bfloat16 [16, 1024, 768], P('dp')
- grad_decoder: float32 [16, 1024, 768], P('dp')
- grad_encoder: float32 [16, 512, 768], P('dp')
- grad_self_gain: float32 [768], replicated
- grad_self_query: float32 [768, 768], P(None, 'tensor')
- grad_self_key: float32 [768, 768], P(None, 'tensor')
- grad_self_value: float32 [768, 768], P(None, 'tensor')
- grad_self_output: float32 [768, 768], P('tensor')
- grad_position_table: float32 [32, 12], P(None, 'tensor')
- grad_cross_gain: float32 [768], replicated
- grad_cross_query: float32 [768, 768], P(None, 'tensor')
- grad_cross_key: float32 [768, 768], P(None, 'tensor')
- grad_cross_value: float32 [768, 768], P(None, 'tensor')
- grad_cross_output: float32 [768, 768], P('tensor')
- grad_hidden_gain: float32 [768], replicated
- grad_hidden_in: float32 [768, 3072], P(None, 'tensor')
- grad_hidden_out: float32 [3072, 768], P('tensor')
The draws below stay inside these ranges and needn't reach their ends.
Inputs may be any that keep to these rules, and one draw needn't show every extreme that they name: `target_length`: some item has 1024 target tokens in every draw. `source_length`: some item has 512 encoder tokens in every draw. `distance_bucket`: Non-decreasing in the distance; equal to the distance below 16; 31 at distance 1024 - 1.
All inputs are finite; a program needn't handle non-finite values. No bound on the sum of `identifier_tags` on one device may be relied on, other than what follows from the above.
Results may differ from the reference program's by a relative error of at most 0.024.
The reference program's roundings to bfloat16 on the way count: a program that leaves them out, or rounds other values in their place, can miss the bound.
Values sent between devices are 32-bit elements; how exact they have to be, the bound alone decides.
No kernel may reach another device: no remote copies, remote signals or barrier semaphores. Data moves between devices by JAX's collectives and lax.ppermute only.
A program may use at most 256 MiB of HBM per device.

```python
import jax
import jax.numpy as jnp
from jax import lax

D = 768
H = 12
HD = 64
FF = 3072
NB = 32
TGT = 1024
SRC = 512
ITEMS = 16


def draw_target_length(key, part):
    key = jax.random.fold_in(key, 11)
    key_lengths, key_choice = jax.random.split(key)
    lengths = jax.random.randint(key_lengths, (ITEMS,), TGT // 8, TGT + 1, dtype=jnp.int32)
    chosen = jax.random.randint(key_choice, (), 0, ITEMS, dtype=jnp.int32)
    return jnp.where(jnp.arange(ITEMS, dtype=jnp.int32) == chosen, TGT, lengths).astype(jnp.int32)


def draw_source_length(key, part):
    key = jax.random.fold_in(key, 23)
    key_lengths, key_choice = jax.random.split(key)
    lengths = jax.random.randint(key_lengths, (ITEMS,), SRC // 4, SRC + 1, dtype=jnp.int32)
    chosen = jax.random.randint(key_choice, (), 0, ITEMS, dtype=jnp.int32)
    return jnp.where(jnp.arange(ITEMS, dtype=jnp.int32) == chosen, SRC, lengths).astype(jnp.int32)


def draw_distance_bucket(key, part):
    key = jax.random.fold_in(key, 37)
    distance = jnp.arange(TGT, dtype=jnp.int32)
    rolled = jax.random.randint(key, (TGT,), 0, 8, dtype=jnp.int32)
    steps_up = jnp.where((rolled == 0) & (distance > NB // 2), 1, 0).astype(jnp.int32)
    stair = NB // 2 + jnp.cumsum(steps_up).astype(jnp.int32)
    bucket = jnp.where(distance < NB // 2, distance, jnp.minimum(stair, NB - 1))
    return jnp.where(distance == TGT - 1, NB - 1, bucket).astype(jnp.int32)


def set_ends(array, key, least, largest):
    place = [jax.random.randint(jax.random.fold_in(key, axis), (), 0, length) for axis, length in enumerate(array.shape)]
    widest = array.shape.index(max(array.shape))
    next_to = place[:widest] + [(place[widest] + 1) % array.shape[widest]] + place[widest + 1:]
    return array.at[tuple(place)].set(least).at[tuple(next_to)].set(largest)


def level_of(key, shape, shards, smallest, high):
    def one(axis_at, shards_of):
        draws = jax.random.uniform(jax.random.fold_in(jax.random.fold_in(key, 6), axis_at), (shards_of,), jnp.float32, smallest / len(shards), high / len(shards))
        return jnp.repeat(jnp.exp(draws), shape[axis_at] // shards_of).reshape((-1,) + (1,) * (len(shape) - axis_at - 1))

    gain = one(*shards[0])
    for cut in shards[1:]:
        gain = gain * one(*cut)
    return gain


def scatter_about(key, extent, deviation, bound, cuts=(), kind=jnp.bfloat16):
    values = jax.random.normal(key, extent, jnp.float32) * deviation
    if len(cuts) > 0:
        values = level_of(key, extent, cuts, -0.22, 0.18) * values
    return jnp.clip(values, min=-bound, max=bound).astype(kind)


def setup_inputs(seed: int = 0) -> dict:
    seeds = jax.random.split(jax.random.key(seed), 22)
    decoder_input = scatter_about(seeds[0], (ITEMS, TGT, D), 1.0, 6.0, ((0, 16),))
    encoder_output = scatter_about(seeds[1], (ITEMS, SRC, D), 1.0, 6.0, ((0, 16),))
    cotangent = scatter_about(seeds[2], (ITEMS, TGT, D), 1.0, 6.0, ((0, 16),))
    target_length = draw_target_length(jax.random.fold_in(seeds[21], 71), 0)
    source_length = draw_source_length(jax.random.fold_in(seeds[21], 71), 0)
    identifier_tags = set_ends((jax.random.randint(seeds[5], (ITEMS, TGT), 0, 4) < 1).astype(jnp.int32), jax.random.fold_in(seeds[5], 1), 0, 1)
    distance_bucket = draw_distance_bucket(jax.random.fold_in(seeds[21], 71), 0)
    self_gain = jnp.clip(1.0 + 0.1 * jax.random.normal(seeds[7], (D,), jnp.float32), 0.5, 1.5)
    self_query = scatter_about(seeds[8], (D, H * HD), (D * 16) ** -0.5, 0.0546875, ((1, 2),))
    self_attention_key = scatter_about(seeds[9], (D, H * HD), D ** -0.5, 0.21875, ((1, 2),))
    self_value = scatter_about(seeds[10], (D, H * HD), D ** -0.5, 0.21875, ((1, 2),))
    self_output = scatter_about(seeds[11], (H * HD, D), (D // 32) ** -0.5, 1.25, ((0, 2),))
    position_table = scatter_about(seeds[12], (NB, H), 1.0, 4.0, ((1, 2),), jnp.float32)
    cross_gain = jnp.clip(1.0 + 0.1 * jax.random.normal(seeds[13], (D,), jnp.float32), 0.5, 1.5)
    cross_query = scatter_about(seeds[14], (D, H * HD), (D * 16) ** -0.5, 0.0546875, ((1, 2),))
    cross_key = scatter_about(seeds[15], (D, H * HD), D ** -0.5, 0.21875, ((1, 2),))
    cross_value = scatter_about(seeds[16], (D, H * HD), D ** -0.5, 0.21875, ((1, 2),))
    cross_output = scatter_about(seeds[17], (H * HD, D), (D // 32) ** -0.5, 1.25, ((0, 2),))
    hidden_gain = jnp.clip(1.0 + 0.1 * jax.random.normal(seeds[18], (D,), jnp.float32), 0.5, 1.5)
    hidden_in = scatter_about(seeds[19], (D, FF), D ** -0.5, 0.21875, ((1, 2),))
    hidden_out = scatter_about(seeds[20], (FF, D), FF ** -0.5, 0.109375, ((0, 2),))
    return dict(decoder_input=decoder_input, encoder_output=encoder_output, cotangent=cotangent, target_length=target_length, source_length=source_length, identifier_tags=identifier_tags, distance_bucket=distance_bucket, self_gain=self_gain, self_query=self_query, self_attention_key=self_attention_key, self_value=self_value, self_output=self_output, position_table=position_table, cross_gain=cross_gain, cross_query=cross_query, cross_key=cross_key, cross_value=cross_value, cross_output=cross_output, hidden_gain=hidden_gain, hidden_in=hidden_in, hidden_out=hidden_out)


EPSILON = 1e-06
MASKED = -1e+30
FULL_ACCURACY = lax.Precision.HIGHEST

@jax.custom_vjp
def low(v):
    return lax.optimization_barrier(v.astype(jnp.bfloat16)).astype(jnp.float32)

@jax.custom_vjp
def low_back(v):
    return v

def low_keep(v):
    return (low(v), None)

def low_pass(kept, grad):
    return (grad,)

def back_keep(v):
    return (v, None)

def back_low(kept, grad):
    return (low(grad),)
low.defvjp(low_keep, low_pass)
low_back.defvjp(back_keep, back_low)

def product(former, latter):
    return jnp.dot(former, latter, precision=FULL_ACCURACY)

def rms_scale(hidden, norm_gain):
    return hidden * lax.rsqrt(lax.optimization_barrier(jnp.mean(hidden * hidden, axis=-1, keepdims=True)) + EPSILON) * norm_gain

def attention(queries, key_rows, value_rows, bias_term, allowed):
    head_width = queries.shape[1] // H
    query_heads = queries.reshape(queries.shape[0], H, head_width)
    key_heads = key_rows.reshape(key_rows.shape[0], H, head_width)
    value_heads = value_rows.reshape(value_rows.shape[0], H, head_width)
    scores = jnp.einsum('qhd,khd->hqk', query_heads, key_heads, precision=FULL_ACCURACY) + bias_term
    scores = jnp.where(allowed[None], low_back(scores), MASKED)
    row_top = lax.optimization_barrier(jnp.max(scores, axis=-1, keepdims=True))
    raised = jnp.exp(scores - row_top)
    shares = raised / lax.optimization_barrier(jnp.sum(raised, axis=-1, keepdims=True))
    mixed = jnp.einsum('hqk,khd->qhd', low(shares), value_heads, precision=FULL_ACCURACY)
    return low_back(low(mixed.reshape(queries.shape[0], H * head_width)))

def layer(weights, distance_bucket, decoder_rows, encoder_rows, target_count, source_count):
    self_gain, self_query, self_attention_key, self_value, self_output, position_table, cross_gain, cross_query, cross_key, cross_value, cross_output, hidden_gain, hidden_in, hidden_out = weights
    places = jnp.arange(TGT, dtype=jnp.int32)
    source_places = jnp.arange(SRC, dtype=jnp.int32)
    normed_one = low(rms_scale(decoder_rows, self_gain))
    queries_one = low_back(low(product(normed_one, self_query)))
    keys_one = low_back(low(product(normed_one, self_attention_key)))
    first_value_rows = low_back(low(product(normed_one, self_value)))
    distance = jnp.clip(places[:, None] - places[None, :], 0, TGT - 1)
    bias_term = jnp.transpose(position_table[distance_bucket[distance]], (2, 0, 1))
    allowed_one = (places[None, :] <= places[:, None]) & (places[None, :] < target_count)
    self_branch = low_back(product(attention(queries_one, keys_one, first_value_rows, bias_term, allowed_one), self_output))
    first = decoder_rows + self_branch
    second_normalized = low(rms_scale(first, cross_gain))
    queries_two = low_back(low(product(second_normalized, cross_query)))
    keys_two = low_back(low(product(encoder_rows, cross_key)))
    values_two = low_back(low(product(encoder_rows, cross_value)))
    allowed_two = jnp.broadcast_to(source_places[None, :] < source_count, (TGT, SRC))
    cross_branch = low_back(product(attention(queries_two, keys_two, values_two, 0.0, allowed_two), cross_output))
    second = first + cross_branch
    normed_three = low(rms_scale(second, hidden_gain))
    before = low_back(product(normed_three, hidden_in))
    active = low(jax.nn.gelu(before, approximate=True))
    hidden_branch = low_back(product(active, hidden_out))
    return second + hidden_branch

def reference(decoder_input, encoder_output, cotangent, target_length, source_length, identifier_tags, distance_bucket, self_gain, self_query, self_attention_key, self_value, self_output, position_table, cross_gain, cross_query, cross_key, cross_value, cross_output, hidden_gain, hidden_in, hidden_out):
    weights = tuple((matrix.astype(jnp.float32) for matrix in (self_gain, self_query, self_attention_key, self_value, self_output, position_table, cross_gain, cross_query, cross_key, cross_value, cross_output, hidden_gain, hidden_in, hidden_out)))

    def whole(weight_set, decoder_rows, encoder_rows):

        def single(item_args):
            return layer(weight_set, distance_bucket, item_args[0], item_args[1], item_args[2], item_args[3])
        return lax.map(jax.checkpoint(single), (decoder_rows, encoder_rows, target_length, source_length))
    decoder_rows = decoder_input.astype(jnp.float32)
    encoder_rows = encoder_output.astype(jnp.float32)
    result, pullback = jax.vjp(whole, weights, decoder_rows, encoder_rows)
    places = jnp.arange(TGT, dtype=jnp.int32)
    factor = jnp.where(places[None, :] < target_length[:, None], 1.0 + identifier_tags.astype(jnp.float32), 0.0)
    seed_grad = cotangent.astype(jnp.float32) * factor[:, :, None]
    grad_weights, grad_decoder, grad_encoder = pullback(seed_grad)
    return (result.astype(jnp.bfloat16), grad_decoder, grad_encoder, grad_weights[0], grad_weights[1], grad_weights[2], grad_weights[3], grad_weights[4], grad_weights[5], grad_weights[6], grad_weights[7], grad_weights[8], grad_weights[9], grad_weights[10], grad_weights[11], grad_weights[12], grad_weights[13])
```

```python
from functools import partial

import jax
import jax.numpy as jnp
from jax import lax
from jax.sharding import PartitionSpec as P

EPSILON = 1e-06
MASKED = -1e30
FULL_ACCURACY = lax.Precision.HIGHEST


def matrix_product(former, latter):
    return jnp.dot(former, latter, preferred_element_type=jnp.float32)


def left_contract(former, latter):
    return jnp.einsum("ti,tj->ij", former, latter, preferred_element_type=jnp.float32)


def right_contract(former, latter):
    return jnp.einsum("ti,ji->tj", former, latter, preferred_element_type=jnp.float32)


def normalize(hidden, norm_gain):
    inverse_rms = lax.rsqrt(jnp.mean(hidden * hidden, axis=-1, keepdims=True) + EPSILON)
    return (hidden * inverse_rms * norm_gain, inverse_rms)


def norm_back(hidden, inverse_rms, norm_gain, grad_normed):
    grad_gain = jnp.sum(grad_normed * hidden * inverse_rms, axis=0)
    grad_scaled = grad_normed * norm_gain
    inner_sum = jnp.mean(grad_scaled * hidden, axis=-1, keepdims=True)
    cubed = inverse_rms * inverse_rms * inverse_rms
    return (inverse_rms * grad_scaled - hidden * cubed * inner_sum, grad_gain)


def bucket_table(distance_bucket, block_start, row_count, key_total, bucket_total):
    bucket_ids = jnp.arange(bucket_total + 1, dtype=jnp.int32)
    starts = jnp.sum((distance_bucket[None, :] < bucket_ids[:, None]).astype(jnp.int32), axis=1)
    rows_at = block_start + jnp.arange(row_count, dtype=jnp.int32)[:, None]
    cols_at = jnp.arange(key_total, dtype=jnp.int32)[None, :]
    distance = jnp.clip(rows_at - cols_at, 0, key_total - 1)
    return (distance[None] >= starts[:bucket_total, None, None]) & (
        distance[None] < starts[1:, None, None]
    )


def lookup_bias(position_bias_grid, one_hot_encoding):
    return jnp.einsum(
        "ptn,po->otn",
        one_hot_encoding.astype(jnp.float32),
        position_bias_grid,
        precision=FULL_ACCURACY,
    )


def causal_mask(length_limit, key_total):

    def allowed(block_start, row_count):
        rows_at = block_start + jnp.arange(row_count, dtype=jnp.int32)[:, None]
        cols_at = jnp.arange(key_total, dtype=jnp.int32)[None, :]
        return (cols_at <= rows_at) & (cols_at < length_limit)

    return allowed


def source_mask(length_limit, key_total):

    def allowed(block_start, row_count):
        cols_at = jnp.arange(key_total, dtype=jnp.int32)[None, :]
        return jnp.broadcast_to(cols_at < length_limit, (row_count, key_total))

    return allowed


def split_heads(matrix, head_count):
    return matrix.reshape(matrix.shape[0], head_count, matrix.shape[1] // head_count)


def block_scores(query_block, key_rows, head_count, bias_term, allowed):
    scores = jnp.einsum(
        "qhd,khd->hqk",
        split_heads(query_block, head_count),
        split_heads(key_rows, head_count),
        preferred_element_type=jnp.float32,
    )
    return jnp.where(allowed[None], scores + bias_term, MASKED)


def forward_layer_pass(query_block, key_rows, value_rows, head_count, bias_term, allowed):
    scores = block_scores(query_block, key_rows, head_count, bias_term, allowed)
    row_top = jnp.max(scores, axis=-1, keepdims=True)
    raised = jnp.exp(scores - row_top)
    row_total = jnp.sum(raised, axis=-1, keepdims=True)
    shares = (raised / row_total).astype(jnp.bfloat16)
    mixed = jnp.einsum(
        "hqk,khd->qhd",
        shares,
        split_heads(value_rows, head_count),
        preferred_element_type=jnp.float32,
    )
    return (
        mixed.reshape(query_block.shape[0], -1).astype(jnp.bfloat16),
        (row_top + jnp.log(row_total))[..., 0],
    )


def backward_block(
    query_block, key_rows, value_rows, grad_block, log_total, head_count, bias_term, allowed
):
    scores = block_scores(query_block, key_rows, head_count, bias_term, allowed)
    shares = jnp.exp(scores - log_total[..., None])
    grad_heads = split_heads(grad_block, head_count)
    grad_shares = jnp.einsum(
        "qhd,khd->hqk",
        grad_heads,
        split_heads(value_rows, head_count),
        preferred_element_type=jnp.float32,
    )
    grad_values = jnp.einsum(
        "hqk,qhd->khd", shares.astype(jnp.bfloat16), grad_heads, preferred_element_type=jnp.float32
    )
    inner_sum = jnp.sum(shares * grad_shares, axis=-1, keepdims=True)
    grad_scores = (shares * (grad_shares - inner_sum)).astype(jnp.bfloat16)
    grad_queries = jnp.einsum(
        "hqk,khd->qhd",
        grad_scores,
        split_heads(key_rows, head_count),
        preferred_element_type=jnp.float32,
    )
    grad_keys = jnp.einsum(
        "hqk,qhd->khd",
        grad_scores,
        split_heads(query_block, head_count),
        preferred_element_type=jnp.float32,
    )
    row_count = query_block.shape[0]
    key_total = key_rows.shape[0]
    return (
        grad_queries.reshape(row_count, -1),
        grad_keys.reshape(key_total, -1),
        grad_values.reshape(key_total, -1),
        grad_scores,
    )


def attend_item(
    queries, key_rows, value_rows, head_count, allowed, position_bias_grid, distance_bucket
):
    row_count = queries.shape[0]
    block_size = min(512, row_count)
    outputs = []
    log_totals = []
    for block_start in range(0, row_count, block_size):
        if position_bias_grid is None:
            bias_term = 0.0
        else:
            one_hot_encoding = bucket_table(
                distance_bucket,
                block_start,
                block_size,
                key_rows.shape[0],
                position_bias_grid.shape[0],
            )
            bias_term = lookup_bias(position_bias_grid, one_hot_encoding)
        mixed, log_total = forward_layer_pass(
            queries[block_start : block_start + block_size],
            key_rows,
            value_rows,
            head_count,
            bias_term,
            allowed(block_start, block_size),
        )
        outputs.append(mixed)
        log_totals.append(log_total)
    return (jnp.concatenate(outputs, axis=0), log_totals)


def attend_back(
    queries,
    key_rows,
    value_rows,
    grad_mixed,
    log_totals,
    head_count,
    allowed,
    position_bias_grid,
    distance_bucket,
):
    row_count = queries.shape[0]
    key_total = key_rows.shape[0]
    block_size = min(512, row_count)
    query_parts = []
    grad_key_rows = jnp.zeros(key_rows.shape, jnp.float32)
    grad_value_rows = jnp.zeros(value_rows.shape, jnp.float32)
    grad_table = (
        None if position_bias_grid is None else jnp.zeros(position_bias_grid.shape, jnp.float32)
    )
    for block_number, block_start in enumerate(range(0, row_count, block_size)):
        if position_bias_grid is None:
            bias_term = 0.0
        else:
            one_hot_encoding = bucket_table(
                distance_bucket, block_start, block_size, key_total, position_bias_grid.shape[0]
            )
            bias_term = lookup_bias(position_bias_grid, one_hot_encoding)
        grad_queries, grad_keys, grad_values, grad_scores = backward_block(
            queries[block_start : block_start + block_size],
            key_rows,
            value_rows,
            grad_mixed[block_start : block_start + block_size],
            log_totals[block_number],
            head_count,
            bias_term,
            allowed(block_start, block_size),
        )
        query_parts.append(grad_queries)
        grad_key_rows = grad_key_rows + grad_keys
        grad_value_rows = grad_value_rows + grad_values
        if position_bias_grid is not None:
            grad_table = grad_table + jnp.einsum(
                "dju,cju->cd",
                grad_scores,
                one_hot_encoding.astype(jnp.bfloat16),
                preferred_element_type=jnp.float32,
            )
    return (jnp.concatenate(query_parts, axis=0), grad_key_rows, grad_value_rows, grad_table)


def flip(array, axis_name, size, bit):
    return lax.ppermute(array, axis_name, [(i, i ^ (1 << bit)) for i in range(size)])


def core_sum(array):
    size = lax.axis_size("tensor")
    if size != 2:
        return lax.psum(array, "tensor")
    return array + lax.ppermute(array, "tensor", [(0, 1), (1, 0)])


def bit_of(bit):
    return (lax.axis_index("dp") >> bit) & 1


def part_of(array, upper, axis):
    half = array.shape[axis] // 2
    return lax.dynamic_slice_in_dim(array, upper * half, half, axis)


def halve(terms, bit, axis):
    mine = bit_of(bit)
    send = sum(part_of(t, 1 - mine, axis) for t in terms)
    keep = sum(part_of(t, mine, axis) for t in terms)
    return [keep, flip(send, "dp", lax.axis_size("dp"), bit)]


def double(array, bit, axis):
    other = flip(array, "dp", lax.axis_size("dp"), bit)
    low = jnp.concatenate([array, other], axis=axis)
    high = jnp.concatenate([other, array], axis=axis)
    return jnp.where(bit_of(bit) == 0, low, high)


def chunk_sum(chunk):
    if lax.axis_size("dp") != 16:
        return lax.psum(chunk, "dp")
    rows = chunk.shape[0]
    terms_a = halve([chunk[: rows // 2]], 0, 0)
    terms_b = halve([chunk[rows // 2 :]], 1, 0)
    terms_a = halve(terms_a, 1, 0)
    terms_b = halve(terms_b, 0, 0)
    terms = [jnp.stack([a, b]) for a, b in zip(terms_a, terms_b)]
    terms = halve(terms, 2, 1)
    terms = halve(terms, 3, 1)
    own = terms[0] + terms[1]
    own = double(own, 3, 1)
    own = double(own, 2, 1)
    a = double(own[0], 1, 0)
    b = double(own[1], 0, 0)
    a = double(a, 0, 0)
    b = double(b, 1, 0)
    return jnp.concatenate([a, b], axis=0)


def small_sum(array):
    size = lax.axis_size("dp")
    if size != 16:
        return lax.psum(array, "dp")
    for bit in range(4):
        array = array + flip(array, "dp", size, bit)
    return array


def body(
    decoder_input,
    encoder_output,
    cotangent,
    target_length,
    source_length,
    identifier_tags,
    distance_bucket,
    self_gain,
    self_query,
    self_attention_key,
    self_value,
    self_output,
    position_table,
    cross_gain,
    cross_query,
    cross_key,
    cross_value,
    cross_output,
    hidden_gain,
    hidden_in,
    hidden_out,
):
    item_count, target, model_width = decoder_input.shape
    source = encoder_output.shape[1]
    head_count = position_table.shape[1]
    decoder_rows = decoder_input.reshape(item_count * target, model_width).astype(jnp.float32)
    encoder_rows = encoder_output.reshape(item_count * source, model_width)
    normed_one, rms_one = normalize(decoder_rows, self_gain)
    input_one = normed_one.astype(jnp.bfloat16)
    queries_one = matrix_product(input_one, self_query).astype(jnp.bfloat16)
    keys_one = matrix_product(input_one, self_attention_key).astype(jnp.bfloat16)
    first_value_rows = matrix_product(input_one, self_value).astype(jnp.bfloat16)
    mixed_parts = []
    number = 0
    mixed, log_totals = attend_item(
        queries_one,
        keys_one,
        first_value_rows,
        head_count,
        causal_mask(target_length[number], target),
        position_table,
        distance_bucket,
    )
    mixed_parts.append(mixed)
    totals_one = [log_totals]
    mixed_one = mixed_parts[0]
    self_branch = core_sum(matrix_product(mixed_one, self_output))
    first = decoder_rows + self_branch
    second_normalized, rms_two = normalize(first, cross_gain)
    input_two = second_normalized.astype(jnp.bfloat16)
    queries_two = matrix_product(input_two, cross_query).astype(jnp.bfloat16)
    keys_two = matrix_product(encoder_rows, cross_key).astype(jnp.bfloat16)
    values_two = matrix_product(encoder_rows, cross_value).astype(jnp.bfloat16)
    mixed_parts = []
    number = 0
    mixed, log_totals = attend_item(
        queries_two,
        keys_two,
        values_two,
        head_count,
        source_mask(source_length[number], source),
        None,
        distance_bucket,
    )
    mixed_parts.append(mixed)
    totals_two = [log_totals]
    mixed_two = mixed_parts[0]
    cross_branch = core_sum(matrix_product(mixed_two, cross_output))
    second = first + cross_branch
    normed_three, rms_three = normalize(second, hidden_gain)
    input_three = normed_three.astype(jnp.bfloat16)
    before = matrix_product(input_three, hidden_in)
    gelu_tanh = partial(jax.nn.gelu, approximate=True)
    active = gelu_tanh(before).astype(jnp.bfloat16)
    hidden_branch = core_sum(matrix_product(active, hidden_out))
    third = second + hidden_branch
    layer_out = third.astype(jnp.bfloat16).reshape(item_count, target, model_width)
    places = jnp.arange(target, dtype=jnp.int32)
    factor = jnp.where(
        places[None, :] < target_length[:, None], 1.0 + identifier_tags.astype(jnp.float32), 0.0
    )
    grad_third = (cotangent.astype(jnp.float32) * factor[:, :, None]).reshape(
        item_count * target, model_width
    )
    grad_branch = grad_third.astype(jnp.bfloat16)
    grad_hidden_out = left_contract(active, grad_branch)
    grad_active = right_contract(grad_branch, hidden_out)
    gelu_value, gelu_pull = jax.vjp(gelu_tanh, before)
    grad_before = gelu_pull(grad_active)[0].astype(jnp.bfloat16)
    grad_hidden_in = left_contract(input_three, grad_before)
    grad_input_three = core_sum(right_contract(grad_before, hidden_in))
    back_three, grad_hidden_gain = norm_back(second, rms_three, hidden_gain, grad_input_three)
    grad_second = grad_third + back_three
    grad_branch_two = grad_second.astype(jnp.bfloat16)
    grad_mixed_two = right_contract(grad_branch_two, cross_output).astype(jnp.bfloat16)
    query_parts = []
    key_parts = []
    value_parts = []
    number = 0
    grad_queries, grad_keys, grad_values, unused_table = attend_back(
        queries_two,
        keys_two,
        values_two,
        grad_mixed_two,
        totals_two[number],
        head_count,
        source_mask(source_length[number], source),
        None,
        distance_bucket,
    )
    query_parts.append(grad_queries)
    key_parts.append(grad_keys)
    value_parts.append(grad_values)
    grad_queries_two = query_parts[0].astype(jnp.bfloat16)
    grad_keys_two = key_parts[0].astype(jnp.bfloat16)
    grad_values_two = value_parts[0].astype(jnp.bfloat16)
    grad_cross_query = left_contract(input_two, grad_queries_two)
    grad_cross_key = left_contract(encoder_rows, grad_keys_two)
    grad_cross_value = left_contract(encoder_rows, grad_values_two)
    grad_input_two = core_sum(right_contract(grad_queries_two, cross_query))
    grad_encoder = core_sum(
        right_contract(grad_keys_two, cross_key) + right_contract(grad_values_two, cross_value)
    )
    back_two, grad_cross_gain = norm_back(first, rms_two, cross_gain, grad_input_two)
    grad_first = grad_second + back_two
    grad_branch_one = grad_first.astype(jnp.bfloat16)
    grad_mixed_one = right_contract(grad_branch_one, self_output).astype(jnp.bfloat16)
    query_parts = []
    key_parts = []
    value_parts = []
    number = 0
    grad_queries, grad_keys, grad_values, grad_table = attend_back(
        queries_one,
        keys_one,
        first_value_rows,
        grad_mixed_one,
        totals_one[number],
        head_count,
        causal_mask(target_length[number], target),
        position_table,
        distance_bucket,
    )
    query_parts.append(grad_queries)
    key_parts.append(grad_keys)
    value_parts.append(grad_values)
    grad_queries_one = query_parts[0].astype(jnp.bfloat16)
    grad_keys_one = key_parts[0].astype(jnp.bfloat16)
    grad_values_one = value_parts[0].astype(jnp.bfloat16)
    grad_self_query = left_contract(input_one, grad_queries_one)
    grad_self_key = left_contract(input_one, grad_keys_one)
    grad_self_value = left_contract(input_one, grad_values_one)
    grad_input_one = core_sum(
        right_contract(grad_queries_one, self_query)
        + right_contract(grad_keys_one, self_attention_key)
        + right_contract(grad_values_one, self_value)
    )
    back_one, grad_self_gain = norm_back(decoder_rows, rms_one, self_gain, grad_input_one)
    grad_decoder = (grad_first + back_one).reshape(item_count, target, model_width)
    grad_encoder = grad_encoder.reshape(item_count, source, model_width)
    width = self_query.shape[1]
    cross_chunk = jnp.concatenate(
        [
            grad_cross_query,
            grad_cross_key,
            grad_cross_value,
            left_contract(grad_branch_two, mixed_two),
        ],
        axis=1,
    )
    self_chunk = jnp.concatenate(
        [
            grad_self_query,
            grad_self_key,
            grad_self_value,
            left_contract(grad_branch_one, mixed_one),
        ],
        axis=1,
    )
    sum_out = chunk_sum(grad_hidden_out)
    sum_in = chunk_sum(grad_hidden_in)
    sum_cross = chunk_sum(cross_chunk)
    sum_self = chunk_sum(self_chunk)
    pieces = [grad_self_gain, grad_cross_gain, grad_hidden_gain, grad_table.reshape(-1)]
    flat = jnp.concatenate(pieces)
    lanes = 512
    flat = jnp.pad(flat, (0, -flat.shape[0] % (8 * lanes))).reshape(-1, lanes)
    flat = small_sum(flat).reshape(-1)
    gains = [flat[i * model_width : (i + 1) * model_width] for i in range(3)]
    table = flat[3 * model_width : 3 * model_width + grad_table.size].reshape(grad_table.shape)
    return (
        layer_out,
        grad_decoder,
        grad_encoder,
        gains[0],
        sum_self[:, :width],
        sum_self[:, width : 2 * width],
        sum_self[:, 2 * width : 3 * width],
        sum_self[:, 3 * width :].T,
        table,
        gains[1],
        sum_cross[:, :width],
        sum_cross[:, width : 2 * width],
        sum_cross[:, 2 * width : 3 * width],
        sum_cross[:, 3 * width :].T,
        gains[2],
        sum_in,
        sum_out,
    )


def solution(mesh):
    placed = (
        P("dp", None, None),
        P("dp", None, None),
        P("dp", None, None),
        P("dp"),
        P("dp"),
        P("dp", None),
        P(),
        P(),
        P(None, "tensor"),
        P(None, "tensor"),
        P(None, "tensor"),
        P("tensor", None),
        P(None, "tensor"),
        P(),
        P(None, "tensor"),
        P(None, "tensor"),
        P(None, "tensor"),
        P("tensor", None),
        P(),
        P(None, "tensor"),
        P("tensor", None),
    )
    return jax.shard_map(
        body,
        mesh=mesh,
        in_specs=placed,
        out_specs=(
            P("dp", None, None),
            P("dp", None, None),
            P("dp", None, None),
            P(),
            P(None, "tensor"),
            P(None, "tensor"),
            P(None, "tensor"),
            P("tensor", None),
            P(None, "tensor"),
            P(),
            P(None, "tensor"),
            P(None, "tensor"),
            P(None, "tensor"),
            P("tensor", None),
            P(),
            P(None, "tensor"),
            P("tensor", None),
        ),
        check_vma=False,
    )
```

```python
import functools

import jax
import jax.numpy as jnp
from jax import lax
from jax.experimental import pallas as pl
from jax.experimental.pallas import tpu as pltpu
from jax.sharding import PartitionSpec as P

EPSILON = 1e-06
MASKED = -1e30
LANES = 128
NT = (((1,), (1,)), ((), ()))
NN = (((1,), (0,)), ((), ()))


def dot(a, b, dims):
    return lax.dot_general(a, b, dims, preferred_element_type=jnp.float32)


def head_lane_masks(rows, width, half):
    lane = lax.broadcasted_iota(jnp.int32, (rows, 2 * width), 1)
    return (lane < width) if half == 0 else (lane >= width)


def only_head(array, half):
    width = array.shape[1] // 2
    keep = head_lane_masks(array.shape[0], width, half)
    return jnp.where(keep, array.astype(jnp.float32), 0.0).astype(jnp.bfloat16)


def with_mark(array, half, mark):
    rows, both = array.shape
    width = both // 2
    lane = lax.broadcasted_iota(jnp.int32, (rows, both), 1)
    keep = (lane < width) if half == 0 else (lane >= width)
    place = width if half == 0 else 0
    other = jnp.where(lane == place, mark, 0.0)
    return jnp.where(keep, array.astype(jnp.float32), other).astype(jnp.bfloat16)


def key_marks(key_ref, limit):
    rows, both = key_ref.shape
    row = lax.broadcasted_iota(jnp.int32, (rows, both), 0)
    mark = jnp.where(row < limit, 0.0, MASKED)
    keys = key_ref[...]
    return [with_mark(keys, half, mark) for half in range(2)]


def diagonal_bias(line):
    wide = jnp.broadcast_to(line, (LANES, line.shape[1]))
    return pltpu.roll(wide, 0, 1, stride=1, stride_axis=0)


def forward_kernel(causal, block, limit_ref, query_ref, key_ref, value_ref, *rest):
    if causal:
        line_ref, out_ref, log_ref, key_scr, value_scr, bias_scr = rest
    else:
        out_ref, log_ref, key_scr, value_scr = rest
    value_scr[...] = value_ref[...].T
    keys = key_marks(key_ref, limit_ref[0])
    for half in range(2):
        key_scr[half] = keys[half]
        if causal:
            bias_scr[half] = diagonal_bias(line_ref[0, half : half + 1, :])
    rows = query_ref.shape[0]
    key_total = key_ref.shape[0]
    width = query_ref.shape[1] // 2
    for start in range(0, rows, block):
        keys_here = min(key_total, start + block) if causal else key_total
        queries = query_ref[start : start + block, :]
        outs = []
        for half in range(2):
            marked = with_mark(queries, half, 1.0)
            scores = dot(key_scr[half, :keys_here, :], marked, NT)
            if causal:
                parts = []
                for key_at in range(0, keys_here, LANES):
                    lane_at = start - key_at + LANES
                    parts.append(
                        scores[key_at : key_at + LANES]
                        + bias_scr[half, :, lane_at : lane_at + block]
                    )
                scores = jnp.concatenate(parts, axis=0)
            top = jnp.max(scores, axis=0, keepdims=True)
            raised = jnp.exp(scores - top)
            total = jnp.sum(raised, axis=0, keepdims=True)
            mixed = dot(
                value_scr[half * width : (half + 1) * width, :keys_here],
                raised.astype(jnp.bfloat16),
                NN,
            )
            outs.append(mixed / total)
            log_ref[0, half : half + 1, start : start + block] = top + jnp.log(total)
        out_ref[start : start + block, :] = jnp.concatenate(outs, axis=0).T


def smem():
    return pl.BlockSpec(memory_space=pltpu.SMEM)


def attend(queries, keys, values, limit, lines):
    rows, wide = queries.shape
    key_total = keys.shape[0]
    pairs = wide // LANES
    causal = lines is not None
    block = min(256, rows)
    in_specs = [
        smem(),
        pl.BlockSpec((rows, LANES), lambda p: (0, p)),
        pl.BlockSpec((key_total, LANES), lambda p: (0, p)),
        pl.BlockSpec((key_total, LANES), lambda p: (0, p)),
    ]
    scratch = [
        pltpu.VMEM((2, key_total, LANES), jnp.bfloat16),
        pltpu.VMEM((LANES, key_total), jnp.bfloat16),
    ]
    args = [limit, queries, keys, values]
    if causal:
        in_specs.append(pl.BlockSpec((1, 2, lines.shape[2]), lambda p: (p, 0, 0)))
        scratch.append(pltpu.VMEM((2, LANES, lines.shape[2]), jnp.float32))
        args.append(lines)
    return pl.pallas_call(
        functools.partial(forward_kernel, causal, block),
        grid=(pairs,),
        in_specs=in_specs,
        out_specs=[
            pl.BlockSpec((rows, LANES), lambda p: (0, p)),
            pl.BlockSpec((1, 2, rows), lambda p: (p, 0, 0)),
        ],
        out_shape=[
            jax.ShapeDtypeStruct((rows, wide), jnp.float32),
            jax.ShapeDtypeStruct((pairs, 2, rows), jnp.float32),
        ],
        scratch_shapes=scratch,
        compiler_params=pltpu.CompilerParams(vmem_limit_bytes=48 * 1024 * 1024),
        cost_estimate=pl.CostEstimate(
            flops=4 * rows * key_total * wide,
            bytes_accessed=10 * rows * wide,
            transcendentals=rows * key_total * pairs * 2,
        ),
    )(*args)


def backward_kernel(
    causal, block, limit_ref, query_ref, key_ref, value_ref, grad_ref, mixed_ref, log_ref, *rest
):
    if causal:
        line_ref, gq_ref, gk_ref, gv_ref, table_ref, key_scr, key_t_scr, bias_scr, diag_scr, gk_scr, gv_scr = rest
    else:
        gq_ref, gk_ref, gv_ref, key_scr, key_t_scr, gk_scr, gv_scr = rest
    key_t_scr[...] = key_ref[...].T
    keys = key_marks(key_ref, limit_ref[0])
    for half in range(2):
        key_scr[half] = keys[half]
        if causal:
            bias_scr[half] = diagonal_bias(line_ref[0, half : half + 1, :])
            diag_scr[half] = jnp.zeros(diag_scr.shape[1:], jnp.float32)
    gk_scr[...] = jnp.zeros(gk_scr.shape, jnp.float32)
    gv_scr[...] = jnp.zeros(gv_scr.shape, jnp.float32)
    rows = query_ref.shape[0]
    key_total = key_ref.shape[0]
    width = query_ref.shape[1] // 2
    step = 2 * LANES
    for start in range(0, rows, block):
        keys_here = min(key_total, start + block) if causal else key_total
        queries = query_ref[start : start + block, :]
        grads = grad_ref[start : start + block, :]
        inner_t = (grads.astype(jnp.float32) * mixed_ref[start : start + block, :]).T
        query_parts = []
        for half in range(2):
            marked = with_mark(queries, half, 1.0)
            plain = only_head(queries, half)
            grads_here = only_head(grads, half)
            inner = jnp.sum(inner_t[half * width : (half + 1) * width], axis=0, keepdims=True)
            log_total = log_ref[0, half : half + 1, start : start + block]
            grad_queries = jnp.zeros((width, block), jnp.float32)
            for key_at in range(0, keys_here, step):
                here = slice(key_at, key_at + step)
                scores = dot(key_scr[half, here, :], marked, NT)
                if causal:
                    lane_at = start - key_at + LANES
                    bias = jnp.concatenate(
                        [
                            bias_scr[half, :, lane_at : lane_at + block],
                            bias_scr[half, :, lane_at - LANES : lane_at - LANES + block],
                        ],
                        axis=0,
                    )
                    scores = scores + bias
                shares = jnp.exp(scores - log_total)
                grad_shares = dot(value_ref[here, :], grads_here, NT)
                grad_scores = shares * (grad_shares - inner)
                if causal:
                    diag_scr[half, :, lane_at : lane_at + block] += grad_scores[:LANES]
                    diag_scr[half, :, lane_at - LANES : lane_at - LANES + block] += grad_scores[LANES:]
                shares = shares.astype(jnp.bfloat16)
                grad_scores = grad_scores.astype(jnp.bfloat16)
                gv_scr[here, :] += dot(shares, grads_here, NN)
                gk_scr[here, :] += dot(grad_scores, plain, NN)
                grad_queries += dot(key_t_scr[half * width : (half + 1) * width, here], grad_scores, NN)
            query_parts.append(grad_queries)
        gq_ref[start : start + block, :] = (
            jnp.concatenate(query_parts, axis=0).T.astype(jnp.bfloat16)
        )
    gk_ref[...] = gk_scr[...].astype(jnp.bfloat16)
    gv_ref[...] = gv_scr[...].astype(jnp.bfloat16)
    if causal:
        lanes = diag_scr.shape[2]
        down = lax.broadcasted_iota(jnp.int32, (LANES, LANES), 0)
        across = lax.broadcasted_iota(jnp.int32, (LANES, LANES), 1)
        backwards = jnp.where(down + across == LANES - 1, 1.0, 0.0)
        for half in range(2):
            turned = lax.dot_general(
                backwards, diag_scr[half], NN, precision=lax.Precision.HIGHEST
            )
            straight = pltpu.roll(turned, lanes - LANES + 1, 1, stride=1, stride_axis=0)
            table_ref[0, half : half + 1, :] = jnp.sum(straight, axis=0, keepdims=True)


def attend_back(queries, keys, values, grads, mixed, logs, limit, lines):
    rows, wide = queries.shape
    key_total = keys.shape[0]
    pairs = wide // LANES
    causal = lines is not None
    block = min(256, rows)
    tall = pl.BlockSpec((rows, LANES), lambda p: (0, p))
    by_key = pl.BlockSpec((key_total, LANES), lambda p: (0, p))
    in_specs = [
        smem(),
        tall,
        by_key,
        by_key,
        tall,
        tall,
        pl.BlockSpec((1, 2, rows), lambda p: (p, 0, 0)),
    ]
    args = [limit, queries, keys, values, grads, mixed, logs]
    out_specs = [tall, by_key, by_key]
    out_shape = [
        jax.ShapeDtypeStruct((rows, wide), jnp.bfloat16),
        jax.ShapeDtypeStruct((key_total, wide), jnp.bfloat16),
        jax.ShapeDtypeStruct((key_total, wide), jnp.bfloat16),
    ]
    scratch = [
        pltpu.VMEM((2, key_total, LANES), jnp.bfloat16),
        pltpu.VMEM((LANES, key_total), jnp.bfloat16),
    ]
    if causal:
        lanes = lines.shape[2]
        in_specs.append(pl.BlockSpec((1, 2, lanes), lambda p: (p, 0, 0)))
        args.append(lines)
        out_specs.append(pl.BlockSpec((1, 2, lanes), lambda p: (p, 0, 0)))
        out_shape.append(jax.ShapeDtypeStruct((pairs, 2, lanes), jnp.float32))
        scratch += [pltpu.VMEM((2, LANES, lanes), jnp.float32)] * 2
    scratch += [pltpu.VMEM((key_total, LANES), jnp.float32)] * 2
    return pl.pallas_call(
        functools.partial(backward_kernel, causal, block),
        grid=(pairs,),
        in_specs=in_specs,
        out_specs=out_specs,
        out_shape=out_shape,
        scratch_shapes=scratch,
        compiler_params=pltpu.CompilerParams(vmem_limit_bytes=48 * 1024 * 1024),
        cost_estimate=pl.CostEstimate(
            flops=10 * rows * key_total * wide,
            bytes_accessed=20 * rows * wide,
            transcendentals=rows * key_total * pairs * 2,
        ),
    )(*args)


def bias_lines(distance_bucket, position_table):
    buckets, heads = position_table.shape
    total = distance_bucket.shape[0]
    hot = distance_bucket[:, None, None] == jnp.arange(buckets)[None, :, None]
    by_distance = jnp.sum(jnp.where(hot, position_table[None], 0.0), axis=1).T
    edge = jnp.full((heads, LANES), MASKED, jnp.float32)
    lines = jnp.concatenate([edge, by_distance, edge], axis=1)
    return lines.reshape(heads // 2, 2, total + 2 * LANES)


def table_grad(lines, distance_bucket, buckets):
    pairs, two, lanes = lines.shape
    by_distance = lines.reshape(pairs * two, lanes)[:, LANES : lanes - LANES]
    hot = distance_bucket[None, :] == jnp.arange(buckets)[:, None]
    return jnp.sum(jnp.where(hot[:, None, :], by_distance[None], 0.0), axis=-1)


def flip(array, bit):
    size = lax.axis_size("dp")
    return lax.ppermute(array, "dp", [(i, i ^ (1 << bit)) for i in range(size)])


def core_sum(array):
    if lax.axis_size("tensor") != 2:
        return lax.psum(array, "tensor")
    return array + lax.ppermute(array, "tensor", [(0, 1), (1, 0)])


def bit_of(bit):
    return (lax.axis_index("dp") >> bit) & 1


def part_of(array, upper, axis):
    half = array.shape[axis] // 2
    return lax.dynamic_slice_in_dim(array, upper * half, half, axis)


def halve(terms, bit, axis):
    mine = bit_of(bit)
    send = sum(part_of(t, 1 - mine, axis) for t in terms)
    keep = sum(part_of(t, mine, axis) for t in terms)
    return [keep, flip(send, bit)]


def double(array, bit, axis):
    other = flip(array, bit)
    low = jnp.concatenate([array, other], axis=axis)
    high = jnp.concatenate([other, array], axis=axis)
    return jnp.where(bit_of(bit) == 0, low, high)


def pair_sum(first, second, axis):
    if lax.axis_size("dp") != 16:
        return lax.psum((first, second), "dp")
    terms_a = halve([first], 0, axis)
    terms_b = halve([second], 1, axis)
    terms_a = halve(terms_a, 1, axis)
    terms_b = halve(terms_b, 0, axis)
    terms = [jnp.stack([a, b]) for a, b in zip(terms_a, terms_b)]
    terms = halve(terms, 2, axis + 1)
    terms = halve(terms, 3, axis + 1)
    own = terms[0] + terms[1]
    own = double(own, 3, axis + 1)
    own = double(own, 2, axis + 1)
    a = double(own[0], 1, axis)
    b = double(own[1], 0, axis)
    a = double(a, 0, axis)
    b = double(b, 1, axis)
    return a, b


def small_sum(array):
    if lax.axis_size("dp") != 16:
        return lax.psum(array, "dp")
    for bit in range(4):
        array = array + flip(array, bit)
    return array


def matrix_product(former, latter):
    return jnp.dot(former, latter, preferred_element_type=jnp.float32)


def left_contract(former, latter):
    return jnp.einsum("ti,tj->ij", former, latter, preferred_element_type=jnp.float32)


def right_contract(former, latter):
    return jnp.einsum("ti,ji->tj", former, latter, preferred_element_type=jnp.float32)


def normalize(hidden, norm_gain):
    inverse_rms = lax.rsqrt(jnp.mean(hidden * hidden, axis=-1, keepdims=True) + EPSILON)
    return (hidden * inverse_rms * norm_gain, inverse_rms)


def norm_back(hidden, inverse_rms, norm_gain, grad_normed):
    grad_gain = jnp.sum(grad_normed * hidden * inverse_rms, axis=0)
    grad_scaled = grad_normed * norm_gain
    inner_sum = jnp.mean(grad_scaled * hidden, axis=-1, keepdims=True)
    cubed = inverse_rms * inverse_rms * inverse_rms
    return (inverse_rms * grad_scaled - hidden * cubed * inner_sum, grad_gain)


def body(
    decoder_input,
    encoder_output,
    cotangent,
    target_length,
    source_length,
    identifier_tags,
    distance_bucket,
    self_gain,
    self_query,
    self_attention_key,
    self_value,
    self_output,
    position_table,
    cross_gain,
    cross_query,
    cross_key,
    cross_value,
    cross_output,
    hidden_gain,
    hidden_in,
    hidden_out,
):
    item_count, target, model_width = decoder_input.shape
    source = encoder_output.shape[1]
    low = jnp.bfloat16
    decoder_rows = decoder_input.reshape(item_count * target, model_width).astype(jnp.float32)
    encoder_rows = encoder_output.reshape(item_count * source, model_width)
    lines = bias_lines(distance_bucket, position_table)

    normed_one, rms_one = normalize(decoder_rows, self_gain)
    input_one = normed_one.astype(low)
    queries_one = matrix_product(input_one, self_query).astype(low)
    keys_one = matrix_product(input_one, self_attention_key).astype(low)
    values_one = matrix_product(input_one, self_value).astype(low)
    exact_one, logs_one = attend(queries_one, keys_one, values_one, target_length, lines)
    mixed_one = exact_one.astype(low)
    first = decoder_rows + core_sum(matrix_product(mixed_one, self_output))

    second_normalized, rms_two = normalize(first, cross_gain)
    input_two = second_normalized.astype(low)
    queries_two = matrix_product(input_two, cross_query).astype(low)
    keys_two = matrix_product(encoder_rows, cross_key).astype(low)
    values_two = matrix_product(encoder_rows, cross_value).astype(low)
    exact_two, logs_two = attend(queries_two, keys_two, values_two, source_length, None)
    mixed_two = exact_two.astype(low)
    second = first + core_sum(matrix_product(mixed_two, cross_output))

    normed_three, rms_three = normalize(second, hidden_gain)
    input_three = normed_three.astype(low)
    before = matrix_product(input_three, hidden_in)
    gelu_tanh = functools.partial(jax.nn.gelu, approximate=True)
    value, pull = jax.vjp(gelu_tanh, before)
    active = value.astype(low)

    places = jnp.arange(target, dtype=jnp.int32)
    factor = jnp.where(
        places[None, :] < target_length[:, None], 1.0 + identifier_tags.astype(jnp.float32), 0.0
    )
    grad_third = (cotangent.astype(jnp.float32) * factor[:, :, None]).reshape(
        item_count * target, model_width
    )
    grad_branch = grad_third.astype(low)
    hidden = active.shape[1]
    sum_out = pair_sum(
        left_contract(active[:, : hidden // 2], grad_branch),
        left_contract(active[:, hidden // 2 :], grad_branch),
        0,
    )
    grad_active = right_contract(grad_branch, hidden_out)
    grad_before = pull(grad_active)[0].astype(low)
    sum_in = pair_sum(
        left_contract(input_three[:, : model_width // 2], grad_before),
        left_contract(input_three[:, model_width // 2 :], grad_before),
        0,
    )
    third = second + core_sum(matrix_product(active, hidden_out))
    layer_out = third.astype(low).reshape(item_count, target, model_width)

    grad_input_three = core_sum(right_contract(grad_before, hidden_in))
    back_three, grad_hidden_gain = norm_back(second, rms_three, hidden_gain, grad_input_three)
    grad_second = grad_third + back_three
    grad_branch_two = grad_second.astype(low)
    grad_mixed_two = right_contract(grad_branch_two, cross_output).astype(low)
    grad_queries_two, grad_keys_two, grad_values_two = attend_back(
        queries_two,
        keys_two,
        values_two,
        grad_mixed_two,
        exact_two,
        logs_two,
        source_length,
        None,
    )
    grad_input_two = core_sum(right_contract(grad_queries_two, cross_query))
    sum_cross = pair_sum(
        jnp.stack(
            [
                left_contract(input_two, grad_queries_two),
                left_contract(encoder_rows, grad_keys_two),
            ]
        ),
        jnp.stack(
            [
                left_contract(encoder_rows, grad_values_two),
                left_contract(grad_branch_two, mixed_two),
            ]
        ),
        1,
    )
    grad_encoder = core_sum(
        right_contract(grad_keys_two, cross_key) + right_contract(grad_values_two, cross_value)
    )
    back_two, grad_cross_gain = norm_back(first, rms_two, cross_gain, grad_input_two)
    grad_first = grad_second + back_two
    grad_branch_one = grad_first.astype(low)
    grad_mixed_one = right_contract(grad_branch_one, self_output).astype(low)
    grad_queries_one, grad_keys_one, grad_values_one, grad_lines = attend_back(
        queries_one,
        keys_one,
        values_one,
        grad_mixed_one,
        exact_one,
        logs_one,
        target_length,
        lines,
    )
    grad_table = table_grad(grad_lines, distance_bucket, position_table.shape[0])
    grad_input_one = core_sum(
        right_contract(grad_queries_one, self_query)
        + right_contract(grad_keys_one, self_attention_key)
        + right_contract(grad_values_one, self_value)
    )
    sum_self = pair_sum(
        jnp.stack(
            [
                left_contract(input_one, grad_queries_one),
                left_contract(input_one, grad_keys_one),
            ]
        ),
        jnp.stack(
            [
                left_contract(input_one, grad_values_one),
                left_contract(grad_branch_one, mixed_one),
            ]
        ),
        1,
    )
    back_one, grad_self_gain = norm_back(decoder_rows, rms_one, self_gain, grad_input_one)
    grad_decoder = (grad_first + back_one).reshape(item_count, target, model_width)
    grad_encoder = grad_encoder.reshape(item_count, source, model_width)

    flat = jnp.concatenate(
        [grad_self_gain, grad_cross_gain, grad_hidden_gain, grad_table.reshape(-1)]
    )
    lanes = 512
    flat = jnp.pad(flat, (0, -flat.shape[0] % (8 * lanes))).reshape(-1, lanes)
    flat = small_sum(flat).reshape(-1)
    gains = [flat[i * model_width : (i + 1) * model_width] for i in range(3)]
    table = flat[3 * model_width : 3 * model_width + grad_table.size].reshape(grad_table.shape)
    return (
        layer_out,
        grad_decoder,
        grad_encoder,
        gains[0],
        sum_self[0][0],
        sum_self[0][1],
        sum_self[1][0],
        sum_self[1][1].T,
        table,
        gains[1],
        sum_cross[0][0],
        sum_cross[0][1],
        sum_cross[1][0],
        sum_cross[1][1].T,
        gains[2],
        jnp.concatenate(sum_in, axis=0),
        jnp.concatenate(sum_out, axis=0),
    )


def solution(mesh):
    by_item = P("dp", None, None)
    columns = P(None, "tensor")
    rows = P("tensor", None)
    attention = (P(), columns, columns, columns, rows)
    return jax.shard_map(
        body,
        mesh=mesh,
        in_specs=(by_item, by_item, by_item, P("dp"), P("dp"), P("dp", None), P())
        + attention
        + (columns,)
        + attention
        + (P(), columns, rows),
        out_specs=(by_item, by_item, by_item)
        + attention
        + (columns,)
        + attention
        + (P(), columns, rows),
        check_vma=False,
    )
```

```python
import functools

import jax
import jax.numpy as jnp
from jax import lax
from jax.experimental import pallas as pl
from jax.experimental.pallas import tpu as pltpu
from jax.sharding import PartitionSpec as P

EPSILON = 1e-06
MASKED = -1e30
LANES = 128
NT = (((1,), (1,)), ((), ()))
NN = (((1,), (0,)), ((), ()))


def dot(a, b, dims):
    return lax.dot_general(a, b, dims, preferred_element_type=jnp.float32)


def head_lane_masks(rows, width, half):
    lane = lax.broadcasted_iota(jnp.int32, (rows, 2 * width), 1)
    return (lane < width) if half == 0 else (lane >= width)


def only_head(array, half):
    width = array.shape[1] // 2
    keep = head_lane_masks(array.shape[0], width, half)
    return jnp.where(keep, array.astype(jnp.float32), 0.0).astype(jnp.bfloat16)


def with_mark(array, half, mark):
    rows, both = array.shape
    width = both // 2
    lane = lax.broadcasted_iota(jnp.int32, (rows, both), 1)
    keep = (lane < width) if half == 0 else (lane >= width)
    place = width if half == 0 else 0
    other = jnp.where(lane == place, mark, 0.0)
    return jnp.where(keep, array.astype(jnp.float32), other).astype(jnp.bfloat16)


def key_marks(key_ref, limit):
    rows, both = key_ref.shape
    row = lax.broadcasted_iota(jnp.int32, (rows, both), 0)
    mark = jnp.where(row < limit, 0.0, MASKED)
    keys = key_ref[...]
    return [with_mark(keys, half, mark) for half in range(2)]


def diagonal_bias(line):
    wide = jnp.broadcast_to(line, (LANES, line.shape[1]))
    return pltpu.roll(wide, 0, 1, stride=1, stride_axis=0)


def forward_kernel(causal, block, limit_ref, query_ref, key_ref, value_ref, *rest):
    if causal:
        line_ref, out_ref, log_ref, key_scr, value_scr, bias_scr = rest
    else:
        out_ref, log_ref, key_scr, value_scr = rest
    value_scr[...] = value_ref[...].T
    keys = key_marks(key_ref, limit_ref[0])
    for half in range(2):
        key_scr[half] = keys[half]
        if causal:
            bias_scr[half] = diagonal_bias(line_ref[0, half : half + 1, :])
    rows = query_ref.shape[0]
    key_total = key_ref.shape[0]
    width = query_ref.shape[1] // 2
    for start in range(0, rows, block):
        keys_here = min(key_total, start + block) if causal else key_total
        queries = query_ref[start : start + block, :]
        outs = []
        for half in range(2):
            marked = with_mark(queries, half, 1.0)
            scores = dot(key_scr[half, :keys_here, :], marked, NT)
            if causal:
                parts = []
                for key_at in range(0, keys_here, LANES):
                    lane_at = start - key_at + LANES
                    parts.append(
                        scores[key_at : key_at + LANES]
                        + bias_scr[half, :, lane_at : lane_at + block]
                    )
                scores = jnp.concatenate(parts, axis=0)
            top = jnp.max(scores, axis=0, keepdims=True)
            raised = jnp.exp(scores - top)
            total = jnp.sum(raised, axis=0, keepdims=True)
            mixed = dot(
                value_scr[half * width : (half + 1) * width, :keys_here],
                raised.astype(jnp.bfloat16),
                NN,
            )
            outs.append(mixed / total)
            log_ref[0, half : half + 1, start : start + block] = top + jnp.log(total)
        out_ref[start : start + block, :] = jnp.concatenate(outs, axis=0).T


def smem():
    return pl.BlockSpec(memory_space=pltpu.SMEM)


def attend(queries, keys, values, limit, lines):
    rows, wide = queries.shape
    key_total = keys.shape[0]
    pairs = wide // LANES
    causal = lines is not None
    block = min(256, rows)
    in_specs = [
        smem(),
        pl.BlockSpec((rows, LANES), lambda p: (0, p)),
        pl.BlockSpec((key_total, LANES), lambda p: (0, p)),
        pl.BlockSpec((key_total, LANES), lambda p: (0, p)),
    ]
    scratch = [
        pltpu.VMEM((2, key_total, LANES), jnp.bfloat16),
        pltpu.VMEM((LANES, key_total), jnp.bfloat16),
    ]
    args = [limit, queries, keys, values]
    if causal:
        in_specs.append(pl.BlockSpec((1, 2, lines.shape[2]), lambda p: (p, 0, 0)))
        scratch.append(pltpu.VMEM((2, LANES, lines.shape[2]), jnp.float32))
        args.append(lines)
    return pl.pallas_call(
        functools.partial(forward_kernel, causal, block),
        grid=(pairs,),
        in_specs=in_specs,
        out_specs=[
            pl.BlockSpec((rows, LANES), lambda p: (0, p)),
            pl.BlockSpec((1, 2, rows), lambda p: (p, 0, 0)),
        ],
        out_shape=[
            jax.ShapeDtypeStruct((rows, wide), jnp.float32),
            jax.ShapeDtypeStruct((pairs, 2, rows), jnp.float32),
        ],
        scratch_shapes=scratch,
        compiler_params=pltpu.CompilerParams(vmem_limit_bytes=48 * 1024 * 1024),
        cost_estimate=free(),
    )(*args)


def backward_kernel(
    causal, block, limit_ref, query_ref, key_ref, value_ref, grad_ref, mixed_ref, log_ref, *rest
):
    if causal:
        line_ref, gq_ref, gk_ref, gv_ref, table_ref, key_scr, key_t_scr, bias_scr, diag_scr, gk_scr, gv_scr = rest
    else:
        gq_ref, gk_ref, gv_ref, key_scr, key_t_scr, gk_scr, gv_scr = rest
    key_t_scr[...] = key_ref[...].T
    keys = key_marks(key_ref, limit_ref[0])
    for half in range(2):
        key_scr[half] = keys[half]
        if causal:
            bias_scr[half] = diagonal_bias(line_ref[0, half : half + 1, :])
            diag_scr[half] = jnp.zeros(diag_scr.shape[1:], jnp.float32)
    gk_scr[...] = jnp.zeros(gk_scr.shape, jnp.float32)
    gv_scr[...] = jnp.zeros(gv_scr.shape, jnp.float32)
    rows = query_ref.shape[0]
    key_total = key_ref.shape[0]
    width = query_ref.shape[1] // 2
    step = 2 * LANES
    for start in range(0, rows, block):
        keys_here = min(key_total, start + block) if causal else key_total
        queries = query_ref[start : start + block, :]
        grads = grad_ref[start : start + block, :]
        inner_t = (grads.astype(jnp.float32) * mixed_ref[start : start + block, :]).T
        query_parts = []
        for half in range(2):
            marked = with_mark(queries, half, 1.0)
            plain = only_head(queries, half)
            grads_here = only_head(grads, half)
            inner = jnp.sum(inner_t[half * width : (half + 1) * width], axis=0, keepdims=True)
            log_total = log_ref[0, half : half + 1, start : start + block]
            grad_queries = jnp.zeros((width, block), jnp.float32)
            for key_at in range(0, keys_here, step):
                here = slice(key_at, key_at + step)
                scores = dot(key_scr[half, here, :], marked, NT)
                if causal:
                    lane_at = start - key_at + LANES
                    bias = jnp.concatenate(
                        [
                            bias_scr[half, :, lane_at : lane_at + block],
                            bias_scr[half, :, lane_at - LANES : lane_at - LANES + block],
                        ],
                        axis=0,
                    )
                    scores = scores + bias
                shares = jnp.exp(scores - log_total)
                grad_shares = dot(value_ref[here, :], grads_here, NT)
                grad_scores = shares * (grad_shares - inner)
                if causal:
                    diag_scr[half, :, lane_at : lane_at + block] += grad_scores[:LANES]
                    diag_scr[half, :, lane_at - LANES : lane_at - LANES + block] += grad_scores[LANES:]
                shares = shares.astype(jnp.bfloat16)
                grad_scores = grad_scores.astype(jnp.bfloat16)
                gv_scr[here, :] += dot(shares, grads_here, NN)
                gk_scr[here, :] += dot(grad_scores, plain, NN)
                grad_queries += dot(key_t_scr[half * width : (half + 1) * width, here], grad_scores, NN)
            query_parts.append(grad_queries)
        gq_ref[start : start + block, :] = (
            jnp.concatenate(query_parts, axis=0).T.astype(jnp.bfloat16)
        )
    gk_ref[...] = gk_scr[...].astype(jnp.bfloat16)
    gv_ref[...] = gv_scr[...].astype(jnp.bfloat16)
    if causal:
        lanes = diag_scr.shape[2]
        down = lax.broadcasted_iota(jnp.int32, (LANES, LANES), 0)
        across = lax.broadcasted_iota(jnp.int32, (LANES, LANES), 1)
        backwards = jnp.where(down + across == LANES - 1, 1.0, 0.0)
        for half in range(2):
            turned = lax.dot_general(
                backwards, diag_scr[half], NN, precision=lax.Precision.HIGHEST
            )
            straight = pltpu.roll(turned, lanes - LANES + 1, 1, stride=1, stride_axis=0)
            table_ref[0, half : half + 1, :] = jnp.sum(straight, axis=0, keepdims=True)


def attend_back(queries, keys, values, grads, mixed, logs, limit, lines):
    rows, wide = queries.shape
    key_total = keys.shape[0]
    pairs = wide // LANES
    causal = lines is not None
    block = min(256, rows)
    tall = pl.BlockSpec((rows, LANES), lambda p: (0, p))
    by_key = pl.BlockSpec((key_total, LANES), lambda p: (0, p))
    in_specs = [
        smem(),
        tall,
        by_key,
        by_key,
        tall,
        tall,
        pl.BlockSpec((1, 2, rows), lambda p: (p, 0, 0)),
    ]
    args = [limit, queries, keys, values, grads, mixed, logs]
    out_specs = [tall, by_key, by_key]
    out_shape = [
        jax.ShapeDtypeStruct((rows, wide), jnp.bfloat16),
        jax.ShapeDtypeStruct((key_total, wide), jnp.bfloat16),
        jax.ShapeDtypeStruct((key_total, wide), jnp.bfloat16),
    ]
    scratch = [
        pltpu.VMEM((2, key_total, LANES), jnp.bfloat16),
        pltpu.VMEM((LANES, key_total), jnp.bfloat16),
    ]
    if causal:
        lanes = lines.shape[2]
        in_specs.append(pl.BlockSpec((1, 2, lanes), lambda p: (p, 0, 0)))
        args.append(lines)
        out_specs.append(pl.BlockSpec((1, 2, lanes), lambda p: (p, 0, 0)))
        out_shape.append(jax.ShapeDtypeStruct((pairs, 2, lanes), jnp.float32))
        scratch += [pltpu.VMEM((2, LANES, lanes), jnp.float32)] * 2
    scratch += [pltpu.VMEM((key_total, LANES), jnp.float32)] * 2
    return pl.pallas_call(
        functools.partial(backward_kernel, causal, block),
        grid=(pairs,),
        in_specs=in_specs,
        out_specs=out_specs,
        out_shape=out_shape,
        scratch_shapes=scratch,
        compiler_params=pltpu.CompilerParams(vmem_limit_bytes=48 * 1024 * 1024),
        cost_estimate=free(),
    )(*args)


def bias_lines(distance_bucket, position_table):
    buckets, heads = position_table.shape
    total = distance_bucket.shape[0]
    hot = distance_bucket[:, None, None] == jnp.arange(buckets)[None, :, None]
    by_distance = jnp.sum(jnp.where(hot, position_table[None], 0.0), axis=1).T
    edge = jnp.full((heads, LANES), MASKED, jnp.float32)
    lines = jnp.concatenate([edge, by_distance, edge], axis=1)
    return lines.reshape(heads // 2, 2, total + 2 * LANES)


def table_grad(lines, distance_bucket, buckets):
    pairs, two, lanes = lines.shape
    by_distance = lines.reshape(pairs * two, lanes)[:, LANES : lanes - LANES]
    hot = distance_bucket[None, :] == jnp.arange(buckets)[:, None]
    return jnp.sum(jnp.where(hot[:, None, :], by_distance[None], 0.0), axis=-1)


def free():
    return pl.CostEstimate(flops=10**11, bytes_accessed=1, transcendentals=1)


def params():
    return pltpu.CompilerParams(vmem_limit_bytes=48 * 1024 * 1024)


def whole(shape):
    zeros = (0,) * len(shape)
    return pl.BlockSpec(shape, lambda i: zeros)


def norm_kernel(terms, products, *refs):
    parts = refs[:terms]
    gain_ref = refs[terms]
    weights = refs[terms + 1 : terms + 1 + products]
    outs = refs[terms + 1 + products :]
    hidden = parts[0][...].astype(jnp.float32)
    if terms > 1:
        hidden = hidden + sum(part[...] for part in parts[1:])
        outs[0][...] = hidden
        outs = outs[1:]
    inverse_rms = lax.rsqrt(jnp.mean(hidden * hidden, axis=-1, keepdims=True) + EPSILON)
    normed = (hidden * inverse_rms * gain_ref[...]).astype(jnp.bfloat16)
    outs[0][...] = normed
    for weight_ref, out_ref in zip(weights, outs[1:]):
        out_ref[...] = dot(normed, weight_ref[...], NN).astype(jnp.bfloat16)


def norm_forward(parts, gain, weights):
    rows, model_width = parts[0].shape
    block = min(256, rows)
    by_rows = pl.BlockSpec((block, model_width), lambda i: (i, 0))
    out_specs = []
    out_shape = []
    if len(parts) > 1:
        out_specs.append(by_rows)
        out_shape.append(jax.ShapeDtypeStruct((rows, model_width), jnp.float32))
    out_specs.append(by_rows)
    out_shape.append(jax.ShapeDtypeStruct((rows, model_width), jnp.bfloat16))
    for weight in weights:
        out_specs.append(pl.BlockSpec((block, weight.shape[1]), lambda i: (i, 0)))
        out_shape.append(jax.ShapeDtypeStruct((rows, weight.shape[1]), jnp.bfloat16))
    return pl.pallas_call(
        functools.partial(norm_kernel, len(parts), len(weights)),
        grid=(rows // block,),
        in_specs=[by_rows] * len(parts)
        + [whole((1, model_width))]
        + [whole(weight.shape) for weight in weights],
        out_specs=out_specs,
        out_shape=out_shape,
        compiler_params=params(),
        cost_estimate=free(),
    )(*parts, gain.reshape(1, model_width), *weights)


def norm_back_kernel(grads, deep, hidden_ref, gain_ref, before_ref, *refs):
    grad_refs = refs[:grads]
    refs = refs[grads:]
    if deep:
        weight_ref, grad_ref, low_ref, gain_grad_ref, back_ref = refs
    else:
        grad_ref, gain_grad_ref = refs
    hidden = hidden_ref[...].astype(jnp.float32)
    grad_normed = sum(ref[...] for ref in grad_refs)
    inverse_rms = lax.rsqrt(jnp.mean(hidden * hidden, axis=-1, keepdims=True) + EPSILON)
    straight = hidden * inverse_rms
    gain_part = jnp.sum(grad_normed * straight, axis=0, keepdims=True)

    @pl.when(pl.program_id(0) == 0)
    def _():
        gain_grad_ref[...] = gain_part

    @pl.when(pl.program_id(0) > 0)
    def _():
        gain_grad_ref[...] += gain_part

    scaled = grad_normed * gain_ref[...]
    inner = jnp.mean(scaled * straight, axis=-1, keepdims=True)
    grad = before_ref[...] + inverse_rms * (scaled - straight * inner)
    grad_ref[...] = grad
    if deep:
        rounded = grad.astype(jnp.bfloat16)
        low_ref[...] = rounded
        back_ref[...] = dot(rounded, weight_ref[...], NT).astype(jnp.bfloat16)


def norm_backward(hidden, gain, before, grads, weight):
    rows, model_width = hidden.shape
    block = min(256, rows)
    by_rows = pl.BlockSpec((block, model_width), lambda i: (i, 0))
    in_specs = [by_rows, whole((1, model_width)), by_rows] + [by_rows] * len(grads)
    args = [hidden, gain.reshape(1, model_width), before, *grads]
    out_specs = [by_rows]
    out_shape = [jax.ShapeDtypeStruct((rows, model_width), jnp.float32)]
    if weight is not None:
        in_specs.append(whole(weight.shape))
        args.append(weight)
        out_specs.append(by_rows)
        out_shape.append(jax.ShapeDtypeStruct((rows, model_width), jnp.bfloat16))
    out_specs.append(whole((1, model_width)))
    out_shape.append(jax.ShapeDtypeStruct((1, model_width), jnp.float32))
    if weight is not None:
        out_specs.append(pl.BlockSpec((block, weight.shape[0]), lambda i: (i, 0)))
        out_shape.append(jax.ShapeDtypeStruct((rows, weight.shape[0]), jnp.bfloat16))
    return pl.pallas_call(
        functools.partial(norm_back_kernel, len(grads), weight is not None),
        grid=(rows // block,),
        in_specs=in_specs,
        out_specs=out_specs,
        out_shape=out_shape,
        compiler_params=params(),
        cost_estimate=free(),
    )(*args)


ROOT = 0.7978845608028654
CUBE = 0.044715


def hidden_kernel(block, input_ref, grad_ref, inward_ref, outward_ref, active_ref, back_ref):
    rows = input_ref.shape[0]
    for start in range(0, rows, block):
        here = slice(start, start + block)
        before = dot(input_ref[here, :], inward_ref[...], NN)
        grad_active = dot(grad_ref[here, :], outward_ref[...], NT)
        square = before * before
        bent = jnp.tanh(ROOT * before * (1.0 + CUBE * square))
        half = 0.5 * (1.0 + bent)
        active_ref[here, :] = (before * half).astype(jnp.bfloat16)
        slope = half + 0.5 * before * (1.0 - bent * bent) * (
            ROOT + (3.0 * CUBE * ROOT) * square
        )
        back_ref[here, :] = (grad_active * slope).astype(jnp.bfloat16)


def hidden_both(inputs, grads, inward, outward):
    rows, model_width = inputs.shape
    hidden = inward.shape[1]
    block = min(512, hidden)
    by_hidden = pl.BlockSpec((rows, block), lambda i: (0, i))
    return pl.pallas_call(
        functools.partial(hidden_kernel, min(256, rows)),
        grid=(hidden // block,),
        in_specs=[
            whole(inputs.shape),
            whole(grads.shape),
            pl.BlockSpec((model_width, block), lambda i: (0, i)),
            pl.BlockSpec((block, model_width), lambda i: (i, 0)),
        ],
        out_specs=[by_hidden, by_hidden],
        out_shape=[jax.ShapeDtypeStruct((rows, hidden), jnp.bfloat16)] * 2,
        compiler_params=params(),
        cost_estimate=free(),
    )(inputs, grads, inward, outward)


def products_kernel(groups, *refs):
    count = 2 * sum(groups)
    at = 0
    for out_ref, size in zip(refs[count:], groups):
        total = None
        for _ in range(size):
            former, latter = refs[at], refs[at + 1]
            turned = former.shape[1] != latter.shape[0] or latter.shape[0] == out_ref.shape[1]
            part = dot(former[...], latter[...], NT if turned else NN)
            total = part if total is None else total + part
            at += 2
        out_ref[...] = total


def products(*groups):
    rows = groups[0][0][0].shape[0]
    block = min(256, rows)
    in_specs = []
    args = []
    out_specs = []
    out_shape = []
    for group in groups:
        for former, latter in group:
            in_specs += [
                pl.BlockSpec((block, former.shape[1]), lambda i: (i, 0)),
                whole(latter.shape),
            ]
            args += [former, latter]
        inner = former.shape[1]
        width = latter.shape[1] if latter.shape[0] == inner else latter.shape[0]
        out_specs.append(pl.BlockSpec((block, width), lambda i: (i, 0)))
        out_shape.append(jax.ShapeDtypeStruct((rows, width), jnp.float32))
    return pl.pallas_call(
        functools.partial(products_kernel, tuple(len(group) for group in groups)),
        grid=(rows // block,),
        in_specs=in_specs,
        out_specs=out_specs,
        out_shape=out_shape,
        compiler_params=params(),
        cost_estimate=free(),
    )(*args)


TN = (((0,), (0,)), ((), ()))


def bits_call(kernel, bits, args, in_specs, out_specs, out_shape, steps):
    return pl.pallas_call(
        kernel,
        grid_spec=pltpu.PrefetchScalarGridSpec(
            num_scalar_prefetch=1, grid=(steps,), in_specs=in_specs, out_specs=out_specs
        ),
        out_shape=out_shape,
        compiler_params=params(),
        cost_estimate=free(),
    )(bits, *args)


def tiles_kernel(widths, bits_ref, *refs):
    column = 0
    for number, width in enumerate(widths):
        refs[-1][:, column : column + width] = dot(
            refs[2 * number][...], refs[2 * number + 1][...], TN
        )
        column += width


def half_grad(bits, mine, tiles, bit):
    in_specs = []
    args = []
    rows = tiles[0][0].shape[1] // 2
    for left, right in tiles:
        total, width = right.shape
        in_specs += [
            pl.BlockSpec((total, rows), lambda i, b: (0, b[bit] if mine else 1 - b[bit])),
            pl.BlockSpec((total, width), lambda i, b: (0, 0)),
        ]
        args += [left, right]
    widths = tuple(right.shape[1] for _, right in tiles)
    shape = (rows, sum(widths))
    return bits_call(
        functools.partial(tiles_kernel, widths),
        bits,
        args,
        in_specs,
        pl.BlockSpec(shape, lambda i, b: (0, 0)),
        jax.ShapeDtypeStruct(shape, jnp.float32),
        1,
    )


def whole_grads(tiles):
    return jnp.concatenate(
        [
            lax.dot_general(left, right, TN, preferred_element_type=jnp.float32)
            for left, right in tiles
        ],
        axis=1,
    )


def at_half(where, size):
    return pl.ds(pl.multiple_of(where * size, 8), size)


def by_columns(rows, block):
    return pl.BlockSpec((rows, block), lambda i, b: (0, i))


def split_kernel(bit, bits_ref, keep_ref, other_ref, send_ref, rest_ref):
    size = send_ref.shape[0]
    mine = bits_ref[bit]
    away = at_half(1 - mine, size)
    here = at_half(mine, size)
    send_ref[...] = keep_ref[away, :] + other_ref[away, :]
    rest_ref[...] = keep_ref[here, :] + other_ref[here, :]


def split_sum(bits, keep, other, bit):
    rows, columns = keep.shape
    block = columns // 2
    shape = jax.ShapeDtypeStruct((rows // 2, columns), jnp.float32)
    return bits_call(
        functools.partial(split_kernel, bit),
        bits,
        [keep, other],
        [by_columns(rows, block)] * 2,
        [by_columns(rows // 2, block)] * 2,
        [shape] * 2,
        2,
    )


def add_kernel(bits_ref, former, latter, out_ref):
    out_ref[...] = former[...] + latter[...]


def add_two(bits, former, latter):
    rows, columns = former.shape
    return bits_call(
        add_kernel,
        bits,
        [former, latter],
        [by_columns(rows, columns)] * 2,
        by_columns(rows, columns),
        jax.ShapeDtypeStruct(former.shape, jnp.float32),
        1,
    )


def join_kernel(bit, bits_ref, own_ref, other_ref, out_ref):
    size = own_ref.shape[0]
    out_ref[at_half(bits_ref[bit], size), :] = own_ref[...]
    out_ref[at_half(1 - bits_ref[bit], size), :] = other_ref[...]


def join(bits, own, other, bit):
    rows, columns = own.shape
    block = columns // 2
    return bits_call(
        functools.partial(join_kernel, bit),
        bits,
        [own, other],
        [by_columns(rows, block)] * 2,
        by_columns(2 * rows, block),
        jax.ShapeDtypeStruct((2 * rows, columns), jnp.float32),
        2,
    )


def last_kernel(bit, bits_ref, own_ref, other_ref, *outs):
    size = own_ref.shape[0]
    width = outs[0].shape[1]
    for ref, where in ((own_ref, bits_ref[bit]), (other_ref, 1 - bits_ref[bit])):
        for number in range(3):
            outs[number][at_half(where, size), :] = ref[:, number * width : (number + 1) * width]
        turned = ref[:, 3 * width :].T

        @pl.when(where == 0)
        def _():
            outs[3][:, :size] = turned

        @pl.when(where == 1)
        def _():
            outs[3][:, size:] = turned


def join_four(bits, own, other, bit):
    rows, columns = own.shape
    width = columns // 4
    shapes = [(2 * rows, width)] * 3 + [(width, 2 * rows)]
    return bits_call(
        functools.partial(last_kernel, bit),
        bits,
        [own, other],
        [by_columns(rows, columns)] * 2,
        [pl.BlockSpec(shape, lambda i, b: (0, 0)) for shape in shapes],
        [jax.ShapeDtypeStruct(shape, jnp.float32) for shape in shapes],
        1,
    )


class Order:
    def __init__(self):
        self.last = None

    def after(self, *arrays):
        if self.last is not None:
            arrays = lax.optimization_barrier((*arrays, self.last))[:-1]
        return arrays if len(arrays) > 1 else arrays[0]

    def done(self, array):
        self.last = array
        return array


def core_swap(array):
    return lax.ppermute(array, "tensor", [(0, 1), (1, 0)])


FLIPS = ((1, 2), (2, 1), (4, 12), (8, 4))
KEPT = ((0, 1), (1, 0), (2, 3), (3, 2))
FLAT = ((0, 1), (2, 3))
DEEP = ((2, 3), (0, 1))


def kept_halves():
    chip = lax.axis_index("dp")
    core = lax.axis_index("tensor")
    shifts = jnp.array(KEPT, jnp.int32)
    return (chip >> jnp.where(core == 0, shifts[:, 0], shifts[:, 1])) & 1


def exchange(array, stage):
    pairs = [
        (2 * chip + core, 2 * (chip ^ FLIPS[stage][core]) + core)
        for chip in range(16)
        for core in range(2)
    ]
    return lax.ppermute(array, ("dp", "tensor"), pairs)


def sum_steps(order, bits, tiles, stages, form, result):
    halves, wholes = stages

    def gated():
        left, right = tiles[0]
        return [(order.after(left), right), *tiles[1:]]

    send = order.done(half_grad(bits, False, gated(), halves[0]))
    other = exchange(send, halves[0])
    yield
    rest = order.done(half_grad(bits, True, gated(), halves[0]))
    yield
    for stage in halves[1:]:
        send, rest = split_sum(bits, rest, order.after(other), stage)
        order.done(send)
        other = exchange(send, stage)
        yield
    for stage in wholes:
        rest = order.done(add_two(bits, rest, order.after(other)))
        other = exchange(rest, stage)
        yield
    own = order.done(add_two(bits, rest, order.after(other)))
    for stage in halves[:0:-1]:
        other = exchange(own, stage)
        yield
        own = order.done(join(bits, own, order.after(other), stage))
    other = exchange(own, halves[0])
    yield
    if form == "four":
        result.extend(join_four(bits, own, order.after(other), halves[0]))
    else:
        result.append(join(bits, own, order.after(other), halves[0]))
    order.done(result[0])
    yield


def small_steps(order, array, result):
    for stage in (*FLAT[0], *FLAT[1]):
        array = order.done(array)
        other = exchange(array, stage)
        yield
        array = array + order.after(other)
    result.append(array)
    yield


def matrix_product(former, latter):
    return jnp.dot(former, latter, preferred_element_type=jnp.float32)


def left_contract(former, latter):
    return jnp.einsum("ti,tj->ij", former, latter, preferred_element_type=jnp.float32)


def right_contract(former, latter):
    return jnp.einsum("ti,ji->tj", former, latter, preferred_element_type=jnp.float32)


ROUTES = {"O": DEEP, "I": FLAT, "C": FLAT, "S": FLAT}
PLAN = (
    "O", "O", "Pga3", "I", "NB3", "CB", "C", "C", "Pgi2", "I", "O", "I", "NB2", "C", "I",
    "SB", "C", "S", "Penc", "S", "I", "O", "Py3", "C", "S", "Lout", "O", "Pga1", "I", "S",
    "NB1", "Genc", "m", "C", "I", "m", "O", "C", "S", "I", "m", "O", "S", "m", "C", "S", "S",
    "m", "O",
)


def body(
    decoder_input,
    encoder_output,
    cotangent,
    target_length,
    source_length,
    identifier_tags,
    distance_bucket,
    self_gain,
    self_query,
    self_attention_key,
    self_value,
    self_output,
    position_table,
    cross_gain,
    cross_query,
    cross_key,
    cross_value,
    cross_output,
    hidden_gain,
    hidden_in,
    hidden_out,
):
    item_count, target, model_width = decoder_input.shape
    source = encoder_output.shape[1]
    low = jnp.bfloat16
    cores = lax.axis_size("tensor")
    devices = lax.axis_size("dp")
    order = Order()
    by_hand = devices == 16 and cores == 2
    bits = kept_halves()

    def both(array):
        return [array, core_swap(array)] if cores == 2 else [lax.psum(array, "tensor")]

    def spread(tiles, stages, form="one"):
        result = []
        if by_hand:
            return sum_steps(order, bits, tiles, stages, form, result), result
        total = lax.psum(whole_grads(tiles), "dp")
        width = total.shape[1] // 4
        if form == "four":
            result += [total[:, i * width : (i + 1) * width] for i in range(3)]
            result.append(total[:, 3 * width :].T)
        else:
            result.append(total)
        return iter(()), result

    decoder_rows = decoder_input.reshape(item_count * target, model_width)
    encoder_rows = encoder_output.reshape(item_count * source, model_width)
    lines = bias_lines(distance_bucket, position_table)
    places = jnp.arange(target, dtype=jnp.int32)
    factor = jnp.where(
        places[None, :] < target_length[:, None], 1.0 + identifier_tags.astype(jnp.float32), 0.0
    )
    grad_third = (cotangent.astype(jnp.float32) * factor[:, :, None]).reshape(
        item_count * target, model_width
    )
    grad_branch = grad_third.astype(low)

    input_one, queries_one, keys_one, values_one = norm_forward(
        [decoder_rows], self_gain, [self_query, self_attention_key, self_value]
    )
    exact_one, logs_one = attend(queries_one, keys_one, values_one, target_length, lines)
    mixed_one = exact_one.astype(low)
    parts = both(matrix_product(mixed_one, self_output))
    first, input_two, queries_two = norm_forward(
        [decoder_rows, *parts], cross_gain, [cross_query]
    )
    keys_two = matrix_product(encoder_rows, cross_key).astype(low)
    values_two = matrix_product(encoder_rows, cross_value).astype(low)
    exact_two, logs_two = attend(queries_two, keys_two, values_two, source_length, None)
    mixed_two = exact_two.astype(low)
    parts = both(matrix_product(mixed_two, cross_output))
    second, input_three = norm_forward([first, *parts], hidden_gain, [])

    active, grad_before = hidden_both(input_three, grad_branch, hidden_in, hidden_out)
    held = {}
    sums = {}

    def products_three():
        (part,) = products([(order.after(grad_before), hidden_in)])
        held["grads_three"] = both(order.done(part))

    def back_three():
        held["second"], held["branch_two"], held["hidden_gain"], held["mixed_two"] = norm_backward(
            second, hidden_gain, order.after(grad_third), held["grads_three"], cross_output
        )
        order.done(held["second"])

    def back_cross():
        held["cross"] = attend_back(
            queries_two,
            keys_two,
            values_two,
            order.after(held["mixed_two"]),
            exact_two,
            logs_two,
            source_length,
            None,
        )
        order.done(held["cross"][0])
        begin(
            "C",
            [
                (input_two, held["cross"][0]),
                (encoder_rows, held["cross"][1]),
                (encoder_rows, held["cross"][2]),
                (held["branch_two"], mixed_two),
            ],
            "four",
        )

    def products_two():
        (part,) = products([(order.after(held["cross"][0]), cross_query)])
        held["grads_two"] = both(order.done(part))

    def back_two():
        held["first"], held["branch_one"], held["cross_gain"], held["mixed_one"] = norm_backward(
            first, cross_gain, order.after(held["second"]), held["grads_two"], self_output
        )
        order.done(held["mixed_one"])

    def back_self():
        held["self"] = attend_back(
            queries_one,
            keys_one,
            values_one,
            order.after(held["mixed_one"]),
            exact_one,
            logs_one,
            target_length,
            lines,
        )
        order.done(held["self"][0])
        begin(
            "S",
            [
                (input_one, held["self"][0]),
                (input_one, held["self"][1]),
                (input_one, held["self"][2]),
                (held["branch_one"], mixed_one),
            ],
            "four",
        )

    def products_one():
        (part,) = products(
            [
                (order.after(held["self"][0]), self_query),
                (held["self"][1], self_attention_key),
                (held["self"][2], self_value),
            ]
        )
        held["grads_one"] = both(order.done(part))

    def back_one():
        grad_decoder, held["self_gain"] = norm_backward(
            decoder_rows, self_gain, order.after(held["first"]), held["grads_one"], None
        )
        order.done(grad_decoder)
        held["decoder"] = grad_decoder.reshape(item_count, target, model_width)

    def products_encoder():
        (part,) = products(
            [(order.after(held["cross"][1]), cross_key), (held["cross"][2], cross_value)]
        )
        held["encoder_parts"] = both(order.done(part))

    def encoder_out():
        parts = order.after(*held["encoder_parts"], order.last)[:-1]
        held["encoder"] = order.done(sum(parts).reshape(item_count, source, model_width))

    def products_out():
        (part,) = products([(order.after(active), hidden_out)])
        held["parts_three"] = both(order.done(part))

    def layer_end():
        third = second + sum(order.after(*held["parts_three"], order.last)[:-1])
        held["layer_out"] = order.done(third.astype(low).reshape(item_count, target, model_width))

    def small_begin():
        flat = jnp.concatenate(
            [
                held["self_gain"].reshape(-1),
                held["cross_gain"].reshape(-1),
                held["hidden_gain"].reshape(-1),
                table_grad(held["self"][3], distance_bucket, position_table.shape[0]).reshape(-1),
            ]
        )
        lanes = 512
        flat = jnp.pad(flat, (0, -flat.shape[0] % (8 * lanes))).reshape(-1, lanes)
        flat = order.after(flat)
        if by_hand:
            sums["m"] = []
            return small_steps(order, flat, sums["m"])
        sums["m"] = [lax.psum(flat, "dp")]
        return iter(())

    running = {}

    def begin(name, tiles, form="one"):
        running[name], sums[name] = spread(tiles, ROUTES[name], form)

    begin("O", [(active, grad_branch)])
    begin("I", [(input_three, grad_before)])
    work = dict(
        Pga3=products_three,
        NB3=back_three,
        CB=back_cross,
        Pgi2=products_two,
        NB2=back_two,
        SB=back_self,
        Pga1=products_one,
        NB1=back_one,
        Penc=products_encoder,
        Genc=encoder_out,
        Py3=products_out,
        Lout=layer_end,
    )
    for name in PLAN:
        if name in work:
            work[name]()
        else:
            if name == "m" and "m" not in running:
                running["m"] = small_begin()
            next(running[name], None)
    flat = sums["m"][0].reshape(-1)
    gains = [flat[i * model_width : (i + 1) * model_width] for i in range(3)]
    table = flat[3 * model_width : 3 * model_width + position_table.size].reshape(
        position_table.shape
    )
    return (
        held["layer_out"],
        held["decoder"],
        held["encoder"],
        gains[0],
        *sums["S"],
        table,
        gains[1],
        *sums["C"],
        gains[2],
        *sums["I"],
        *sums["O"],
    )


def solution(mesh):
    by_item = P("dp", None, None)
    columns = P(None, "tensor")
    rows = P("tensor", None)
    attention = (P(), columns, columns, columns, rows)
    return jax.shard_map(
        body,
        mesh=mesh,
        in_specs=(by_item, by_item, by_item, P("dp"), P("dp"), P("dp", None), P())
        + attention
        + (columns,)
        + attention
        + (P(), columns, rows),
        out_specs=(by_item, by_item, by_item)
        + attention
        + (columns,)
        + attention
        + (P(), columns, rows),
        check_vma=False,
    )
```

```python
import functools

import jax
import jax.numpy as jnp
from jax import lax
from jax.experimental import pallas as pl
from jax.experimental.pallas import tpu as pltpu
from jax.sharding import PartitionSpec as P

EPSILON = 1e-06
MASKED = -1e30
LANES = 128
NT = (((1,), (1,)), ((), ()))
NN = (((1,), (0,)), ((), ()))


def dot(a, b, dims):
    return lax.dot_general(a, b, dims, preferred_element_type=jnp.float32)


def head_lane_masks(rows, width, half):
    lane = lax.broadcasted_iota(jnp.int32, (rows, 2 * width), 1)
    return (lane < width) if half == 0 else (lane >= width)


def only_head(array, half):
    width = array.shape[1] // 2
    keep = head_lane_masks(array.shape[0], width, half)
    return jnp.where(keep, array.astype(jnp.float32), 0.0).astype(jnp.bfloat16)


def with_mark(array, half, mark):
    rows, both = array.shape
    width = both // 2
    lane = lax.broadcasted_iota(jnp.int32, (rows, both), 1)
    keep = (lane < width) if half == 0 else (lane >= width)
    place = width if half == 0 else 0
    other = jnp.where(lane == place, mark, 0.0)
    return jnp.where(keep, array.astype(jnp.float32), other).astype(jnp.bfloat16)


def key_marks(key_ref, limit):
    rows, both = key_ref.shape
    row = lax.broadcasted_iota(jnp.int32, (rows, both), 0)
    mark = jnp.where(row < limit, 0.0, MASKED)
    keys = key_ref[...]
    return [with_mark(keys, half, mark) for half in range(2)]


def diagonal_bias(line):
    wide = jnp.broadcast_to(line, (LANES, line.shape[1]))
    return pltpu.roll(wide, 0, 1, stride=1, stride_axis=0)


def forward_kernel(causal, block, limit_ref, query_ref, key_ref, value_ref, *rest):
    if causal:
        line_ref, out_ref, log_ref, key_scr, value_scr, bias_scr = rest
    else:
        out_ref, log_ref, key_scr, value_scr = rest
    value_scr[...] = value_ref[...].T
    keys = key_marks(key_ref, limit_ref[0])
    for half in range(2):
        key_scr[half] = keys[half]
        if causal:
            bias_scr[half] = diagonal_bias(line_ref[0, half : half + 1, :])
    rows = query_ref.shape[0]
    key_total = key_ref.shape[0]
    width = query_ref.shape[1] // 2
    for start in range(0, rows, block):
        keys_here = min(key_total, start + block) if causal else key_total
        queries = query_ref[start : start + block, :]
        outs = []
        for half in range(2):
            marked = with_mark(queries, half, 1.0)
            scores = dot(key_scr[half, :keys_here, :], marked, NT)
            if causal:
                parts = []
                for key_at in range(0, keys_here, LANES):
                    lane_at = start - key_at + LANES
                    parts.append(
                        scores[key_at : key_at + LANES]
                        + bias_scr[half, :, lane_at : lane_at + block]
                    )
                scores = jnp.concatenate(parts, axis=0)
            top = jnp.max(scores, axis=0, keepdims=True)
            raised = jnp.exp(scores - top)
            total = jnp.sum(raised, axis=0, keepdims=True)
            mixed = dot(
                value_scr[half * width : (half + 1) * width, :keys_here],
                raised.astype(jnp.bfloat16),
                NN,
            )
            outs.append(mixed / total)
            log_ref[0, half : half + 1, start : start + block] = top + jnp.log(total)
        out_ref[start : start + block, :] = jnp.concatenate(outs, axis=0).T


def smem():
    return pl.BlockSpec(memory_space=pltpu.SMEM)


def attend(queries, keys, values, limit, lines):
    rows, wide = queries.shape
    key_total = keys.shape[0]
    pairs = wide // LANES
    causal = lines is not None
    block = min(256, rows)
    in_specs = [
        smem(),
        pl.BlockSpec((rows, LANES), lambda p: (0, p)),
        pl.BlockSpec((key_total, LANES), lambda p: (0, p)),
        pl.BlockSpec((key_total, LANES), lambda p: (0, p)),
    ]
    scratch = [
        pltpu.VMEM((2, key_total, LANES), jnp.bfloat16),
        pltpu.VMEM((LANES, key_total), jnp.bfloat16),
    ]
    args = [limit, queries, keys, values]
    if causal:
        in_specs.append(pl.BlockSpec((1, 2, lines.shape[2]), lambda p: (p, 0, 0)))
        scratch.append(pltpu.VMEM((2, LANES, lines.shape[2]), jnp.float32))
        args.append(lines)
    return pl.pallas_call(
        functools.partial(forward_kernel, causal, block),
        grid=(pairs,),
        in_specs=in_specs,
        out_specs=[
            pl.BlockSpec((rows, LANES), lambda p: (0, p)),
            pl.BlockSpec((1, 2, rows), lambda p: (p, 0, 0)),
        ],
        out_shape=[
            jax.ShapeDtypeStruct((rows, wide), jnp.float32),
            jax.ShapeDtypeStruct((pairs, 2, rows), jnp.float32),
        ],
        scratch_shapes=scratch,
        compiler_params=pltpu.CompilerParams(vmem_limit_bytes=32 * 1024 * 1024),
        cost_estimate=free(),
    )(*args)


def backward_kernel(
    causal, block, limit_ref, query_ref, key_ref, value_ref, grad_ref, mixed_ref, log_ref, *rest
):
    if causal:
        line_ref, gq_ref, gk_ref, gv_ref, table_ref, key_scr, key_t_scr, bias_scr, diag_scr, gk_scr, gv_scr = rest
    else:
        gq_ref, gk_ref, gv_ref, key_scr, key_t_scr, gk_scr, gv_scr = rest
    key_t_scr[...] = key_ref[...].T
    keys = key_marks(key_ref, limit_ref[0])
    for half in range(2):
        key_scr[half] = keys[half]
        if causal:
            bias_scr[half] = diagonal_bias(line_ref[0, half : half + 1, :])
            diag_scr[half] = jnp.zeros(diag_scr.shape[1:], jnp.float32)
    gk_scr[...] = jnp.zeros(gk_scr.shape, jnp.float32)
    gv_scr[...] = jnp.zeros(gv_scr.shape, jnp.float32)
    rows = query_ref.shape[0]
    key_total = key_ref.shape[0]
    width = query_ref.shape[1] // 2
    step = 2 * LANES
    for start in range(0, rows, block):
        keys_here = min(key_total, start + block) if causal else key_total
        queries = query_ref[start : start + block, :]
        grads = grad_ref[start : start + block, :]
        inner_t = (grads.astype(jnp.float32) * mixed_ref[start : start + block, :]).T
        query_parts = []
        for half in range(2):
            marked = with_mark(queries, half, 1.0)
            plain = only_head(queries, half)
            grads_here = only_head(grads, half)
            inner = jnp.sum(inner_t[half * width : (half + 1) * width], axis=0, keepdims=True)
            log_total = log_ref[0, half : half + 1, start : start + block]
            grad_queries = jnp.zeros((width, block), jnp.float32)
            for key_at in range(0, keys_here, step):
                here = slice(key_at, key_at + step)
                scores = dot(key_scr[half, here, :], marked, NT)
                if causal:
                    lane_at = start - key_at + LANES
                    bias = jnp.concatenate(
                        [
                            bias_scr[half, :, lane_at : lane_at + block],
                            bias_scr[half, :, lane_at - LANES : lane_at - LANES + block],
                        ],
                        axis=0,
                    )
                    scores = scores + bias
                shares = jnp.exp(scores - log_total)
                grad_shares = dot(value_ref[here, :], grads_here, NT)
                grad_scores = shares * (grad_shares - inner)
                if causal:
                    diag_scr[half, :, lane_at : lane_at + block] += grad_scores[:LANES]
                    diag_scr[half, :, lane_at - LANES : lane_at - LANES + block] += grad_scores[LANES:]
                shares = shares.astype(jnp.bfloat16)
                grad_scores = grad_scores.astype(jnp.bfloat16)
                gv_scr[here, :] += dot(shares, grads_here, NN)
                gk_scr[here, :] += dot(grad_scores, plain, NN)
                grad_queries += dot(key_t_scr[half * width : (half + 1) * width, here], grad_scores, NN)
            query_parts.append(grad_queries)
        gq_ref[start : start + block, :] = (
            jnp.concatenate(query_parts, axis=0).T.astype(jnp.bfloat16)
        )
    gk_ref[...] = gk_scr[...].astype(jnp.bfloat16)
    gv_ref[...] = gv_scr[...].astype(jnp.bfloat16)
    if causal:
        lanes = diag_scr.shape[2]
        down = lax.broadcasted_iota(jnp.int32, (LANES, LANES), 0)
        across = lax.broadcasted_iota(jnp.int32, (LANES, LANES), 1)
        backwards = jnp.where(down + across == LANES - 1, 1.0, 0.0)
        for half in range(2):
            turned = lax.dot_general(
                backwards, diag_scr[half], NN, precision=lax.Precision.HIGHEST
            )
            straight = pltpu.roll(turned, lanes - LANES + 1, 1, stride=1, stride_axis=0)
            table_ref[0, half : half + 1, :] = jnp.sum(straight, axis=0, keepdims=True)


def attend_back(queries, keys, values, grads, mixed, logs, limit, lines):
    rows, wide = queries.shape
    key_total = keys.shape[0]
    pairs = wide // LANES
    causal = lines is not None
    block = min(256, rows)
    tall = pl.BlockSpec((rows, LANES), lambda p: (0, p))
    by_key = pl.BlockSpec((key_total, LANES), lambda p: (0, p))
    in_specs = [
        smem(),
        tall,
        by_key,
        by_key,
        tall,
        tall,
        pl.BlockSpec((1, 2, rows), lambda p: (p, 0, 0)),
    ]
    args = [limit, queries, keys, values, grads, mixed, logs]
    out_specs = [tall, by_key, by_key]
    out_shape = [
        jax.ShapeDtypeStruct((rows, wide), jnp.bfloat16),
        jax.ShapeDtypeStruct((key_total, wide), jnp.bfloat16),
        jax.ShapeDtypeStruct((key_total, wide), jnp.bfloat16),
    ]
    scratch = [
        pltpu.VMEM((2, key_total, LANES), jnp.bfloat16),
        pltpu.VMEM((LANES, key_total), jnp.bfloat16),
    ]
    if causal:
        lanes = lines.shape[2]
        in_specs.append(pl.BlockSpec((1, 2, lanes), lambda p: (p, 0, 0)))
        args.append(lines)
        out_specs.append(pl.BlockSpec((1, 2, lanes), lambda p: (p, 0, 0)))
        out_shape.append(jax.ShapeDtypeStruct((pairs, 2, lanes), jnp.float32))
        scratch += [pltpu.VMEM((2, LANES, lanes), jnp.float32)] * 2
    scratch += [pltpu.VMEM((key_total, LANES), jnp.float32)] * 2
    return pl.pallas_call(
        functools.partial(backward_kernel, causal, block),
        grid=(pairs,),
        in_specs=in_specs,
        out_specs=out_specs,
        out_shape=out_shape,
        scratch_shapes=scratch,
        compiler_params=pltpu.CompilerParams(vmem_limit_bytes=32 * 1024 * 1024),
        cost_estimate=free(),
    )(*args)


def bias_lines(distance_bucket, position_table):
    buckets, heads = position_table.shape
    total = distance_bucket.shape[0]
    hot = distance_bucket[:, None, None] == jnp.arange(buckets)[None, :, None]
    by_distance = jnp.sum(jnp.where(hot, position_table[None], 0.0), axis=1).T
    edge = jnp.full((heads, LANES), MASKED, jnp.float32)
    lines = jnp.concatenate([edge, by_distance, edge], axis=1)
    return lines.reshape(heads // 2, 2, total + 2 * LANES)


def table_grad(lines, distance_bucket, buckets):
    pairs, two, lanes = lines.shape
    by_distance = lines.reshape(pairs * two, lanes)[:, LANES : lanes - LANES]
    hot = distance_bucket[None, :] == jnp.arange(buckets)[:, None]
    return jnp.sum(jnp.where(hot[:, None, :], by_distance[None], 0.0), axis=-1)


def free():
    return pl.CostEstimate(flops=10**11, bytes_accessed=1, transcendentals=1)


def params():
    return pltpu.CompilerParams(vmem_limit_bytes=32 * 1024 * 1024)


def whole(shape):
    zeros = (0,) * len(shape)
    return pl.BlockSpec(shape, lambda i: zeros)


def norm_kernel(terms, products, *refs):
    parts = refs[:terms]
    gain_ref = refs[terms]
    weights = refs[terms + 1 : terms + 1 + products]
    outs = refs[terms + 1 + products :]
    hidden = parts[0][...].astype(jnp.float32)
    if terms > 1:
        hidden = hidden + sum(part[...] for part in parts[1:])
        outs[0][...] = hidden
        outs = outs[1:]
    inverse_rms = lax.rsqrt(jnp.mean(hidden * hidden, axis=-1, keepdims=True) + EPSILON)
    normed = (hidden * inverse_rms * gain_ref[...]).astype(jnp.bfloat16)
    outs[0][...] = normed
    for weight_ref, out_ref in zip(weights, outs[1:]):
        out_ref[...] = dot(normed, weight_ref[...], NN).astype(jnp.bfloat16)


def norm_forward(parts, gain, weights):
    rows, model_width = parts[0].shape
    block = min(256, rows)
    by_rows = pl.BlockSpec((block, model_width), lambda i: (i, 0))
    out_specs = []
    out_shape = []
    if len(parts) > 1:
        out_specs.append(by_rows)
        out_shape.append(jax.ShapeDtypeStruct((rows, model_width), jnp.float32))
    out_specs.append(by_rows)
    out_shape.append(jax.ShapeDtypeStruct((rows, model_width), jnp.bfloat16))
    for weight in weights:
        out_specs.append(pl.BlockSpec((block, weight.shape[1]), lambda i: (i, 0)))
        out_shape.append(jax.ShapeDtypeStruct((rows, weight.shape[1]), jnp.bfloat16))
    return pl.pallas_call(
        functools.partial(norm_kernel, len(parts), len(weights)),
        grid=(rows // block,),
        in_specs=[by_rows] * len(parts)
        + [whole((1, model_width))]
        + [whole(weight.shape) for weight in weights],
        out_specs=out_specs,
        out_shape=out_shape,
        compiler_params=params(),
        cost_estimate=free(),
    )(*parts, gain.reshape(1, model_width), *weights)


def norm_back_kernel(grads, deep, hidden_ref, gain_ref, before_ref, *refs):
    grad_refs = refs[:grads]
    refs = refs[grads:]
    if deep:
        weight_ref, grad_ref, low_ref, gain_grad_ref, back_ref = refs
    else:
        grad_ref, gain_grad_ref = refs
    hidden = hidden_ref[...].astype(jnp.float32)
    grad_normed = sum(ref[...] for ref in grad_refs)
    inverse_rms = lax.rsqrt(jnp.mean(hidden * hidden, axis=-1, keepdims=True) + EPSILON)
    straight = hidden * inverse_rms
    gain_part = jnp.sum(grad_normed * straight, axis=0, keepdims=True)

    @pl.when(pl.program_id(0) == 0)
    def _():
        gain_grad_ref[...] = gain_part

    @pl.when(pl.program_id(0) > 0)
    def _():
        gain_grad_ref[...] += gain_part

    scaled = grad_normed * gain_ref[...]
    inner = jnp.mean(scaled * straight, axis=-1, keepdims=True)
    grad = before_ref[...] + inverse_rms * (scaled - straight * inner)
    grad_ref[...] = grad
    if deep:
        rounded = grad.astype(jnp.bfloat16)
        low_ref[...] = rounded
        back_ref[...] = dot(rounded, weight_ref[...], NT).astype(jnp.bfloat16)


def norm_backward(hidden, gain, before, grads, weight):
    rows, model_width = hidden.shape
    block = min(256, rows)
    by_rows = pl.BlockSpec((block, model_width), lambda i: (i, 0))
    in_specs = [by_rows, whole((1, model_width)), by_rows] + [by_rows] * len(grads)
    args = [hidden, gain.reshape(1, model_width), before, *grads]
    out_specs = [by_rows]
    out_shape = [jax.ShapeDtypeStruct((rows, model_width), jnp.float32)]
    if weight is not None:
        in_specs.append(whole(weight.shape))
        args.append(weight)
        out_specs.append(by_rows)
        out_shape.append(jax.ShapeDtypeStruct((rows, model_width), jnp.bfloat16))
    out_specs.append(whole((1, model_width)))
    out_shape.append(jax.ShapeDtypeStruct((1, model_width), jnp.float32))
    if weight is not None:
        out_specs.append(pl.BlockSpec((block, weight.shape[0]), lambda i: (i, 0)))
        out_shape.append(jax.ShapeDtypeStruct((rows, weight.shape[0]), jnp.bfloat16))
    return pl.pallas_call(
        functools.partial(norm_back_kernel, len(grads), weight is not None),
        grid=(rows // block,),
        in_specs=in_specs,
        out_specs=out_specs,
        out_shape=out_shape,
        compiler_params=params(),
        cost_estimate=free(),
    )(*args)


ROOT = 0.7978845608028654
CUBE = 0.044715


def hidden_kernel(block, input_ref, grad_ref, inward_ref, outward_ref, active_ref, back_ref):
    rows = input_ref.shape[0]
    for start in range(0, rows, block):
        here = slice(start, start + block)
        before = dot(input_ref[here, :], inward_ref[...], NN)
        grad_active = dot(grad_ref[here, :], outward_ref[...], NT)
        square = before * before
        bent = jnp.tanh(ROOT * before * (1.0 + CUBE * square))
        half = 0.5 * (1.0 + bent)
        active_ref[here, :] = (before * half).astype(jnp.bfloat16)
        slope = half + 0.5 * before * (1.0 - bent * bent) * (
            ROOT + (3.0 * CUBE * ROOT) * square
        )
        back_ref[here, :] = (grad_active * slope).astype(jnp.bfloat16)


def hidden_both(inputs, grads, inward, outward):
    rows, model_width = inputs.shape
    hidden = inward.shape[1]
    block = min(512, hidden)
    by_hidden = pl.BlockSpec((rows, block), lambda i: (0, i))
    return pl.pallas_call(
        functools.partial(hidden_kernel, min(256, rows)),
        grid=(hidden // block,),
        in_specs=[
            whole(inputs.shape),
            whole(grads.shape),
            pl.BlockSpec((model_width, block), lambda i: (0, i)),
            pl.BlockSpec((block, model_width), lambda i: (i, 0)),
        ],
        out_specs=[by_hidden, by_hidden],
        out_shape=[jax.ShapeDtypeStruct((rows, hidden), jnp.bfloat16)] * 2,
        compiler_params=params(),
        cost_estimate=free(),
    )(inputs, grads, inward, outward)


def products_kernel(groups, *refs):
    count = 2 * sum(groups)
    at = 0
    for out_ref, size in zip(refs[count:], groups):
        total = None
        for _ in range(size):
            former, latter = refs[at], refs[at + 1]
            turned = former.shape[1] != latter.shape[0] or latter.shape[0] == out_ref.shape[1]
            part = dot(former[...], latter[...], NT if turned else NN)
            total = part if total is None else total + part
            at += 2
        out_ref[...] = total


def products(*groups):
    rows = groups[0][0][0].shape[0]
    block = min(256, rows)
    in_specs = []
    args = []
    out_specs = []
    out_shape = []
    for group in groups:
        for former, latter in group:
            in_specs += [
                pl.BlockSpec((block, former.shape[1]), lambda i: (i, 0)),
                whole(latter.shape),
            ]
            args += [former, latter]
        inner = former.shape[1]
        width = latter.shape[1] if latter.shape[0] == inner else latter.shape[0]
        out_specs.append(pl.BlockSpec((block, width), lambda i: (i, 0)))
        out_shape.append(jax.ShapeDtypeStruct((rows, width), jnp.float32))
    return pl.pallas_call(
        functools.partial(products_kernel, tuple(len(group) for group in groups)),
        grid=(rows // block,),
        in_specs=in_specs,
        out_specs=out_specs,
        out_shape=out_shape,
        compiler_params=params(),
        cost_estimate=free(),
    )(*args)


TN = (((0,), (0,)), ((), ()))


def bits_call(kernel, bits, args, in_specs, out_specs, out_shape, steps):
    return pl.pallas_call(
        kernel,
        grid_spec=pltpu.PrefetchScalarGridSpec(
            num_scalar_prefetch=1, grid=(steps,), in_specs=in_specs, out_specs=out_specs
        ),
        out_shape=out_shape,
        compiler_params=params(),
        cost_estimate=free(),
    )(bits, *args)


def tiles_kernel(widths, bits_ref, *refs):
    column = 0
    for number, width in enumerate(widths):
        refs[-1][:, column : column + width] = dot(
            refs[2 * number][...], refs[2 * number + 1][...], TN
        )
        column += width


def half_grad(bits, mine, tiles, bit):
    in_specs = []
    args = []
    rows = tiles[0][0].shape[1] // 2
    for left, right in tiles:
        total, width = right.shape
        in_specs += [
            pl.BlockSpec((total, rows), lambda i, b: (0, b[bit] if mine else 1 - b[bit])),
            pl.BlockSpec((total, width), lambda i, b: (0, 0)),
        ]
        args += [left, right]
    widths = tuple(right.shape[1] for _, right in tiles)
    shape = (rows, sum(widths))
    return bits_call(
        functools.partial(tiles_kernel, widths),
        bits,
        args,
        in_specs,
        pl.BlockSpec(shape, lambda i, b: (0, 0)),
        jax.ShapeDtypeStruct(shape, jnp.float32),
        1,
    )


def whole_grads(tiles):
    return jnp.concatenate(
        [
            lax.dot_general(left, right, TN, preferred_element_type=jnp.float32)
            for left, right in tiles
        ],
        axis=1,
    )


def at_half(where, size):
    return pl.ds(pl.multiple_of(where * size, 8), size)


def by_columns(rows, block):
    return pl.BlockSpec((rows, block), lambda i, b: (0, i))


def split_kernel(bit, bits_ref, keep_ref, other_ref, send_ref, rest_ref):
    size = send_ref.shape[0]
    mine = bits_ref[bit]
    away = at_half(1 - mine, size)
    here = at_half(mine, size)
    send_ref[...] = keep_ref[away, :] + other_ref[away, :]
    rest_ref[...] = keep_ref[here, :] + other_ref[here, :]


def split_sum(bits, keep, other, bit):
    rows, columns = keep.shape
    block = columns // 2
    shape = jax.ShapeDtypeStruct((rows // 2, columns), jnp.float32)
    return bits_call(
        functools.partial(split_kernel, bit),
        bits,
        [keep, other],
        [by_columns(rows, block)] * 2,
        [by_columns(rows // 2, block)] * 2,
        [shape] * 2,
        2,
    )


def join_kernel(bit, bits_ref, own_ref, other_ref, out_ref):
    size = own_ref.shape[0]
    out_ref[at_half(bits_ref[bit], size), :] = own_ref[...]
    out_ref[at_half(1 - bits_ref[bit], size), :] = other_ref[...]


def join(bits, own, other, bit):
    rows, columns = own.shape
    steps = 3 if rows > 96 else 1
    block = columns // steps
    return bits_call(
        functools.partial(join_kernel, bit),
        bits,
        [own, other],
        [by_columns(rows, block)] * 2,
        by_columns(2 * rows, block),
        jax.ShapeDtypeStruct((2 * rows, columns), jnp.float32),
        steps,
    )


def last_kernel(bit, bits_ref, own_ref, other_ref, *outs):
    size = own_ref.shape[0]
    width = outs[0].shape[1]
    for ref, where in ((own_ref, bits_ref[bit]), (other_ref, 1 - bits_ref[bit])):
        for number in range(3):
            outs[number][at_half(where, size), :] = ref[:, number * width : (number + 1) * width]
        turned = ref[:, 3 * width :].T

        @pl.when(where == 0)
        def _():
            outs[3][:, :size] = turned

        @pl.when(where == 1)
        def _():
            outs[3][:, size:] = turned


def join_four(bits, own, other, bit):
    rows, columns = own.shape
    width = columns // 4
    shapes = [(2 * rows, width)] * 3 + [(width, 2 * rows)]
    return bits_call(
        functools.partial(last_kernel, bit),
        bits,
        [own, other],
        [by_columns(rows, columns)] * 2,
        [pl.BlockSpec(shape, lambda i, b: (0, 0)) for shape in shapes],
        [jax.ShapeDtypeStruct(shape, jnp.float32) for shape in shapes],
        1,
    )


class Order:
    def __init__(self):
        self.last = None

    def after(self, *arrays):
        if self.last is not None:
            arrays = lax.optimization_barrier((*arrays, self.last))[:-1]
        return arrays if len(arrays) > 1 else arrays[0]

    def done(self, array):
        self.last = array
        return array


def core_swap(array):
    return lax.ppermute(array, "tensor", [(0, 1), (1, 0)])


FLIPS = ((1, 2), (2, 1), (4, 12), (8, 4))
KEPT = ((0, 1), (1, 0), (2, 3), (3, 2))
FLAT = ((0, 1, 2, 3), ())
FLAT_WHOLE = ((0, 1), (2, 3))
DEEP = ((2, 3, 0, 1), ())
DEEP_WHOLE = ((2, 3), (0, 1))


def kept_halves():
    chip = lax.axis_index("dp")
    core = lax.axis_index("tensor")
    shifts = jnp.array(KEPT, jnp.int32)
    return (chip >> jnp.where(core == 0, shifts[:, 0], shifts[:, 1])) & 1


def exchange(array, stage):
    pairs = [
        (2 * chip + core, 2 * (chip ^ FLIPS[stage][core]) + core)
        for chip in range(16)
        for core in range(2)
    ]
    return lax.ppermute(array, ("dp", "tensor"), pairs)


def sum_steps(order, bits, tiles, stages, form, result):
    halves, wholes = stages

    def gated():
        left, right = tiles[0]
        return [(order.after(left), right), *tiles[1:]]

    send = order.done(half_grad(bits, False, gated(), halves[0]))
    other = exchange(send, halves[0])
    yield
    rest = order.done(half_grad(bits, True, gated(), halves[0]))
    yield
    for stage in halves[1:]:
        send, rest = split_sum(bits, rest, order.after(other), stage)
        order.done(send)
        other = exchange(send, stage)
        yield
    for stage in wholes:
        rest = order.done(rest + order.after(other))
        other = exchange(rest, stage)
        yield
    own = order.done(rest + order.after(other))
    for stage in halves[:0:-1]:
        other = exchange(own, stage)
        yield
        own = order.done(join(bits, own, order.after(other), stage))
    other = exchange(own, halves[0])
    yield
    if form == "four":
        result.extend(join_four(bits, own, order.after(other), halves[0]))
    else:
        result.append(join(bits, own, order.after(other), halves[0]))
    order.done(result[0])
    yield


def small_steps(order, array, result):
    for stage in FLAT[0]:
        array = order.done(array)
        other = exchange(array, stage)
        yield
        array = array + order.after(other)
    result.append(array)
    yield


def matrix_product(former, latter):
    return jnp.dot(former, latter, preferred_element_type=jnp.float32)


def left_contract(former, latter):
    return jnp.einsum("ti,tj->ij", former, latter, preferred_element_type=jnp.float32)


def right_contract(former, latter):
    return jnp.einsum("ti,ji->tj", former, latter, preferred_element_type=jnp.float32)


ROUTES = {"O": DEEP_WHOLE, "I": FLAT, "C": FLAT, "S": FLAT}
PLAN = (
    "I", "O", "Pga3", "I", "O", "NB3", "CB", "Pgi2", "C", "C", "I", "NB2", "O", "SB", "C",
    "I", "S", "Py3", "C", "I", "Lout", "O", "C", "S", "I", "S", "C", "I", "Penc", "O", "S",
    "Genc", "C", "I", "O", "Pga1", "S", "I", "NB1", "C", "m", "S", "I", "C", "m", "S", "O",
    "S", "S", "m", "C", "O", "m", "S", "m",
)


def body(
    decoder_input,
    encoder_output,
    cotangent,
    target_length,
    source_length,
    identifier_tags,
    distance_bucket,
    self_gain,
    self_query,
    self_attention_key,
    self_value,
    self_output,
    position_table,
    cross_gain,
    cross_query,
    cross_key,
    cross_value,
    cross_output,
    hidden_gain,
    hidden_in,
    hidden_out,
):
    item_count, target, model_width = decoder_input.shape
    source = encoder_output.shape[1]
    low = jnp.bfloat16
    cores = lax.axis_size("tensor")
    devices = lax.axis_size("dp")
    order = Order()
    by_hand = devices == 16 and cores == 2
    bits = kept_halves()

    def both(array):
        return [array, core_swap(array)] if cores == 2 else [lax.psum(array, "tensor")]

    def spread(tiles, stages, form="one"):
        result = []
        if by_hand:
            return sum_steps(order, bits, tiles, stages, form, result), result
        total = lax.psum(whole_grads(tiles), "dp")
        width = total.shape[1] // 4
        if form == "four":
            result += [total[:, i * width : (i + 1) * width] for i in range(3)]
            result.append(total[:, 3 * width :].T)
        else:
            result.append(total)
        return iter(()), result

    decoder_rows = decoder_input.reshape(item_count * target, model_width)
    encoder_rows = encoder_output.reshape(item_count * source, model_width)
    lines = bias_lines(distance_bucket, position_table)
    places = jnp.arange(target, dtype=jnp.int32)
    factor = jnp.where(
        places[None, :] < target_length[:, None], 1.0 + identifier_tags.astype(jnp.float32), 0.0
    )
    grad_third = (cotangent.astype(jnp.float32) * factor[:, :, None]).reshape(
        item_count * target, model_width
    )
    grad_branch = grad_third.astype(low)

    input_one, queries_one, keys_one, values_one = norm_forward(
        [decoder_rows], self_gain, [self_query, self_attention_key, self_value]
    )
    exact_one, logs_one = attend(queries_one, keys_one, values_one, target_length, lines)
    mixed_one = exact_one.astype(low)
    parts = both(matrix_product(mixed_one, self_output))
    first, input_two, queries_two = norm_forward(
        [decoder_rows, *parts], cross_gain, [cross_query]
    )
    keys_two = matrix_product(encoder_rows, cross_key).astype(low)
    values_two = matrix_product(encoder_rows, cross_value).astype(low)
    exact_two, logs_two = attend(queries_two, keys_two, values_two, source_length, None)
    mixed_two = exact_two.astype(low)
    parts = both(matrix_product(mixed_two, cross_output))
    second, input_three = norm_forward([first, *parts], hidden_gain, [])

    active, grad_before = hidden_both(input_three, grad_branch, hidden_in, hidden_out)
    held = {}
    sums = {}

    def products_three():
        (part,) = products([(order.after(grad_before), hidden_in)])
        held["grads_three"] = both(order.done(part))

    def back_three():
        held["second"], held["branch_two"], held["hidden_gain"], held["mixed_two"] = norm_backward(
            second, hidden_gain, order.after(grad_third), held["grads_three"], cross_output
        )
        order.done(held["second"])

    def back_cross():
        held["cross"] = attend_back(
            queries_two,
            keys_two,
            values_two,
            order.after(held["mixed_two"]),
            exact_two,
            logs_two,
            source_length,
            None,
        )
        order.done(held["cross"][0])
        begin(
            "C",
            [
                (input_two, held["cross"][0]),
                (encoder_rows, held["cross"][1]),
                (encoder_rows, held["cross"][2]),
                (held["branch_two"], mixed_two),
            ],
            "four",
        )

    def products_two():
        (part,) = products([(order.after(held["cross"][0]), cross_query)])
        held["grads_two"] = both(order.done(part))

    def back_two():
        held["first"], held["branch_one"], held["cross_gain"], held["mixed_one"] = norm_backward(
            first, cross_gain, order.after(held["second"]), held["grads_two"], self_output
        )
        order.done(held["mixed_one"])

    def back_self():
        held["self"] = attend_back(
            queries_one,
            keys_one,
            values_one,
            order.after(held["mixed_one"]),
            exact_one,
            logs_one,
            target_length,
            lines,
        )
        order.done(held["self"][0])
        begin(
            "S",
            [
                (input_one, held["self"][0]),
                (input_one, held["self"][1]),
                (input_one, held["self"][2]),
                (held["branch_one"], mixed_one),
            ],
            "four",
        )

    def products_one():
        (part,) = products(
            [
                (order.after(held["self"][0]), self_query),
                (held["self"][1], self_attention_key),
                (held["self"][2], self_value),
            ]
        )
        held["grads_one"] = both(order.done(part))

    def back_one():
        grad_decoder, held["self_gain"] = norm_backward(
            decoder_rows, self_gain, order.after(held["first"]), held["grads_one"], None
        )
        order.done(grad_decoder)
        held["decoder"] = grad_decoder.reshape(item_count, target, model_width)

    def products_encoder():
        (part,) = products(
            [(order.after(held["cross"][1]), cross_key), (held["cross"][2], cross_value)]
        )
        held["encoder_parts"] = both(order.done(part))

    def encoder_out():
        parts = order.after(*held["encoder_parts"], order.last)[:-1]
        held["encoder"] = order.done(sum(parts).reshape(item_count, source, model_width))

    def products_out():
        (part,) = products([(order.after(active), hidden_out)])
        held["parts_three"] = both(order.done(part))

    def layer_end():
        third = second + sum(order.after(*held["parts_three"], order.last)[:-1])
        held["layer_out"] = order.done(third.astype(low).reshape(item_count, target, model_width))

    def small_begin():
        flat = jnp.concatenate(
            [
                held["self_gain"].reshape(-1),
                held["cross_gain"].reshape(-1),
                held["hidden_gain"].reshape(-1),
                table_grad(held["self"][3], distance_bucket, position_table.shape[0]).reshape(-1),
            ]
        )
        lanes = 512
        flat = jnp.pad(flat, (0, -flat.shape[0] % (8 * lanes))).reshape(-1, lanes)
        flat = order.after(flat)
        if by_hand:
            sums["m"] = []
            return small_steps(order, flat, sums["m"])
        sums["m"] = [lax.psum(flat, "dp")]
        return iter(())

    running = {}

    def begin(name, tiles, form="one"):
        running[name], sums[name] = spread(tiles, ROUTES[name], form)

    begin("O", [(active, grad_branch)])
    begin("I", [(input_three, grad_before)])
    work = dict(
        Pga3=products_three,
        NB3=back_three,
        CB=back_cross,
        Pgi2=products_two,
        NB2=back_two,
        SB=back_self,
        Pga1=products_one,
        NB1=back_one,
        Penc=products_encoder,
        Genc=encoder_out,
        Py3=products_out,
        Lout=layer_end,
    )
    for name in PLAN:
        if name in work:
            work[name]()
        else:
            if name == "m" and "m" not in running:
                running["m"] = small_begin()
            next(running[name], None)
    flat = sums["m"][0].reshape(-1)
    gains = [flat[i * model_width : (i + 1) * model_width] for i in range(3)]
    table = flat[3 * model_width : 3 * model_width + position_table.size].reshape(
        position_table.shape
    )
    return (
        held["layer_out"],
        held["decoder"],
        held["encoder"],
        gains[0],
        *sums["S"],
        table,
        gains[1],
        *sums["C"],
        gains[2],
        *sums["I"],
        *sums["O"],
    )


def solution(mesh):
    by_item = P("dp", None, None)
    columns = P(None, "tensor")
    rows = P("tensor", None)
    attention = (P(), columns, columns, columns, rows)
    return jax.shard_map(
        body,
        mesh=mesh,
        in_specs=(by_item, by_item, by_item, P("dp"), P("dp"), P("dp", None), P())
        + attention
        + (columns,)
        + attention
        + (P(), columns, rows),
        out_specs=(by_item, by_item, by_item)
        + attention
        + (columns,)
        + attention
        + (P(), columns, rows),
        check_vma=False,
    )
```

```python
import functools

import jax
import jax.numpy as jnp
from jax import lax
from jax.experimental import pallas as pl
from jax.experimental.pallas import tpu as pltpu
from jax.sharding import PartitionSpec as P

EPSILON = 1e-06
MASKED = -1e30
LANES = 128
NT = (((1,), (1,)), ((), ()))
NN = (((1,), (0,)), ((), ()))


def dot(a, b, dims):
    return lax.dot_general(a, b, dims, preferred_element_type=jnp.float32)


def head_lane_masks(rows, width, half):
    lane = lax.broadcasted_iota(jnp.int32, (rows, 2 * width), 1)
    return (lane < width) if half == 0 else (lane >= width)


def only_head(array, half):
    width = array.shape[1] // 2
    keep = head_lane_masks(array.shape[0], width, half)
    return jnp.where(keep, array.astype(jnp.float32), 0.0).astype(jnp.bfloat16)


def with_mark(array, half, mark):
    rows, both = array.shape
    width = both // 2
    lane = lax.broadcasted_iota(jnp.int32, (rows, both), 1)
    keep = (lane < width) if half == 0 else (lane >= width)
    place = width if half == 0 else 0
    other = jnp.where(lane == place, mark, 0.0)
    return jnp.where(keep, array.astype(jnp.float32), other).astype(jnp.bfloat16)


def key_marks(key_ref, limit):
    rows, both = key_ref.shape
    row = lax.broadcasted_iota(jnp.int32, (rows, both), 0)
    mark = jnp.where(row < limit, 0.0, MASKED)
    keys = key_ref[...]
    return [with_mark(keys, half, mark) for half in range(2)]


def diagonal_bias(line):
    wide = jnp.broadcast_to(line, (LANES, line.shape[1]))
    return pltpu.roll(wide, 0, 1, stride=1, stride_axis=0)


def forward_kernel(causal, block, limit_ref, query_ref, key_ref, value_ref, *rest):
    if causal:
        line_ref, out_ref, log_ref, key_scr, value_scr, bias_scr = rest
    else:
        out_ref, log_ref, key_scr, value_scr = rest
    value_scr[...] = value_ref[...].T
    keys = key_marks(key_ref, limit_ref[0])
    for half in range(2):
        key_scr[half] = keys[half]
        if causal:
            bias_scr[half] = diagonal_bias(line_ref[0, half : half + 1, :])
    rows = query_ref.shape[0]
    key_total = key_ref.shape[0]
    width = query_ref.shape[1] // 2
    step = 2 * LANES

    def scores_of(start, half):
        keys_here = min(key_total, start + block) if causal else key_total
        marked = with_mark(query_ref[start : start + block, :], half, 1.0)
        kept = []
        top = None
        for key_at in range(0, keys_here, step):
            scores = dot(key_scr[half, key_at : key_at + step, :], marked, NT)
            if causal:
                lane_at = start - key_at + LANES
                scores = scores + jnp.concatenate(
                    [
                        bias_scr[half, :, lane_at : lane_at + block],
                        bias_scr[half, :, lane_at - LANES : lane_at - LANES + block],
                    ],
                    axis=0,
                )
            kept.append(scores)
            here = jnp.max(scores, axis=0, keepdims=True)
            top = here if top is None else jnp.maximum(top, here)
        return kept, top

    def mix(start, half, kept, top):
        total = None
        for number, scores in enumerate(kept):
            here = slice(number * step, (number + 1) * step)
            raised = jnp.exp(scores - top)
            count = jnp.sum(raised, axis=0, keepdims=True)
            part = dot(
                value_scr[half * width : (half + 1) * width, here],
                raised.astype(jnp.bfloat16),
                NN,
            )
            total, mixed = (count, part) if total is None else (total + count, mixed + part)
        log_ref[0, half : half + 1, start : start + block] = top + jnp.log(total)
        return mixed / total

    units = [(start, half) for start in range(0, rows, block) for half in range(2)]
    outs = []
    waiting = scores_of(*units[0])
    for number, unit in enumerate(units):
        following = scores_of(*units[number + 1]) if number + 1 < len(units) else None
        outs.append(mix(*unit, *waiting))
        waiting = following
        if unit[1] == 1:
            out_ref[unit[0] : unit[0] + block, :] = jnp.concatenate(outs, axis=0).T
            outs = []


def smem():
    return pl.BlockSpec(memory_space=pltpu.SMEM)


def attend(queries, keys, values, limit, lines):
    rows, wide = queries.shape
    key_total = keys.shape[0]
    pairs = wide // LANES
    causal = lines is not None
    block = min(256, rows)
    in_specs = [
        smem(),
        pl.BlockSpec((rows, LANES), lambda p: (0, p)),
        pl.BlockSpec((key_total, LANES), lambda p: (0, p)),
        pl.BlockSpec((key_total, LANES), lambda p: (0, p)),
    ]
    scratch = [
        pltpu.VMEM((2, key_total, LANES), jnp.bfloat16),
        pltpu.VMEM((LANES, key_total), jnp.bfloat16),
    ]
    args = [limit, queries, keys, values]
    if causal:
        in_specs.append(pl.BlockSpec((1, 2, lines.shape[2]), lambda p: (p, 0, 0)))
        scratch.append(pltpu.VMEM((2, LANES, lines.shape[2]), jnp.float32))
        args.append(lines)
    return pl.pallas_call(
        functools.partial(forward_kernel, causal, block),
        grid=(pairs,),
        in_specs=in_specs,
        out_specs=[
            pl.BlockSpec((rows, LANES), lambda p: (0, p)),
            pl.BlockSpec((1, 2, rows), lambda p: (p, 0, 0)),
        ],
        out_shape=[
            jax.ShapeDtypeStruct((rows, wide), jnp.float32),
            jax.ShapeDtypeStruct((pairs, 2, rows), jnp.float32),
        ],
        scratch_shapes=scratch,
        compiler_params=pltpu.CompilerParams(vmem_limit_bytes=32 * 1024 * 1024),
        cost_estimate=free(),
    )(*args)


def backward_kernel(
    causal, block, limit_ref, query_ref, key_ref, value_ref, grad_ref, mixed_ref, log_ref, *rest
):
    if causal:
        line_ref, gq_ref, gk_ref, gv_ref, table_ref, key_scr, key_t_scr, bias_scr, diag_scr, gk_scr, gv_scr = rest
    else:
        gq_ref, gk_ref, gv_ref, key_scr, key_t_scr, gk_scr, gv_scr = rest
    key_t_scr[...] = key_ref[...].T
    keys = key_marks(key_ref, limit_ref[0])
    for half in range(2):
        key_scr[half] = keys[half]
        if causal:
            bias_scr[half] = diagonal_bias(line_ref[0, half : half + 1, :])
            diag_scr[half] = jnp.zeros(diag_scr.shape[1:], jnp.float32)
    gk_scr[...] = jnp.zeros(gk_scr.shape, jnp.float32)
    gv_scr[...] = jnp.zeros(gv_scr.shape, jnp.float32)
    rows = query_ref.shape[0]
    key_total = key_ref.shape[0]
    width = query_ref.shape[1] // 2
    step = 2 * LANES
    def weigh(start, half):
        keys_here = min(key_total, start + block) if causal else key_total
        queries = query_ref[start : start + block, :]
        grads = grad_ref[start : start + block, :]
        product = (grads.astype(jnp.float32) * mixed_ref[start : start + block, :]).T
        inner = jnp.sum(product[half * width : (half + 1) * width], axis=0, keepdims=True)
        marked = with_mark(queries, half, 1.0)
        grads_here = only_head(grads, half)
        log_total = log_ref[0, half : half + 1, start : start + block]
        both = []
        for key_at in range(0, keys_here, step):
            here = slice(key_at, key_at + step)
            scores = dot(key_scr[half, here, :], marked, NT)
            if causal:
                lane_at = start - key_at + LANES
                scores = scores + jnp.concatenate(
                    [
                        bias_scr[half, :, lane_at : lane_at + block],
                        bias_scr[half, :, lane_at - LANES : lane_at - LANES + block],
                    ],
                    axis=0,
                )
            shares = jnp.exp(scores - log_total)
            grad_scores = shares * (dot(value_ref[here, :], grads_here, NT) - inner)
            if causal:
                diag_scr[half, :, lane_at : lane_at + block] += grad_scores[:LANES]
                diag_scr[half, :, lane_at - LANES : lane_at - LANES + block] += grad_scores[LANES:]
            both.append((shares.astype(jnp.bfloat16), grad_scores.astype(jnp.bfloat16)))
        return both, only_head(queries, half), grads_here

    def spread_back(half, both, plain, grads_here):
        total = None
        for number, (shares, grad_scores) in enumerate(both):
            here = slice(number * step, (number + 1) * step)
            gv_scr[here, :] += dot(shares, grads_here, NN)
            gk_scr[here, :] += dot(grad_scores, plain, NN)
            part = dot(key_t_scr[half * width : (half + 1) * width, here], grad_scores, NN)
            total = part if total is None else total + part
        return total

    units = [(start, half) for start in range(0, rows, block) for half in range(2)]
    query_parts = []
    waiting = weigh(*units[0])
    for number, (start, half) in enumerate(units):
        following = weigh(*units[number + 1]) if number + 1 < len(units) else None
        query_parts.append(spread_back(half, *waiting))
        waiting = following
        if half == 1:
            gq_ref[start : start + block, :] = (
                jnp.concatenate(query_parts, axis=0).T.astype(jnp.bfloat16)
            )
            query_parts = []
    gk_ref[...] = gk_scr[...].astype(jnp.bfloat16)
    gv_ref[...] = gv_scr[...].astype(jnp.bfloat16)
    if causal:
        lanes = diag_scr.shape[2]
        down = lax.broadcasted_iota(jnp.int32, (LANES, LANES), 0)
        across = lax.broadcasted_iota(jnp.int32, (LANES, LANES), 1)
        backwards = jnp.where(down + across == LANES - 1, 1.0, 0.0)
        for half in range(2):
            turned = lax.dot_general(
                backwards, diag_scr[half], NN, precision=lax.Precision.HIGHEST
            )
            straight = pltpu.roll(turned, lanes - LANES + 1, 1, stride=1, stride_axis=0)
            table_ref[0, half : half + 1, :] = jnp.sum(straight, axis=0, keepdims=True)


def attend_back(queries, keys, values, grads, mixed, logs, limit, lines):
    rows, wide = queries.shape
    key_total = keys.shape[0]
    pairs = wide // LANES
    causal = lines is not None
    block = min(256, rows)
    tall = pl.BlockSpec((rows, LANES), lambda p: (0, p))
    by_key = pl.BlockSpec((key_total, LANES), lambda p: (0, p))
    in_specs = [
        smem(),
        tall,
        by_key,
        by_key,
        tall,
        tall,
        pl.BlockSpec((1, 2, rows), lambda p: (p, 0, 0)),
    ]
    args = [limit, queries, keys, values, grads, mixed, logs]
    out_specs = [tall, by_key, by_key]
    out_shape = [
        jax.ShapeDtypeStruct((rows, wide), jnp.bfloat16),
        jax.ShapeDtypeStruct((key_total, wide), jnp.bfloat16),
        jax.ShapeDtypeStruct((key_total, wide), jnp.bfloat16),
    ]
    scratch = [
        pltpu.VMEM((2, key_total, LANES), jnp.bfloat16),
        pltpu.VMEM((LANES, key_total), jnp.bfloat16),
    ]
    if causal:
        lanes = lines.shape[2]
        in_specs.append(pl.BlockSpec((1, 2, lanes), lambda p: (p, 0, 0)))
        args.append(lines)
        out_specs.append(pl.BlockSpec((1, 2, lanes), lambda p: (p, 0, 0)))
        out_shape.append(jax.ShapeDtypeStruct((pairs, 2, lanes), jnp.float32))
        scratch += [pltpu.VMEM((2, LANES, lanes), jnp.float32)] * 2
    scratch += [pltpu.VMEM((key_total, LANES), jnp.float32)] * 2
    return pl.pallas_call(
        functools.partial(backward_kernel, causal, block),
        grid=(pairs,),
        in_specs=in_specs,
        out_specs=out_specs,
        out_shape=out_shape,
        scratch_shapes=scratch,
        compiler_params=pltpu.CompilerParams(vmem_limit_bytes=32 * 1024 * 1024),
        cost_estimate=free(),
    )(*args)


def bias_lines(distance_bucket, position_table):
    buckets, heads = position_table.shape
    total = distance_bucket.shape[0]
    hot = distance_bucket[:, None, None] == jnp.arange(buckets)[None, :, None]
    by_distance = jnp.sum(jnp.where(hot, position_table[None], 0.0), axis=1).T
    edge = jnp.full((heads, LANES), MASKED, jnp.float32)
    lines = jnp.concatenate([edge, by_distance, edge], axis=1)
    return lines.reshape(heads // 2, 2, total + 2 * LANES)


def table_grad(lines, distance_bucket, buckets):
    pairs, two, lanes = lines.shape
    by_distance = lines.reshape(pairs * two, lanes)[:, LANES : lanes - LANES]
    hot = distance_bucket[None, :] == jnp.arange(buckets)[:, None]
    return jnp.sum(jnp.where(hot[:, None, :], by_distance[None], 0.0), axis=-1)


def free():
    return pl.CostEstimate(flops=10**11, bytes_accessed=1, transcendentals=1)


def params():
    return pltpu.CompilerParams(vmem_limit_bytes=32 * 1024 * 1024)


def whole(shape):
    zeros = (0,) * len(shape)
    return pl.BlockSpec(shape, lambda i: zeros)


def norm_kernel(terms, products, *refs):
    parts = refs[:terms]
    gain_ref = refs[terms]
    weights = refs[terms + 1 : terms + 1 + products]
    outs = refs[terms + 1 + products :]
    hidden = parts[0][...].astype(jnp.float32)
    if terms > 1:
        hidden = hidden + sum(part[...] for part in parts[1:])
        outs[0][...] = hidden
        outs = outs[1:]
    inverse_rms = lax.rsqrt(jnp.mean(hidden * hidden, axis=-1, keepdims=True) + EPSILON)
    normed = (hidden * inverse_rms * gain_ref[...]).astype(jnp.bfloat16)
    outs[0][...] = normed
    for weight_ref, out_ref in zip(weights, outs[1:]):
        out_ref[...] = dot(normed, weight_ref[...], NN).astype(jnp.bfloat16)


def norm_forward(parts, gain, weights):
    rows, model_width = parts[0].shape
    block = min(256, rows)
    by_rows = pl.BlockSpec((block, model_width), lambda i: (i, 0))
    out_specs = []
    out_shape = []
    if len(parts) > 1:
        out_specs.append(by_rows)
        out_shape.append(jax.ShapeDtypeStruct((rows, model_width), jnp.float32))
    out_specs.append(by_rows)
    out_shape.append(jax.ShapeDtypeStruct((rows, model_width), jnp.bfloat16))
    for weight in weights:
        out_specs.append(pl.BlockSpec((block, weight.shape[1]), lambda i: (i, 0)))
        out_shape.append(jax.ShapeDtypeStruct((rows, weight.shape[1]), jnp.bfloat16))
    return pl.pallas_call(
        functools.partial(norm_kernel, len(parts), len(weights)),
        grid=(rows // block,),
        in_specs=[by_rows] * len(parts)
        + [whole((1, model_width))]
        + [whole(weight.shape) for weight in weights],
        out_specs=out_specs,
        out_shape=out_shape,
        compiler_params=params(),
        cost_estimate=free(),
    )(*parts, gain.reshape(1, model_width), *weights)


def norm_back_kernel(grads, deep, hidden_ref, gain_ref, before_ref, *refs):
    grad_refs = refs[:grads]
    refs = refs[grads:]
    if deep:
        weight_ref, grad_ref, low_ref, gain_grad_ref, back_ref = refs
    else:
        grad_ref, gain_grad_ref = refs
    hidden = hidden_ref[...].astype(jnp.float32)
    grad_normed = sum(ref[...] for ref in grad_refs)
    inverse_rms = lax.rsqrt(jnp.mean(hidden * hidden, axis=-1, keepdims=True) + EPSILON)
    straight = hidden * inverse_rms
    gain_part = jnp.sum(grad_normed * straight, axis=0, keepdims=True)

    @pl.when(pl.program_id(0) == 0)
    def _():
        gain_grad_ref[...] = gain_part

    @pl.when(pl.program_id(0) > 0)
    def _():
        gain_grad_ref[...] += gain_part

    scaled = grad_normed * gain_ref[...]
    inner = jnp.mean(scaled * straight, axis=-1, keepdims=True)
    grad = before_ref[...] + inverse_rms * (scaled - straight * inner)
    grad_ref[...] = grad
    if deep:
        rounded = grad.astype(jnp.bfloat16)
        low_ref[...] = rounded
        back_ref[...] = dot(rounded, weight_ref[...], NT).astype(jnp.bfloat16)


def norm_backward(hidden, gain, before, grads, weight):
    rows, model_width = hidden.shape
    block = min(256, rows)
    by_rows = pl.BlockSpec((block, model_width), lambda i: (i, 0))
    in_specs = [by_rows, whole((1, model_width)), by_rows] + [by_rows] * len(grads)
    args = [hidden, gain.reshape(1, model_width), before, *grads]
    out_specs = [by_rows]
    out_shape = [jax.ShapeDtypeStruct((rows, model_width), jnp.float32)]
    if weight is not None:
        in_specs.append(whole(weight.shape))
        args.append(weight)
        out_specs.append(by_rows)
        out_shape.append(jax.ShapeDtypeStruct((rows, model_width), jnp.bfloat16))
    out_specs.append(whole((1, model_width)))
    out_shape.append(jax.ShapeDtypeStruct((1, model_width), jnp.float32))
    if weight is not None:
        out_specs.append(pl.BlockSpec((block, weight.shape[0]), lambda i: (i, 0)))
        out_shape.append(jax.ShapeDtypeStruct((rows, weight.shape[0]), jnp.bfloat16))
    return pl.pallas_call(
        functools.partial(norm_back_kernel, len(grads), weight is not None),
        grid=(rows // block,),
        in_specs=in_specs,
        out_specs=out_specs,
        out_shape=out_shape,
        compiler_params=params(),
        cost_estimate=free(),
    )(*args)


ROOT = 0.7978845608028654
CUBE = 0.044715


def hidden_kernel(block, input_ref, grad_ref, inward_ref, outward_ref, active_ref, back_ref):
    rows = input_ref.shape[0]
    for start in range(0, rows, block):
        here = slice(start, start + block)
        before = dot(input_ref[here, :], inward_ref[...], NN)
        grad_active = dot(grad_ref[here, :], outward_ref[...], NT)
        square = before * before
        bent = jnp.tanh(ROOT * before * (1.0 + CUBE * square))
        half = 0.5 * (1.0 + bent)
        active_ref[here, :] = (before * half).astype(jnp.bfloat16)
        slope = half + 0.5 * before * (1.0 - bent * bent) * (
            ROOT + (3.0 * CUBE * ROOT) * square
        )
        back_ref[here, :] = (grad_active * slope).astype(jnp.bfloat16)


def hidden_both(inputs, grads, inward, outward):
    rows, model_width = inputs.shape
    hidden = inward.shape[1]
    block = min(512, hidden)
    by_hidden = pl.BlockSpec((rows, block), lambda i: (0, i))
    return pl.pallas_call(
        functools.partial(hidden_kernel, min(256, rows)),
        grid=(hidden // block,),
        in_specs=[
            whole(inputs.shape),
            whole(grads.shape),
            pl.BlockSpec((model_width, block), lambda i: (0, i)),
            pl.BlockSpec((block, model_width), lambda i: (i, 0)),
        ],
        out_specs=[by_hidden, by_hidden],
        out_shape=[jax.ShapeDtypeStruct((rows, hidden), jnp.bfloat16)] * 2,
        compiler_params=params(),
        cost_estimate=free(),
    )(inputs, grads, inward, outward)


def products_kernel(groups, *refs):
    count = 2 * sum(groups)
    at = 0
    for out_ref, size in zip(refs[count:], groups):
        total = None
        for _ in range(size):
            former, latter = refs[at], refs[at + 1]
            turned = former.shape[1] != latter.shape[0] or latter.shape[0] == out_ref.shape[1]
            part = dot(former[...], latter[...], NT if turned else NN)
            total = part if total is None else total + part
            at += 2
        out_ref[...] = total


def products(*groups):
    rows = groups[0][0][0].shape[0]
    block = min(256, rows)
    in_specs = []
    args = []
    out_specs = []
    out_shape = []
    for group in groups:
        for former, latter in group:
            in_specs += [
                pl.BlockSpec((block, former.shape[1]), lambda i: (i, 0)),
                whole(latter.shape),
            ]
            args += [former, latter]
        inner = former.shape[1]
        width = latter.shape[1] if latter.shape[0] == inner else latter.shape[0]
        out_specs.append(pl.BlockSpec((block, width), lambda i: (i, 0)))
        out_shape.append(jax.ShapeDtypeStruct((rows, width), jnp.float32))
    return pl.pallas_call(
        functools.partial(products_kernel, tuple(len(group) for group in groups)),
        grid=(rows // block,),
        in_specs=in_specs,
        out_specs=out_specs,
        out_shape=out_shape,
        compiler_params=params(),
        cost_estimate=free(),
    )(*args)


TN = (((0,), (0,)), ((), ()))


def bits_call(kernel, bits, args, in_specs, out_specs, out_shape, steps):
    return pl.pallas_call(
        kernel,
        grid_spec=pltpu.PrefetchScalarGridSpec(
            num_scalar_prefetch=1, grid=(steps,), in_specs=in_specs, out_specs=out_specs
        ),
        out_shape=out_shape,
        compiler_params=params(),
        cost_estimate=free(),
    )(bits, *args)


def tiles_kernel(widths, bits_ref, *refs):
    column = 0
    for number, width in enumerate(widths):
        refs[-1][:, column : column + width] = dot(
            refs[2 * number][...], refs[2 * number + 1][...], TN
        )
        column += width


def half_grad(bits, mine, tiles, bit):
    in_specs = []
    args = []
    rows = tiles[0][0].shape[1] // 2
    for left, right in tiles:
        total, width = right.shape
        in_specs += [
            pl.BlockSpec((total, rows), lambda i, b: (0, b[bit] if mine else 1 - b[bit])),
            pl.BlockSpec((total, width), lambda i, b: (0, 0)),
        ]
        args += [left, right]
    widths = tuple(right.shape[1] for _, right in tiles)
    shape = (rows, sum(widths))
    return bits_call(
        functools.partial(tiles_kernel, widths),
        bits,
        args,
        in_specs,
        pl.BlockSpec(shape, lambda i, b: (0, 0)),
        jax.ShapeDtypeStruct(shape, jnp.float32),
        1,
    )


def whole_grads(tiles):
    return jnp.concatenate(
        [
            lax.dot_general(left, right, TN, preferred_element_type=jnp.float32)
            for left, right in tiles
        ],
        axis=1,
    )


def at_half(where, size):
    return pl.ds(pl.multiple_of(where * size, 8), size)


def by_columns(rows, block):
    return pl.BlockSpec((rows, block), lambda i, b: (0, i))


def split_kernel(bit, bits_ref, keep_ref, other_ref, send_ref, rest_ref):
    size = send_ref.shape[0]
    mine = bits_ref[bit]
    away = at_half(1 - mine, size)
    here = at_half(mine, size)
    send_ref[...] = keep_ref[away, :] + other_ref[away, :]
    rest_ref[...] = keep_ref[here, :] + other_ref[here, :]


def split_sum(bits, keep, other, bit):
    rows, columns = keep.shape
    block = columns // 2
    shape = jax.ShapeDtypeStruct((rows // 2, columns), jnp.float32)
    return bits_call(
        functools.partial(split_kernel, bit),
        bits,
        [keep, other],
        [by_columns(rows, block)] * 2,
        [by_columns(rows // 2, block)] * 2,
        [shape] * 2,
        2,
    )


def add_kernel(bits_ref, former, latter, out_ref):
    out_ref[...] = former[...] + latter[...]


def add_two(bits, former, latter):
    rows, columns = former.shape
    steps = 2 if rows > 96 else 1
    part = by_columns(rows, columns // steps)
    return bits_call(
        add_kernel,
        bits,
        [former, latter],
        [part] * 2,
        part,
        jax.ShapeDtypeStruct(former.shape, jnp.float32),
        steps,
    )


def join_kernel(bit, bits_ref, own_ref, other_ref, out_ref):
    size = own_ref.shape[0]
    out_ref[at_half(bits_ref[bit], size), :] = own_ref[...]
    out_ref[at_half(1 - bits_ref[bit], size), :] = other_ref[...]


def join(bits, own, other, bit):
    rows, columns = own.shape
    steps = 3 if rows > 96 else 1
    block = columns // steps
    return bits_call(
        functools.partial(join_kernel, bit),
        bits,
        [own, other],
        [by_columns(rows, block)] * 2,
        by_columns(2 * rows, block),
        jax.ShapeDtypeStruct((2 * rows, columns), jnp.float32),
        steps,
    )


def last_kernel(bit, bits_ref, own_ref, other_ref, *outs):
    size = own_ref.shape[0]
    width = outs[0].shape[1]
    for ref, where in ((own_ref, bits_ref[bit]), (other_ref, 1 - bits_ref[bit])):
        for number in range(3):
            outs[number][at_half(where, size), :] = ref[:, number * width : (number + 1) * width]
        turned = ref[:, 3 * width :].T

        @pl.when(where == 0)
        def _():
            outs[3][:, :size] = turned

        @pl.when(where == 1)
        def _():
            outs[3][:, size:] = turned


def join_four(bits, own, other, bit):
    rows, columns = own.shape
    width = columns // 4
    shapes = [(2 * rows, width)] * 3 + [(width, 2 * rows)]
    return bits_call(
        functools.partial(last_kernel, bit),
        bits,
        [own, other],
        [by_columns(rows, columns)] * 2,
        [pl.BlockSpec(shape, lambda i, b: (0, 0)) for shape in shapes],
        [jax.ShapeDtypeStruct(shape, jnp.float32) for shape in shapes],
        1,
    )


class Order:
    def __init__(self):
        self.last = None

    def after(self, *arrays):
        if self.last is not None:
            arrays = lax.optimization_barrier((*arrays, self.last))[:-1]
        return arrays if len(arrays) > 1 else arrays[0]

    def done(self, array):
        self.last = array
        return array


def core_swap(array):
    return lax.ppermute(array, "tensor", [(0, 1), (1, 0)])


FLIPS = ((1, 2), (2, 1), (4, 12), (8, 4))
KEPT = ((0, 1), (1, 0), (2, 3), (3, 2))
FLAT = ((0, 1, 2, 3), ())
FLAT_WHOLE = ((0, 1), (2, 3))
DEEP = ((2, 3, 0, 1), ())
DEEP_WHOLE = ((2, 3), (0, 1))


def kept_halves():
    chip = lax.axis_index("dp")
    core = lax.axis_index("tensor")
    shifts = jnp.array(KEPT, jnp.int32)
    return (chip >> jnp.where(core == 0, shifts[:, 0], shifts[:, 1])) & 1


def exchange(array, stage):
    pairs = [
        (2 * chip + core, 2 * (chip ^ FLIPS[stage][core]) + core)
        for chip in range(16)
        for core in range(2)
    ]
    return lax.ppermute(array, ("dp", "tensor"), pairs)


def sum_steps(order, bits, tiles, stages, form, result):
    halves, wholes = stages

    def gated():
        left, right = tiles[0]
        return [(order.after(left), right), *tiles[1:]]

    send = order.done(half_grad(bits, False, gated(), halves[0]))
    other = exchange(send, halves[0])
    yield
    rest = order.done(half_grad(bits, True, gated(), halves[0]))
    yield
    for stage in halves[1:]:
        send, rest = split_sum(bits, rest, order.after(other), stage)
        order.done(send)
        other = exchange(send, stage)
        yield
    for stage in wholes:
        rest = order.done(rest + order.after(other))
        other = exchange(rest, stage)
        yield
    own = order.done(rest + order.after(other))
    for stage in halves[:0:-1]:
        other = exchange(own, stage)
        yield
        own = order.done(join(bits, own, order.after(other), stage))
    other = exchange(own, halves[0])
    yield
    if form == "four":
        result.extend(join_four(bits, own, order.after(other), halves[0]))
    else:
        result.append(join(bits, own, order.after(other), halves[0]))
    order.done(result[0])
    yield


def small_steps(order, bits, array, result):
    for stage in FLAT[0]:
        array = order.done(array)
        other = exchange(array, stage)
        yield
        array = array + order.after(other)
    result.append(array)
    yield


def matrix_product(former, latter):
    return jnp.dot(former, latter, preferred_element_type=jnp.float32)


def left_contract(former, latter):
    return jnp.einsum("ti,tj->ij", former, latter, preferred_element_type=jnp.float32)


def right_contract(former, latter):
    return jnp.einsum("ti,ji->tj", former, latter, preferred_element_type=jnp.float32)


ROUTES = {"O": DEEP_WHOLE, "I": FLAT, "C": FLAT, "S": FLAT}
PLAN = (
    "I", "O", "Pga3", "I", "O", "NB3", "CB", "Pgi2", "C", "C", "I", "NB2", "O", "SB", "C",
    "I", "S", "Py3", "C", "I", "Lout", "O", "C", "S", "I", "S", "C", "I", "Penc", "O", "S",
    "Genc", "C", "I", "O", "Pga1", "S", "I", "NB1", "C", "m", "S", "I", "C", "m", "S", "O",
    "S", "S", "m", "C", "O", "m", "S", "m",
)


def body(
    decoder_input,
    encoder_output,
    cotangent,
    target_length,
    source_length,
    identifier_tags,
    distance_bucket,
    self_gain,
    self_query,
    self_attention_key,
    self_value,
    self_output,
    position_table,
    cross_gain,
    cross_query,
    cross_key,
    cross_value,
    cross_output,
    hidden_gain,
    hidden_in,
    hidden_out,
):
    item_count, target, model_width = decoder_input.shape
    source = encoder_output.shape[1]
    low = jnp.bfloat16
    cores = lax.axis_size("tensor")
    devices = lax.axis_size("dp")
    order = Order()
    by_hand = devices == 16 and cores == 2
    bits = kept_halves()

    def both(array):
        return [array, core_swap(array)] if cores == 2 else [lax.psum(array, "tensor")]

    def spread(tiles, stages, form="one"):
        result = []
        if by_hand:
            return sum_steps(order, bits, tiles, stages, form, result), result
        total = lax.psum(whole_grads(tiles), "dp")
        width = total.shape[1] // 4
        if form == "four":
            result += [total[:, i * width : (i + 1) * width] for i in range(3)]
            result.append(total[:, 3 * width :].T)
        else:
            result.append(total)
        return iter(()), result

    decoder_rows = decoder_input.reshape(item_count * target, model_width)
    encoder_rows = encoder_output.reshape(item_count * source, model_width)
    lines = bias_lines(distance_bucket, position_table)
    places = jnp.arange(target, dtype=jnp.int32)
    factor = jnp.where(
        places[None, :] < target_length[:, None], 1.0 + identifier_tags.astype(jnp.float32), 0.0
    )
    grad_third = (cotangent.astype(jnp.float32) * factor[:, :, None]).reshape(
        item_count * target, model_width
    )
    grad_branch = grad_third.astype(low)

    input_one, queries_one, keys_one, values_one = norm_forward(
        [decoder_rows], self_gain, [self_query, self_attention_key, self_value]
    )
    exact_one, logs_one = attend(queries_one, keys_one, values_one, target_length, lines)
    mixed_one = exact_one.astype(low)
    parts = both(matrix_product(mixed_one, self_output))
    first, input_two, queries_two = norm_forward(
        [decoder_rows, *parts], cross_gain, [cross_query]
    )
    keys_two = matrix_product(encoder_rows, cross_key).astype(low)
    values_two = matrix_product(encoder_rows, cross_value).astype(low)
    exact_two, logs_two = attend(queries_two, keys_two, values_two, source_length, None)
    mixed_two = exact_two.astype(low)
    parts = both(matrix_product(mixed_two, cross_output))
    second, input_three = norm_forward([first, *parts], hidden_gain, [])

    active, grad_before = hidden_both(input_three, grad_branch, hidden_in, hidden_out)
    held = {}
    sums = {}

    def products_three():
        (part,) = products([(order.after(grad_before), hidden_in)])
        held["grads_three"] = both(order.done(part))

    def back_three():
        held["second"], held["branch_two"], held["hidden_gain"], held["mixed_two"] = norm_backward(
            second, hidden_gain, order.after(grad_third), held["grads_three"], cross_output
        )
        order.done(held["second"])

    def back_cross():
        held["cross"] = attend_back(
            queries_two,
            keys_two,
            values_two,
            order.after(held["mixed_two"]),
            exact_two,
            logs_two,
            source_length,
            None,
        )
        order.done(held["cross"][0])
        begin(
            "C",
            [
                (input_two, held["cross"][0]),
                (encoder_rows, held["cross"][1]),
                (encoder_rows, held["cross"][2]),
                (held["branch_two"], mixed_two),
            ],
            "four",
        )

    def products_two():
        (part,) = products([(order.after(held["cross"][0]), cross_query)])
        held["grads_two"] = both(order.done(part))

    def back_two():
        held["first"], held["branch_one"], held["cross_gain"], held["mixed_one"] = norm_backward(
            first, cross_gain, order.after(held["second"]), held["grads_two"], self_output
        )
        order.done(held["mixed_one"])

    def back_self():
        held["self"] = attend_back(
            queries_one,
            keys_one,
            values_one,
            order.after(held["mixed_one"]),
            exact_one,
            logs_one,
            target_length,
            lines,
        )
        order.done(held["self"][0])
        begin(
            "S",
            [
                (input_one, held["self"][0]),
                (input_one, held["self"][1]),
                (input_one, held["self"][2]),
                (held["branch_one"], mixed_one),
            ],
            "four",
        )

    def products_one():
        (part,) = products(
            [
                (order.after(held["self"][0]), self_query),
                (held["self"][1], self_attention_key),
                (held["self"][2], self_value),
            ]
        )
        held["grads_one"] = both(order.done(part))

    def back_one():
        grad_decoder, held["self_gain"] = norm_backward(
            decoder_rows, self_gain, order.after(held["first"]), held["grads_one"], None
        )
        order.done(grad_decoder)
        held["decoder"] = grad_decoder.reshape(item_count, target, model_width)

    def products_encoder():
        (part,) = products(
            [(order.after(held["cross"][1]), cross_key), (held["cross"][2], cross_value)]
        )
        held["encoder_parts"] = both(order.done(part))

    def encoder_out():
        parts = order.after(*held["encoder_parts"], order.last)[:-1]
        held["encoder"] = order.done(sum(parts).reshape(item_count, source, model_width))

    def products_out():
        (part,) = products([(order.after(active), hidden_out)])
        held["parts_three"] = both(order.done(part))

    def layer_end():
        third = second + sum(order.after(*held["parts_three"], order.last)[:-1])
        held["layer_out"] = order.done(third.astype(low).reshape(item_count, target, model_width))

    def small_begin():
        flat = jnp.concatenate(
            [
                held["self_gain"].reshape(-1),
                held["cross_gain"].reshape(-1),
                held["hidden_gain"].reshape(-1),
                table_grad(held["self"][3], distance_bucket, position_table.shape[0]).reshape(-1),
            ]
        )
        lanes = 512
        flat = jnp.pad(flat, (0, -flat.shape[0] % (8 * lanes))).reshape(-1, lanes)
        flat = order.after(flat)
        if by_hand:
            sums["m"] = []
            return small_steps(order, bits, flat, sums["m"])
        sums["m"] = [lax.psum(flat, "dp")]
        return iter(())

    running = {}

    def begin(name, tiles, form="one"):
        running[name], sums[name] = spread(tiles, ROUTES[name], form)

    begin("O", [(active, grad_branch)])
    begin("I", [(input_three, grad_before)])
    work = dict(
        Pga3=products_three,
        NB3=back_three,
        CB=back_cross,
        Pgi2=products_two,
        NB2=back_two,
        SB=back_self,
        Pga1=products_one,
        NB1=back_one,
        Penc=products_encoder,
        Genc=encoder_out,
        Py3=products_out,
        Lout=layer_end,
    )
    for name in PLAN:
        if name in work:
            work[name]()
        else:
            if name == "m" and "m" not in running:
                running["m"] = small_begin()
            next(running[name], None)
    flat = sums["m"][0].reshape(-1)
    gains = [flat[i * model_width : (i + 1) * model_width] for i in range(3)]
    table = flat[3 * model_width : 3 * model_width + position_table.size].reshape(
        position_table.shape
    )
    return (
        held["layer_out"],
        held["decoder"],
        held["encoder"],
        gains[0],
        *sums["S"],
        table,
        gains[1],
        *sums["C"],
        gains[2],
        *sums["I"],
        *sums["O"],
    )


def solution(mesh):
    by_item = P("dp", None, None)
    columns = P(None, "tensor")
    rows = P("tensor", None)
    attention = (P(), columns, columns, columns, rows)
    return jax.shard_map(
        body,
        mesh=mesh,
        in_specs=(by_item, by_item, by_item, P("dp"), P("dp"), P("dp", None), P())
        + attention
        + (columns,)
        + attention
        + (P(), columns, rows),
        out_specs=(by_item, by_item, by_item)
        + attention
        + (columns,)
        + attention
        + (P(), columns, rows),
        check_vma=False,
    )
```

```python
import functools

import jax
import jax.numpy as jnp
from jax import lax
from jax.experimental import pallas as pl
from jax.experimental.pallas import tpu as pltpu
from jax.sharding import PartitionSpec as P

EPSILON = 1e-06
MASKED = -1e30
LANES = 128
NT = (((1,), (1,)), ((), ()))
NN = (((1,), (0,)), ((), ()))


def dot(a, b, dims):
    return lax.dot_general(a, b, dims, preferred_element_type=jnp.float32)


def head_lane_masks(rows, width, half):
    lane = lax.broadcasted_iota(jnp.int32, (rows, 2 * width), 1)
    return (lane < width) if half == 0 else (lane >= width)


def only_head(array, half):
    width = array.shape[1] // 2
    keep = head_lane_masks(array.shape[0], width, half)
    return jnp.where(keep, array.astype(jnp.float32), 0.0).astype(jnp.bfloat16)


def with_mark(array, half, mark):
    rows, both = array.shape
    width = both // 2
    lane = lax.broadcasted_iota(jnp.int32, (rows, both), 1)
    keep = (lane < width) if half == 0 else (lane >= width)
    place = width if half == 0 else 0
    other = jnp.where(lane == place, mark, 0.0)
    return jnp.where(keep, array.astype(jnp.float32), other).astype(jnp.bfloat16)


def key_marks(key_ref, limit):
    rows, both = key_ref.shape
    row = lax.broadcasted_iota(jnp.int32, (rows, both), 0)
    mark = jnp.where(row < limit, 0.0, MASKED)
    keys = key_ref[...]
    return [with_mark(keys, half, mark) for half in range(2)]


def diagonal_bias(line):
    wide = jnp.broadcast_to(line, (LANES, line.shape[1]))
    return pltpu.roll(wide, 0, 1, stride=1, stride_axis=0)


def forward_kernel(causal, block, limit_ref, query_ref, key_ref, value_ref, *rest):
    if causal:
        line_ref, out_ref, log_ref, key_scr, value_scr, bias_scr = rest
    else:
        out_ref, log_ref, key_scr, value_scr = rest
    value_scr[...] = value_ref[...].T
    keys = key_marks(key_ref, limit_ref[0])
    for half in range(2):
        key_scr[half] = keys[half]
        if causal:
            bias_scr[half] = diagonal_bias(line_ref[0, half : half + 1, :])
    rows = query_ref.shape[0]
    key_total = key_ref.shape[0]
    width = query_ref.shape[1] // 2
    step = 2 * LANES

    def scores_of(start, half):
        keys_here = min(key_total, start + block) if causal else key_total
        marked = with_mark(query_ref[start : start + block, :], half, 1.0)
        kept = []
        top = None
        for key_at in range(0, keys_here, step):
            scores = dot(key_scr[half, key_at : key_at + step, :], marked, NT)
            if causal:
                lane_at = start - key_at + LANES
                scores = scores + jnp.concatenate(
                    [
                        bias_scr[half, :, lane_at : lane_at + block],
                        bias_scr[half, :, lane_at - LANES : lane_at - LANES + block],
                    ],
                    axis=0,
                )
            kept.append(scores)
            here = jnp.max(scores, axis=0, keepdims=True)
            top = here if top is None else jnp.maximum(top, here)
        return kept, top

    def mix(start, half, kept, top):
        total = None
        for number, scores in enumerate(kept):
            here = slice(number * step, (number + 1) * step)
            raised = jnp.exp(scores - top)
            count = jnp.sum(raised, axis=0, keepdims=True)
            part = dot(
                value_scr[half * width : (half + 1) * width, here],
                raised.astype(jnp.bfloat16),
                NN,
            )
            total, mixed = (count, part) if total is None else (total + count, mixed + part)
        log_ref[0, half : half + 1, start : start + block] = top + jnp.log(total)
        return mixed / total

    units = [(start, half) for start in range(0, rows, block) for half in range(2)]
    outs = []
    waiting = scores_of(*units[0])
    for number, unit in enumerate(units):
        following = scores_of(*units[number + 1]) if number + 1 < len(units) else None
        outs.append(mix(*unit, *waiting))
        waiting = following
        if unit[1] == 1:
            out_ref[unit[0] : unit[0] + block, :] = jnp.concatenate(outs, axis=0).T
            outs = []


def smem():
    return pl.BlockSpec(memory_space=pltpu.SMEM)


def attend(queries, keys, values, limit, lines):
    rows, wide = queries.shape
    key_total = keys.shape[0]
    pairs = wide // LANES
    causal = lines is not None
    block = min(256, rows)
    in_specs = [
        smem(),
        pl.BlockSpec((rows, LANES), lambda p: (0, p)),
        pl.BlockSpec((key_total, LANES), lambda p: (0, p)),
        pl.BlockSpec((key_total, LANES), lambda p: (0, p)),
    ]
    scratch = [
        pltpu.VMEM((2, key_total, LANES), jnp.bfloat16),
        pltpu.VMEM((LANES, key_total), jnp.bfloat16),
    ]
    args = [limit, queries, keys, values]
    if causal:
        in_specs.append(pl.BlockSpec((1, 2, lines.shape[2]), lambda p: (p, 0, 0)))
        scratch.append(pltpu.VMEM((2, LANES, lines.shape[2]), jnp.float32))
        args.append(lines)
    return pl.pallas_call(
        functools.partial(forward_kernel, causal, block),
        grid=(pairs,),
        in_specs=in_specs,
        out_specs=[
            pl.BlockSpec((rows, LANES), lambda p: (0, p)),
            pl.BlockSpec((1, 2, rows), lambda p: (p, 0, 0)),
        ],
        out_shape=[
            jax.ShapeDtypeStruct((rows, wide), jnp.float32),
            jax.ShapeDtypeStruct((pairs, 2, rows), jnp.float32),
        ],
        scratch_shapes=scratch,
        compiler_params=pltpu.CompilerParams(vmem_limit_bytes=32 * 1024 * 1024),
        cost_estimate=free(),
    )(*args)


def backward_kernel(
    causal, block, limit_ref, query_ref, key_ref, value_ref, grad_ref, mixed_ref, log_ref, *rest
):
    if causal:
        line_ref, gq_ref, gk_ref, gv_ref, table_ref, key_scr, key_t_scr, bias_scr, diag_scr, gk_scr, gv_scr = rest
    else:
        gq_ref, gk_ref, gv_ref, key_scr, key_t_scr, gk_scr, gv_scr = rest
    key_t_scr[...] = key_ref[...].T
    keys = key_marks(key_ref, limit_ref[0])
    for half in range(2):
        key_scr[half] = keys[half]
        if causal:
            bias_scr[half] = diagonal_bias(line_ref[0, half : half + 1, :])
            diag_scr[half] = jnp.zeros(diag_scr.shape[1:], jnp.float32)
    gk_scr[...] = jnp.zeros(gk_scr.shape, jnp.float32)
    gv_scr[...] = jnp.zeros(gv_scr.shape, jnp.float32)
    rows = query_ref.shape[0]
    key_total = key_ref.shape[0]
    width = query_ref.shape[1] // 2
    step = 2 * LANES
    def weigh(start, half):
        keys_here = min(key_total, start + block) if causal else key_total
        queries = query_ref[start : start + block, :]
        grads = grad_ref[start : start + block, :]
        product = (grads.astype(jnp.float32) * mixed_ref[start : start + block, :]).T
        inner = jnp.sum(product[half * width : (half + 1) * width], axis=0, keepdims=True)
        marked = with_mark(queries, half, 1.0)
        grads_here = only_head(grads, half)
        log_total = log_ref[0, half : half + 1, start : start + block]
        both = []
        for key_at in range(0, keys_here, step):
            here = slice(key_at, key_at + step)
            scores = dot(key_scr[half, here, :], marked, NT)
            if causal:
                lane_at = start - key_at + LANES
                scores = scores + jnp.concatenate(
                    [
                        bias_scr[half, :, lane_at : lane_at + block],
                        bias_scr[half, :, lane_at - LANES : lane_at - LANES + block],
                    ],
                    axis=0,
                )
            shares = jnp.exp(scores - log_total)
            grad_scores = shares * (dot(value_ref[here, :], grads_here, NT) - inner)
            if causal:
                diag_scr[half, :, lane_at : lane_at + block] += grad_scores[:LANES]
                diag_scr[half, :, lane_at - LANES : lane_at - LANES + block] += grad_scores[LANES:]
            both.append((shares.astype(jnp.bfloat16), grad_scores.astype(jnp.bfloat16)))
        return both, only_head(queries, half), grads_here

    def spread_back(half, both, plain, grads_here):
        total = None
        for number, (shares, grad_scores) in enumerate(both):
            here = slice(number * step, (number + 1) * step)
            gv_scr[here, :] += dot(shares, grads_here, NN)
            gk_scr[here, :] += dot(grad_scores, plain, NN)
            part = dot(key_t_scr[half * width : (half + 1) * width, here], grad_scores, NN)
            total = part if total is None else total + part
        return total

    units = [(start, half) for start in range(0, rows, block) for half in range(2)]
    query_parts = []
    waiting = weigh(*units[0])
    for number, (start, half) in enumerate(units):
        following = weigh(*units[number + 1]) if number + 1 < len(units) else None
        query_parts.append(spread_back(half, *waiting))
        waiting = following
        if half == 1:
            gq_ref[start : start + block, :] = (
                jnp.concatenate(query_parts, axis=0).T.astype(jnp.bfloat16)
            )
            query_parts = []
    gk_ref[...] = gk_scr[...].astype(jnp.bfloat16)
    gv_ref[...] = gv_scr[...].astype(jnp.bfloat16)
    if causal:
        lanes = diag_scr.shape[2]
        down = lax.broadcasted_iota(jnp.int32, (LANES, LANES), 0)
        across = lax.broadcasted_iota(jnp.int32, (LANES, LANES), 1)
        backwards = jnp.where(down + across == LANES - 1, 1.0, 0.0)
        for half in range(2):
            turned = lax.dot_general(
                backwards, diag_scr[half], NN, precision=lax.Precision.HIGHEST
            )
            straight = pltpu.roll(turned, lanes - LANES + 1, 1, stride=1, stride_axis=0)
            table_ref[0, half : half + 1, :] = jnp.sum(straight, axis=0, keepdims=True)


def attend_back(queries, keys, values, grads, mixed, logs, limit, lines):
    rows, wide = queries.shape
    key_total = keys.shape[0]
    pairs = wide // LANES
    causal = lines is not None
    block = min(256, rows)
    tall = pl.BlockSpec((rows, LANES), lambda p: (0, p))
    by_key = pl.BlockSpec((key_total, LANES), lambda p: (0, p))
    in_specs = [
        smem(),
        tall,
        by_key,
        by_key,
        tall,
        tall,
        pl.BlockSpec((1, 2, rows), lambda p: (p, 0, 0)),
    ]
    args = [limit, queries, keys, values, grads, mixed, logs]
    out_specs = [tall, by_key, by_key]
    out_shape = [
        jax.ShapeDtypeStruct((rows, wide), jnp.bfloat16),
        jax.ShapeDtypeStruct((key_total, wide), jnp.bfloat16),
        jax.ShapeDtypeStruct((key_total, wide), jnp.bfloat16),
    ]
    scratch = [
        pltpu.VMEM((2, key_total, LANES), jnp.bfloat16),
        pltpu.VMEM((LANES, key_total), jnp.bfloat16),
    ]
    if causal:
        lanes = lines.shape[2]
        in_specs.append(pl.BlockSpec((1, 2, lanes), lambda p: (p, 0, 0)))
        args.append(lines)
        out_specs.append(pl.BlockSpec((1, 2, lanes), lambda p: (p, 0, 0)))
        out_shape.append(jax.ShapeDtypeStruct((pairs, 2, lanes), jnp.float32))
        scratch += [pltpu.VMEM((2, LANES, lanes), jnp.float32)] * 2
    scratch += [pltpu.VMEM((key_total, LANES), jnp.float32)] * 2
    return pl.pallas_call(
        functools.partial(backward_kernel, causal, block),
        grid=(pairs,),
        in_specs=in_specs,
        out_specs=out_specs,
        out_shape=out_shape,
        scratch_shapes=scratch,
        compiler_params=pltpu.CompilerParams(vmem_limit_bytes=32 * 1024 * 1024),
        cost_estimate=free(),
    )(*args)


def bias_lines(distance_bucket, position_table):
    buckets, heads = position_table.shape
    total = distance_bucket.shape[0]
    hot = distance_bucket[:, None, None] == jnp.arange(buckets)[None, :, None]
    by_distance = jnp.sum(jnp.where(hot, position_table[None], 0.0), axis=1).T
    edge = jnp.full((heads, LANES), MASKED, jnp.float32)
    lines = jnp.concatenate([edge, by_distance, edge], axis=1)
    return lines.reshape(heads // 2, 2, total + 2 * LANES)


def table_grad(lines, distance_bucket, buckets):
    pairs, two, lanes = lines.shape
    by_distance = lines.reshape(pairs * two, lanes)[:, LANES : lanes - LANES]
    hot = distance_bucket[None, :] == jnp.arange(buckets)[:, None]
    return jnp.sum(jnp.where(hot[:, None, :], by_distance[None], 0.0), axis=-1)


def free():
    return pl.CostEstimate(flops=10**11, bytes_accessed=1, transcendentals=1)


def params():
    return pltpu.CompilerParams(vmem_limit_bytes=32 * 1024 * 1024)


def whole(shape):
    zeros = (0,) * len(shape)
    return pl.BlockSpec(shape, lambda i: zeros)


def norm_kernel(terms, products, *refs):
    parts = refs[:terms]
    gain_ref = refs[terms]
    weights = refs[terms + 1 : terms + 1 + products]
    outs = refs[terms + 1 + products :]
    hidden = parts[0][...].astype(jnp.float32)
    if terms > 1:
        hidden = hidden + sum(part[...] for part in parts[1:])
        outs[0][...] = hidden
        outs = outs[1:]
    inverse_rms = lax.rsqrt(jnp.mean(hidden * hidden, axis=-1, keepdims=True) + EPSILON)
    normed = (hidden * inverse_rms * gain_ref[...]).astype(jnp.bfloat16)
    outs[0][...] = normed
    for weight_ref, out_ref in zip(weights, outs[1:]):
        out_ref[...] = dot(normed, weight_ref[...], NN).astype(jnp.bfloat16)


def norm_forward(parts, gain, weights):
    rows, model_width = parts[0].shape
    block = min(256, rows)
    by_rows = pl.BlockSpec((block, model_width), lambda i: (i, 0))
    out_specs = []
    out_shape = []
    if len(parts) > 1:
        out_specs.append(by_rows)
        out_shape.append(jax.ShapeDtypeStruct((rows, model_width), jnp.float32))
    out_specs.append(by_rows)
    out_shape.append(jax.ShapeDtypeStruct((rows, model_width), jnp.bfloat16))
    for weight in weights:
        out_specs.append(pl.BlockSpec((block, weight.shape[1]), lambda i: (i, 0)))
        out_shape.append(jax.ShapeDtypeStruct((rows, weight.shape[1]), jnp.bfloat16))
    return pl.pallas_call(
        functools.partial(norm_kernel, len(parts), len(weights)),
        grid=(rows // block,),
        in_specs=[by_rows] * len(parts)
        + [whole((1, model_width))]
        + [whole(weight.shape) for weight in weights],
        out_specs=out_specs,
        out_shape=out_shape,
        compiler_params=params(),
        cost_estimate=free(),
    )(*parts, gain.reshape(1, model_width), *weights)


def norm_back_kernel(grads, deep, hidden_ref, gain_ref, before_ref, *refs):
    grad_refs = refs[:grads]
    refs = refs[grads:]
    if deep:
        weight_ref, grad_ref, low_ref, gain_grad_ref, back_ref = refs
    else:
        grad_ref, gain_grad_ref = refs
    hidden = hidden_ref[...].astype(jnp.float32)
    grad_normed = sum(ref[...] for ref in grad_refs)
    inverse_rms = lax.rsqrt(jnp.mean(hidden * hidden, axis=-1, keepdims=True) + EPSILON)
    straight = hidden * inverse_rms
    gain_part = jnp.sum(grad_normed * straight, axis=0, keepdims=True)

    @pl.when(pl.program_id(0) == 0)
    def _():
        gain_grad_ref[...] = gain_part

    @pl.when(pl.program_id(0) > 0)
    def _():
        gain_grad_ref[...] += gain_part

    scaled = grad_normed * gain_ref[...]
    inner = jnp.mean(scaled * straight, axis=-1, keepdims=True)
    grad = before_ref[...] + inverse_rms * (scaled - straight * inner)
    grad_ref[...] = grad
    if deep:
        rounded = grad.astype(jnp.bfloat16)
        low_ref[...] = rounded
        back_ref[...] = dot(rounded, weight_ref[...], NT).astype(jnp.bfloat16)


def norm_backward(hidden, gain, before, grads, weight):
    rows, model_width = hidden.shape
    block = min(256, rows)
    by_rows = pl.BlockSpec((block, model_width), lambda i: (i, 0))
    in_specs = [by_rows, whole((1, model_width)), by_rows] + [by_rows] * len(grads)
    args = [hidden, gain.reshape(1, model_width), before, *grads]
    out_specs = [by_rows]
    out_shape = [jax.ShapeDtypeStruct((rows, model_width), jnp.float32)]
    if weight is not None:
        in_specs.append(whole(weight.shape))
        args.append(weight)
        out_specs.append(by_rows)
        out_shape.append(jax.ShapeDtypeStruct((rows, model_width), jnp.bfloat16))
    out_specs.append(whole((1, model_width)))
    out_shape.append(jax.ShapeDtypeStruct((1, model_width), jnp.float32))
    if weight is not None:
        out_specs.append(pl.BlockSpec((block, weight.shape[0]), lambda i: (i, 0)))
        out_shape.append(jax.ShapeDtypeStruct((rows, weight.shape[0]), jnp.bfloat16))
    return pl.pallas_call(
        functools.partial(norm_back_kernel, len(grads), weight is not None),
        grid=(rows // block,),
        in_specs=in_specs,
        out_specs=out_specs,
        out_shape=out_shape,
        compiler_params=params(),
        cost_estimate=free(),
    )(*args)


ROOT = 0.7978845608028654
CUBE = 0.044715


def hidden_kernel(block, input_ref, grad_ref, inward_ref, outward_ref, active_ref, back_ref):
    rows = input_ref.shape[0]
    for start in range(0, rows, block):
        here = slice(start, start + block)
        before = dot(input_ref[here, :], inward_ref[...], NN)
        grad_active = dot(grad_ref[here, :], outward_ref[...], NT)
        square = before * before
        bent = jnp.tanh(ROOT * before * (1.0 + CUBE * square))
        half = 0.5 * (1.0 + bent)
        active_ref[here, :] = (before * half).astype(jnp.bfloat16)
        slope = half + 0.5 * before * (1.0 - bent * bent) * (
            ROOT + (3.0 * CUBE * ROOT) * square
        )
        back_ref[here, :] = (grad_active * slope).astype(jnp.bfloat16)


def hidden_both(inputs, grads, inward, outward):
    rows, model_width = inputs.shape
    hidden = inward.shape[1]
    block = min(512, hidden)
    by_hidden = pl.BlockSpec((rows, block), lambda i: (0, i))
    return pl.pallas_call(
        functools.partial(hidden_kernel, min(256, rows)),
        grid=(hidden // block,),
        in_specs=[
            whole(inputs.shape),
            whole(grads.shape),
            pl.BlockSpec((model_width, block), lambda i: (0, i)),
            pl.BlockSpec((block, model_width), lambda i: (i, 0)),
        ],
        out_specs=[by_hidden, by_hidden],
        out_shape=[jax.ShapeDtypeStruct((rows, hidden), jnp.bfloat16)] * 2,
        compiler_params=params(),
        cost_estimate=free(),
    )(inputs, grads, inward, outward)


def products_kernel(groups, *refs):
    count = 2 * sum(groups)
    at = 0
    for out_ref, size in zip(refs[count:], groups):
        total = None
        for _ in range(size):
            former, latter = refs[at], refs[at + 1]
            turned = former.shape[1] != latter.shape[0] or latter.shape[0] == out_ref.shape[1]
            part = dot(former[...], latter[...], NT if turned else NN)
            total = part if total is None else total + part
            at += 2
        out_ref[...] = total


def products(*groups):
    rows = groups[0][0][0].shape[0]
    block = min(256, rows)
    in_specs = []
    args = []
    out_specs = []
    out_shape = []
    for group in groups:
        for former, latter in group:
            in_specs += [
                pl.BlockSpec((block, former.shape[1]), lambda i: (i, 0)),
                whole(latter.shape),
            ]
            args += [former, latter]
        inner = former.shape[1]
        width = latter.shape[1] if latter.shape[0] == inner else latter.shape[0]
        out_specs.append(pl.BlockSpec((block, width), lambda i: (i, 0)))
        out_shape.append(jax.ShapeDtypeStruct((rows, width), jnp.float32))
    return pl.pallas_call(
        functools.partial(products_kernel, tuple(len(group) for group in groups)),
        grid=(rows // block,),
        in_specs=in_specs,
        out_specs=out_specs,
        out_shape=out_shape,
        compiler_params=params(),
        cost_estimate=free(),
    )(*args)


TN = (((0,), (0,)), ((), ()))


def bits_call(kernel, bits, args, in_specs, out_specs, out_shape, steps):
    return pl.pallas_call(
        kernel,
        grid_spec=pltpu.PrefetchScalarGridSpec(
            num_scalar_prefetch=1, grid=(steps,), in_specs=in_specs, out_specs=out_specs
        ),
        out_shape=out_shape,
        compiler_params=params(),
        cost_estimate=free(),
    )(bits, *args)


def tiles_kernel(widths, bits_ref, *refs):
    column = 0
    for number, width in enumerate(widths):
        refs[-1][:, column : column + width] = dot(
            refs[2 * number][...], refs[2 * number + 1][...], TN
        )
        column += width


def half_grad(bits, mine, tiles, bit):
    in_specs = []
    args = []
    rows = tiles[0][0].shape[1] // 2
    for left, right in tiles:
        total, width = right.shape
        in_specs += [
            pl.BlockSpec((total, rows), lambda i, b: (0, b[bit] if mine else 1 - b[bit])),
            pl.BlockSpec((total, width), lambda i, b: (0, 0)),
        ]
        args += [left, right]
    widths = tuple(right.shape[1] for _, right in tiles)
    shape = (rows, sum(widths))
    return bits_call(
        functools.partial(tiles_kernel, widths),
        bits,
        args,
        in_specs,
        pl.BlockSpec(shape, lambda i, b: (0, 0)),
        jax.ShapeDtypeStruct(shape, jnp.float32),
        1,
    )


def whole_grads(tiles):
    return jnp.concatenate(
        [
            lax.dot_general(left, right, TN, preferred_element_type=jnp.float32)
            for left, right in tiles
        ],
        axis=1,
    )


def at_half(where, size):
    return pl.ds(pl.multiple_of(where * size, 8), size)


def by_columns(rows, block):
    return pl.BlockSpec((rows, block), lambda i, b: (0, i))


def split_kernel(bit, bits_ref, keep_ref, other_ref, send_ref, rest_ref):
    size = send_ref.shape[0]
    mine = bits_ref[bit]
    away = at_half(1 - mine, size)
    here = at_half(mine, size)
    send_ref[...] = keep_ref[away, :] + other_ref[away, :]
    rest_ref[...] = keep_ref[here, :] + other_ref[here, :]


def split_sum(bits, keep, other, bit):
    rows, columns = keep.shape
    block = columns // 2
    shape = jax.ShapeDtypeStruct((rows // 2, columns), jnp.float32)
    return bits_call(
        functools.partial(split_kernel, bit),
        bits,
        [keep, other],
        [by_columns(rows, block)] * 2,
        [by_columns(rows // 2, block)] * 2,
        [shape] * 2,
        2,
    )


def add_kernel(bits_ref, former, latter, out_ref):
    out_ref[...] = former[...] + latter[...]


def add_two(bits, former, latter):
    rows, columns = former.shape
    steps = 2 if rows > 96 else 1
    part = by_columns(rows, columns // steps)
    return bits_call(
        add_kernel,
        bits,
        [former, latter],
        [part] * 2,
        part,
        jax.ShapeDtypeStruct(former.shape, jnp.float32),
        steps,
    )


def join_kernel(bit, bits_ref, own_ref, other_ref, out_ref):
    size = own_ref.shape[0]
    out_ref[at_half(bits_ref[bit], size), :] = own_ref[...]
    out_ref[at_half(1 - bits_ref[bit], size), :] = other_ref[...]


def join(bits, own, other, bit):
    rows, columns = own.shape
    steps = 3 if rows > 96 else 1
    block = columns // steps
    return bits_call(
        functools.partial(join_kernel, bit),
        bits,
        [own, other],
        [by_columns(rows, block)] * 2,
        by_columns(2 * rows, block),
        jax.ShapeDtypeStruct((2 * rows, columns), jnp.float32),
        steps,
    )


def last_kernel(bit, bits_ref, own_ref, other_ref, *outs):
    size = own_ref.shape[0]
    width = outs[0].shape[1]
    for ref, where in ((own_ref, bits_ref[bit]), (other_ref, 1 - bits_ref[bit])):
        for number in range(3):
            outs[number][at_half(where, size), :] = ref[:, number * width : (number + 1) * width]
        turned = ref[:, 3 * width :].T

        @pl.when(where == 0)
        def _():
            outs[3][:, :size] = turned

        @pl.when(where == 1)
        def _():
            outs[3][:, size:] = turned


def join_four(bits, own, other, bit):
    rows, columns = own.shape
    width = columns // 4
    shapes = [(2 * rows, width)] * 3 + [(width, 2 * rows)]
    return bits_call(
        functools.partial(last_kernel, bit),
        bits,
        [own, other],
        [by_columns(rows, columns)] * 2,
        [pl.BlockSpec(shape, lambda i, b: (0, 0)) for shape in shapes],
        [jax.ShapeDtypeStruct(shape, jnp.float32) for shape in shapes],
        1,
    )


class Order:
    def __init__(self):
        self.last = None

    def after(self, *arrays):
        if self.last is not None:
            arrays = lax.optimization_barrier((*arrays, self.last))[:-1]
        return arrays if len(arrays) > 1 else arrays[0]

    def done(self, array):
        self.last = array
        return array


def core_swap(array):
    return lax.ppermute(array, "tensor", [(0, 1), (1, 0)])


FLIPS = ((1, 2), (2, 1), (4, 12), (8, 4))
KEPT = ((0, 1), (1, 0), (2, 3), (3, 2))
FLAT = ((0, 1, 2, 3), ())
FLAT_WHOLE = ((0, 1), (2, 3))
DEEP = ((2, 3, 0, 1), ())
DEEP_WHOLE = ((2, 3), (0, 1))


def kept_halves():
    chip = lax.axis_index("dp")
    core = lax.axis_index("tensor")
    shifts = jnp.array(KEPT, jnp.int32)
    return (chip >> jnp.where(core == 0, shifts[:, 0], shifts[:, 1])) & 1


def exchange(array, stage):
    pairs = [
        (2 * chip + core, 2 * (chip ^ FLIPS[stage][core]) + core)
        for chip in range(16)
        for core in range(2)
    ]
    return lax.ppermute(array, ("dp", "tensor"), pairs)


def sum_steps(order, bits, tiles, stages, form, result):
    halves, wholes = stages

    def gated():
        left, right = tiles[0]
        return [(order.after(left), right), *tiles[1:]]

    send = order.done(half_grad(bits, False, gated(), halves[0]))
    other = exchange(send, halves[0])
    yield
    rest = order.done(half_grad(bits, True, gated(), halves[0]))
    yield
    for stage in halves[1:]:
        send, rest = split_sum(bits, rest, order.after(other), stage)
        order.done(send)
        other = exchange(send, stage)
        yield
    for stage in wholes:
        rest = order.done(rest + order.after(other))
        other = exchange(rest, stage)
        yield
    own = order.done(rest + order.after(other))
    for stage in halves[:0:-1]:
        other = exchange(own, stage)
        yield
        own = order.done(join(bits, own, order.after(other), stage))
    other = exchange(own, halves[0])
    yield
    if form == "four":
        result.extend(join_four(bits, own, order.after(other), halves[0]))
    else:
        result.append(join(bits, own, order.after(other), halves[0]))
    order.done(result[0])
    yield


def small_steps(order, bits, array, result):
    for stage in FLAT[0]:
        array = order.done(array)
        other = exchange(array, stage)
        yield
        array = array + order.after(other)
    result.append(array)
    yield


def matrix_product(former, latter):
    return jnp.dot(former, latter, preferred_element_type=jnp.float32)


def left_contract(former, latter):
    return jnp.einsum("ti,tj->ij", former, latter, preferred_element_type=jnp.float32)


def right_contract(former, latter):
    return jnp.einsum("ti,ji->tj", former, latter, preferred_element_type=jnp.float32)


ROUTES = {"O": DEEP_WHOLE, "I": FLAT, "C": FLAT, "S": FLAT}
PLAN = (
    "I", "Pga3", "O", "O", "I", "NB3", "CB", "Pgi2", "C", "C", "I", "NB2", "O", "SB", "C",
    "I", "S", "Py3", "C", "I", "Lout", "O", "C", "S", "I", "S", "C", "I", "Penc", "O", "S",
    "Genc", "C", "I", "O", "Pga1", "S", "I", "NB1", "C", "m", "S", "C", "m", "S", "O", "S",
    "I", "S", "m", "C", "m", "S", "m", "O",
)


def body(
    decoder_input,
    encoder_output,
    cotangent,
    target_length,
    source_length,
    identifier_tags,
    distance_bucket,
    self_gain,
    self_query,
    self_attention_key,
    self_value,
    self_output,
    position_table,
    cross_gain,
    cross_query,
    cross_key,
    cross_value,
    cross_output,
    hidden_gain,
    hidden_in,
    hidden_out,
):
    item_count, target, model_width = decoder_input.shape
    source = encoder_output.shape[1]
    low = jnp.bfloat16
    cores = lax.axis_size("tensor")
    devices = lax.axis_size("dp")
    order = Order()
    by_hand = devices == 16 and cores == 2
    bits = kept_halves()

    def both(array):
        return [array, core_swap(array)] if cores == 2 else [lax.psum(array, "tensor")]

    def spread(tiles, stages, form="one"):
        result = []
        if by_hand:
            return sum_steps(order, bits, tiles, stages, form, result), result
        total = lax.psum(whole_grads(tiles), "dp")
        width = total.shape[1] // 4
        if form == "four":
            result += [total[:, i * width : (i + 1) * width] for i in range(3)]
            result.append(total[:, 3 * width :].T)
        else:
            result.append(total)
        return iter(()), result

    decoder_rows = decoder_input.reshape(item_count * target, model_width)
    encoder_rows = encoder_output.reshape(item_count * source, model_width)
    lines = bias_lines(distance_bucket, position_table)
    places = jnp.arange(target, dtype=jnp.int32)
    factor = jnp.where(
        places[None, :] < target_length[:, None], 1.0 + identifier_tags.astype(jnp.float32), 0.0
    )
    grad_third = (cotangent.astype(jnp.float32) * factor[:, :, None]).reshape(
        item_count * target, model_width
    )
    grad_branch = grad_third.astype(low)

    input_one, queries_one, keys_one, values_one = norm_forward(
        [decoder_rows], self_gain, [self_query, self_attention_key, self_value]
    )
    exact_one, logs_one = attend(queries_one, keys_one, values_one, target_length, lines)
    mixed_one = exact_one.astype(low)
    parts = both(matrix_product(mixed_one, self_output))
    first, input_two, queries_two = norm_forward(
        [decoder_rows, *parts], cross_gain, [cross_query]
    )
    keys_two = matrix_product(encoder_rows, cross_key).astype(low)
    values_two = matrix_product(encoder_rows, cross_value).astype(low)
    exact_two, logs_two = attend(queries_two, keys_two, values_two, source_length, None)
    mixed_two = exact_two.astype(low)
    parts = both(matrix_product(mixed_two, cross_output))
    second, input_three = norm_forward([first, *parts], hidden_gain, [])

    active, grad_before = hidden_both(input_three, grad_branch, hidden_in, hidden_out)
    held = {}
    sums = {}

    def products_three():
        (part,) = products([(order.after(grad_before), hidden_in)])
        held["grads_three"] = both(order.done(part))

    def back_three():
        held["second"], held["branch_two"], held["hidden_gain"], held["mixed_two"] = norm_backward(
            second, hidden_gain, order.after(grad_third), held["grads_three"], cross_output
        )
        order.done(held["second"])

    def back_cross():
        held["cross"] = attend_back(
            queries_two,
            keys_two,
            values_two,
            order.after(held["mixed_two"]),
            exact_two,
            logs_two,
            source_length,
            None,
        )
        order.done(held["cross"][0])
        begin(
            "C",
            [
                (input_two, held["cross"][0]),
                (encoder_rows, held["cross"][1]),
                (encoder_rows, held["cross"][2]),
                (held["branch_two"], mixed_two),
            ],
            "four",
        )

    def products_two():
        (part,) = products([(order.after(held["cross"][0]), cross_query)])
        held["grads_two"] = both(order.done(part))

    def back_two():
        held["first"], held["branch_one"], held["cross_gain"], held["mixed_one"] = norm_backward(
            first, cross_gain, order.after(held["second"]), held["grads_two"], self_output
        )
        order.done(held["mixed_one"])

    def back_self():
        held["self"] = attend_back(
            queries_one,
            keys_one,
            values_one,
            order.after(held["mixed_one"]),
            exact_one,
            logs_one,
            target_length,
            lines,
        )
        order.done(held["self"][0])
        begin(
            "S",
            [
                (input_one, held["self"][0]),
                (input_one, held["self"][1]),
                (input_one, held["self"][2]),
                (held["branch_one"], mixed_one),
            ],
            "four",
        )

    def products_one():
        (part,) = products(
            [
                (order.after(held["self"][0]), self_query),
                (held["self"][1], self_attention_key),
                (held["self"][2], self_value),
            ]
        )
        held["grads_one"] = both(order.done(part))

    def back_one():
        grad_decoder, held["self_gain"] = norm_backward(
            decoder_rows, self_gain, order.after(held["first"]), held["grads_one"], None
        )
        order.done(grad_decoder)
        held["decoder"] = grad_decoder.reshape(item_count, target, model_width)

    def products_encoder():
        (part,) = products(
            [(order.after(held["cross"][1]), cross_key), (held["cross"][2], cross_value)]
        )
        held["encoder_parts"] = both(order.done(part))

    def encoder_out():
        parts = order.after(*held["encoder_parts"], order.last)[:-1]
        held["encoder"] = order.done(sum(parts).reshape(item_count, source, model_width))

    def products_out():
        (part,) = products([(order.after(active), hidden_out)])
        held["parts_three"] = both(order.done(part))

    def layer_end():
        third = second + sum(order.after(*held["parts_three"], order.last)[:-1])
        held["layer_out"] = order.done(third.astype(low).reshape(item_count, target, model_width))

    def small_begin():
        flat = jnp.concatenate(
            [
                held["self_gain"].reshape(-1),
                held["cross_gain"].reshape(-1),
                held["hidden_gain"].reshape(-1),
                table_grad(held["self"][3], distance_bucket, position_table.shape[0]).reshape(-1),
            ]
        )
        lanes = 512
        flat = jnp.pad(flat, (0, -flat.shape[0] % (8 * lanes))).reshape(-1, lanes)
        flat = order.after(flat)
        if by_hand:
            sums["m"] = []
            return small_steps(order, bits, flat, sums["m"])
        sums["m"] = [lax.psum(flat, "dp")]
        return iter(())

    running = {}

    def begin(name, tiles, form="one"):
        running[name], sums[name] = spread(tiles, ROUTES[name], form)

    begin("O", [(active, grad_branch)])
    begin("I", [(input_three, grad_before)])
    work = dict(
        Pga3=products_three,
        NB3=back_three,
        CB=back_cross,
        Pgi2=products_two,
        NB2=back_two,
        SB=back_self,
        Pga1=products_one,
        NB1=back_one,
        Penc=products_encoder,
        Genc=encoder_out,
        Py3=products_out,
        Lout=layer_end,
    )
    for name in PLAN:
        if name in work:
            work[name]()
        else:
            if name == "m" and "m" not in running:
                running["m"] = small_begin()
            next(running[name], None)
    flat = sums["m"][0].reshape(-1)
    gains = [flat[i * model_width : (i + 1) * model_width] for i in range(3)]
    table = flat[3 * model_width : 3 * model_width + position_table.size].reshape(
        position_table.shape
    )
    return (
        held["layer_out"],
        held["decoder"],
        held["encoder"],
        gains[0],
        *sums["S"],
        table,
        gains[1],
        *sums["C"],
        gains[2],
        *sums["I"],
        *sums["O"],
    )


def solution(mesh):
    by_item = P("dp", None, None)
    columns = P(None, "tensor")
    rows = P("tensor", None)
    attention = (P(), columns, columns, columns, rows)
    return jax.shard_map(
        body,
        mesh=mesh,
        in_specs=(by_item, by_item, by_item, P("dp"), P("dp"), P("dp", None), P())
        + attention
        + (columns,)
        + attention
        + (P(), columns, rows),
        out_specs=(by_item, by_item, by_item)
        + attention
        + (columns,)
        + attention
        + (P(), columns, rows),
        check_vma=False,
    )
```

```python
import functools

import jax
import jax.numpy as jnp
from jax import lax
from jax.experimental import pallas as pl
from jax.experimental.pallas import tpu as pltpu
from jax.sharding import PartitionSpec as P

EPSILON = 1e-06
MASKED = -1e30
LANES = 128
NT = (((1,), (1,)), ((), ()))
NN = (((1,), (0,)), ((), ()))


def dot(a, b, dims):
    return lax.dot_general(a, b, dims, preferred_element_type=jnp.float32)


def head_lane_masks(rows, width, half):
    lane = lax.broadcasted_iota(jnp.int32, (rows, 2 * width), 1)
    return (lane < width) if half == 0 else (lane >= width)


def only_head(array, half):
    width = array.shape[1] // 2
    keep = head_lane_masks(array.shape[0], width, half)
    return jnp.where(keep, array.astype(jnp.float32), 0.0).astype(jnp.bfloat16)


def with_mark(array, half, mark):
    rows, both = array.shape
    width = both // 2
    lane = lax.broadcasted_iota(jnp.int32, (rows, both), 1)
    keep = (lane < width) if half == 0 else (lane >= width)
    place = width if half == 0 else 0
    other = jnp.where(lane == place, mark, 0.0)
    return jnp.where(keep, array.astype(jnp.float32), other).astype(jnp.bfloat16)


def key_marks(key_ref, limit):
    rows, both = key_ref.shape
    row = lax.broadcasted_iota(jnp.int32, (rows, both), 0)
    mark = jnp.where(row < limit, 0.0, MASKED)
    keys = key_ref[...]
    return [with_mark(keys, half, mark) for half in range(2)]


def diagonal_bias(line):
    wide = jnp.broadcast_to(line, (LANES, line.shape[1]))
    return pltpu.roll(wide, 0, 1, stride=1, stride_axis=0)


def forward_kernel(causal, block, limit_ref, query_ref, key_ref, value_ref, *rest):
    if causal:
        line_ref, out_ref, log_ref, key_scr, value_scr, bias_scr = rest
    else:
        out_ref, log_ref, key_scr, value_scr = rest
    value_scr[...] = value_ref[...].T
    keys = key_marks(key_ref, limit_ref[0])
    for half in range(2):
        key_scr[half] = keys[half]
        if causal:
            bias_scr[half] = diagonal_bias(line_ref[0, half : half + 1, :])
    rows = query_ref.shape[0]
    key_total = key_ref.shape[0]
    width = query_ref.shape[1] // 2
    step = 2 * LANES

    def scores_of(start, half):
        keys_here = min(key_total, start + block) if causal else key_total
        marked = with_mark(query_ref[start : start + block, :], half, 1.0)
        kept = []
        top = None
        for key_at in range(0, keys_here, step):
            scores = dot(key_scr[half, key_at : key_at + step, :], marked, NT)
            if causal:
                lane_at = start - key_at + LANES
                scores = scores + jnp.concatenate(
                    [
                        bias_scr[half, :, lane_at : lane_at + block],
                        bias_scr[half, :, lane_at - LANES : lane_at - LANES + block],
                    ],
                    axis=0,
                )
            kept.append(scores)
            here = jnp.max(scores, axis=0, keepdims=True)
            top = here if top is None else jnp.maximum(top, here)
        return kept, top

    def mix(start, half, kept, top):
        total = None
        for number, scores in enumerate(kept):
            here = slice(number * step, (number + 1) * step)
            raised = jnp.exp(scores - top)
            count = jnp.sum(raised, axis=0, keepdims=True)
            part = dot(
                value_scr[half * width : (half + 1) * width, here],
                raised.astype(jnp.bfloat16),
                NN,
            )
            total, mixed = (count, part) if total is None else (total + count, mixed + part)
        log_ref[0, half : half + 1, start : start + block] = top + jnp.log(total)
        return mixed / total

    units = [(start, half) for start in range(0, rows, block) for half in range(2)]
    outs = []
    waiting = scores_of(*units[0])
    for number, unit in enumerate(units):
        following = scores_of(*units[number + 1]) if number + 1 < len(units) else None
        outs.append(mix(*unit, *waiting))
        waiting = following
        if unit[1] == 1:
            out_ref[unit[0] : unit[0] + block, :] = jnp.concatenate(outs, axis=0).T
            outs = []


def smem():
    return pl.BlockSpec(memory_space=pltpu.SMEM)


def attend(queries, keys, values, limit, lines):
    rows, wide = queries.shape
    key_total = keys.shape[0]
    pairs = wide // LANES
    causal = lines is not None
    block = min(256, rows)
    in_specs = [
        smem(),
        pl.BlockSpec((rows, LANES), lambda p: (0, p)),
        pl.BlockSpec((key_total, LANES), lambda p: (0, p)),
        pl.BlockSpec((key_total, LANES), lambda p: (0, p)),
    ]
    scratch = [
        pltpu.VMEM((2, key_total, LANES), jnp.bfloat16),
        pltpu.VMEM((LANES, key_total), jnp.bfloat16),
    ]
    args = [limit, queries, keys, values]
    if causal:
        in_specs.append(pl.BlockSpec((1, 2, lines.shape[2]), lambda p: (p, 0, 0)))
        scratch.append(pltpu.VMEM((2, LANES, lines.shape[2]), jnp.float32))
        args.append(lines)
    return pl.pallas_call(
        functools.partial(forward_kernel, causal, block),
        grid=(pairs,),
        in_specs=in_specs,
        out_specs=[
            pl.BlockSpec((rows, LANES), lambda p: (0, p)),
            pl.BlockSpec((1, 2, rows), lambda p: (p, 0, 0)),
        ],
        out_shape=[
            jax.ShapeDtypeStruct((rows, wide), jnp.float32),
            jax.ShapeDtypeStruct((pairs, 2, rows), jnp.float32),
        ],
        scratch_shapes=scratch,
        compiler_params=pltpu.CompilerParams(vmem_limit_bytes=32 * 1024 * 1024),
        cost_estimate=free(),
    )(*args)


def backward_kernel(
    causal, block, limit_ref, query_ref, key_ref, value_ref, grad_ref, mixed_ref, log_ref, *rest
):
    if causal:
        line_ref, gq_ref, gk_ref, gv_ref, table_ref, key_scr, key_t_scr, bias_scr, diag_scr, gk_scr, gv_scr = rest
    else:
        gq_ref, gk_ref, gv_ref, key_scr, key_t_scr, gk_scr, gv_scr = rest
    key_t_scr[...] = key_ref[...].T
    keys = key_marks(key_ref, limit_ref[0])
    for half in range(2):
        key_scr[half] = keys[half]
        if causal:
            bias_scr[half] = diagonal_bias(line_ref[0, half : half + 1, :])
            diag_scr[half] = jnp.zeros(diag_scr.shape[1:], jnp.float32)
    gk_scr[...] = jnp.zeros(gk_scr.shape, jnp.float32)
    gv_scr[...] = jnp.zeros(gv_scr.shape, jnp.float32)
    rows = query_ref.shape[0]
    key_total = key_ref.shape[0]
    width = query_ref.shape[1] // 2
    step = 2 * LANES
    def weigh(start, half):
        keys_here = min(key_total, start + block) if causal else key_total
        queries = query_ref[start : start + block, :]
        grads = grad_ref[start : start + block, :]
        product = (grads.astype(jnp.float32) * mixed_ref[start : start + block, :]).T
        inner = jnp.sum(product[half * width : (half + 1) * width], axis=0, keepdims=True)
        marked = with_mark(queries, half, 1.0)
        grads_here = only_head(grads, half)
        log_total = log_ref[0, half : half + 1, start : start + block]
        both = []
        for key_at in range(0, keys_here, step):
            here = slice(key_at, key_at + step)
            scores = dot(key_scr[half, here, :], marked, NT)
            if causal:
                lane_at = start - key_at + LANES
                scores = scores + jnp.concatenate(
                    [
                        bias_scr[half, :, lane_at : lane_at + block],
                        bias_scr[half, :, lane_at - LANES : lane_at - LANES + block],
                    ],
                    axis=0,
                )
            shares = jnp.exp(scores - log_total)
            grad_scores = shares * (dot(value_ref[here, :], grads_here, NT) - inner)
            if causal:
                diag_scr[half, :, lane_at : lane_at + block] += grad_scores[:LANES]
                diag_scr[half, :, lane_at - LANES : lane_at - LANES + block] += grad_scores[LANES:]
            both.append((shares.astype(jnp.bfloat16), grad_scores.astype(jnp.bfloat16)))
        return both, only_head(queries, half), grads_here

    def spread_back(half, both, plain, grads_here):
        total = None
        for number, (shares, grad_scores) in enumerate(both):
            here = slice(number * step, (number + 1) * step)
            gv_scr[here, :] += dot(shares, grads_here, NN)
            gk_scr[here, :] += dot(grad_scores, plain, NN)
            part = dot(key_t_scr[half * width : (half + 1) * width, here], grad_scores, NN)
            total = part if total is None else total + part
        return total

    units = [(start, half) for start in range(0, rows, block) for half in range(2)]
    query_parts = []
    waiting = weigh(*units[0])
    for number, (start, half) in enumerate(units):
        following = weigh(*units[number + 1]) if number + 1 < len(units) else None
        query_parts.append(spread_back(half, *waiting))
        waiting = following
        if half == 1:
            gq_ref[start : start + block, :] = (
                jnp.concatenate(query_parts, axis=0).T.astype(jnp.bfloat16)
            )
            query_parts = []
    gk_ref[...] = gk_scr[...].astype(jnp.bfloat16)
    gv_ref[...] = gv_scr[...].astype(jnp.bfloat16)
    if causal:
        lanes = diag_scr.shape[2]
        down = lax.broadcasted_iota(jnp.int32, (LANES, LANES), 0)
        across = lax.broadcasted_iota(jnp.int32, (LANES, LANES), 1)
        backwards = jnp.where(down + across == LANES - 1, 1.0, 0.0)
        for half in range(2):
            turned = lax.dot_general(
                backwards, diag_scr[half], NN, precision=lax.Precision.HIGHEST
            )
            straight = pltpu.roll(turned, lanes - LANES + 1, 1, stride=1, stride_axis=0)
            table_ref[0, half : half + 1, :] = jnp.sum(straight, axis=0, keepdims=True)


def attend_back(queries, keys, values, grads, mixed, logs, limit, lines):
    rows, wide = queries.shape
    key_total = keys.shape[0]
    pairs = wide // LANES
    causal = lines is not None
    block = min(256, rows)
    tall = pl.BlockSpec((rows, LANES), lambda p: (0, p))
    by_key = pl.BlockSpec((key_total, LANES), lambda p: (0, p))
    in_specs = [
        smem(),
        tall,
        by_key,
        by_key,
        tall,
        tall,
        pl.BlockSpec((1, 2, rows), lambda p: (p, 0, 0)),
    ]
    args = [limit, queries, keys, values, grads, mixed, logs]
    out_specs = [tall, by_key, by_key]
    out_shape = [
        jax.ShapeDtypeStruct((rows, wide), jnp.bfloat16),
        jax.ShapeDtypeStruct((key_total, wide), jnp.bfloat16),
        jax.ShapeDtypeStruct((key_total, wide), jnp.bfloat16),
    ]
    scratch = [
        pltpu.VMEM((2, key_total, LANES), jnp.bfloat16),
        pltpu.VMEM((LANES, key_total), jnp.bfloat16),
    ]
    if causal:
        lanes = lines.shape[2]
        in_specs.append(pl.BlockSpec((1, 2, lanes), lambda p: (p, 0, 0)))
        args.append(lines)
        out_specs.append(pl.BlockSpec((1, 2, lanes), lambda p: (p, 0, 0)))
        out_shape.append(jax.ShapeDtypeStruct((pairs, 2, lanes), jnp.float32))
        scratch += [pltpu.VMEM((2, LANES, lanes), jnp.float32)] * 2
    scratch += [pltpu.VMEM((key_total, LANES), jnp.float32)] * 2
    return pl.pallas_call(
        functools.partial(backward_kernel, causal, block),
        grid=(pairs,),
        in_specs=in_specs,
        out_specs=out_specs,
        out_shape=out_shape,
        scratch_shapes=scratch,
        compiler_params=pltpu.CompilerParams(vmem_limit_bytes=32 * 1024 * 1024),
        cost_estimate=free(),
    )(*args)


def bias_lines(distance_bucket, position_table):
    buckets, heads = position_table.shape
    total = distance_bucket.shape[0]
    hot = distance_bucket[:, None, None] == jnp.arange(buckets)[None, :, None]
    by_distance = jnp.sum(jnp.where(hot, position_table[None], 0.0), axis=1).T
    edge = jnp.full((heads, LANES), MASKED, jnp.float32)
    lines = jnp.concatenate([edge, by_distance, edge], axis=1)
    return lines.reshape(heads // 2, 2, total + 2 * LANES)


def table_grad(lines, distance_bucket, buckets):
    pairs, two, lanes = lines.shape
    by_distance = lines.reshape(pairs * two, lanes)[:, LANES : lanes - LANES]
    hot = distance_bucket[None, :] == jnp.arange(buckets)[:, None]
    return jnp.sum(jnp.where(hot[:, None, :], by_distance[None], 0.0), axis=-1)


def free():
    return pl.CostEstimate(flops=10**11, bytes_accessed=1, transcendentals=1)


def params():
    return pltpu.CompilerParams(vmem_limit_bytes=32 * 1024 * 1024)


def whole(shape):
    zeros = (0,) * len(shape)
    return pl.BlockSpec(shape, lambda i: zeros)


def norm_kernel(terms, products, *refs):
    parts = refs[:terms]
    gain_ref = refs[terms]
    weights = refs[terms + 1 : terms + 1 + products]
    outs = refs[terms + 1 + products :]
    hidden = parts[0][...].astype(jnp.float32)
    if terms > 1:
        hidden = hidden + sum(part[...] for part in parts[1:])
        outs[0][...] = hidden
        outs = outs[1:]
    inverse_rms = lax.rsqrt(jnp.mean(hidden * hidden, axis=-1, keepdims=True) + EPSILON)
    normed = (hidden * inverse_rms * gain_ref[...]).astype(jnp.bfloat16)
    outs[0][...] = normed
    for weight_ref, out_ref in zip(weights, outs[1:]):
        out_ref[...] = dot(normed, weight_ref[...], NN).astype(jnp.bfloat16)


def norm_forward(parts, gain, weights):
    rows, model_width = parts[0].shape
    block = min(256, rows)
    by_rows = pl.BlockSpec((block, model_width), lambda i: (i, 0))
    out_specs = []
    out_shape = []
    if len(parts) > 1:
        out_specs.append(by_rows)
        out_shape.append(jax.ShapeDtypeStruct((rows, model_width), jnp.float32))
    out_specs.append(by_rows)
    out_shape.append(jax.ShapeDtypeStruct((rows, model_width), jnp.bfloat16))
    for weight in weights:
        out_specs.append(pl.BlockSpec((block, weight.shape[1]), lambda i: (i, 0)))
        out_shape.append(jax.ShapeDtypeStruct((rows, weight.shape[1]), jnp.bfloat16))
    return pl.pallas_call(
        functools.partial(norm_kernel, len(parts), len(weights)),
        grid=(rows // block,),
        in_specs=[by_rows] * len(parts)
        + [whole((1, model_width))]
        + [whole(weight.shape) for weight in weights],
        out_specs=out_specs,
        out_shape=out_shape,
        compiler_params=params(),
        cost_estimate=free(),
    )(*parts, gain.reshape(1, model_width), *weights)


def norm_back_kernel(grads, deep, hidden_ref, gain_ref, before_ref, *refs):
    grad_refs = refs[:grads]
    refs = refs[grads:]
    if deep:
        weight_ref, grad_ref, low_ref, gain_grad_ref, back_ref = refs
    else:
        grad_ref, gain_grad_ref = refs
    hidden = hidden_ref[...].astype(jnp.float32)
    grad_normed = sum(ref[...] for ref in grad_refs)
    inverse_rms = lax.rsqrt(jnp.mean(hidden * hidden, axis=-1, keepdims=True) + EPSILON)
    straight = hidden * inverse_rms
    gain_part = jnp.sum(grad_normed * straight, axis=0, keepdims=True)

    @pl.when(pl.program_id(0) == 0)
    def _():
        gain_grad_ref[...] = gain_part

    @pl.when(pl.program_id(0) > 0)
    def _():
        gain_grad_ref[...] += gain_part

    scaled = grad_normed * gain_ref[...]
    inner = jnp.mean(scaled * straight, axis=-1, keepdims=True)
    grad = before_ref[...] + inverse_rms * (scaled - straight * inner)
    grad_ref[...] = grad
    if deep:
        rounded = grad.astype(jnp.bfloat16)
        low_ref[...] = rounded
        back_ref[...] = dot(rounded, weight_ref[...], NT).astype(jnp.bfloat16)


def norm_backward(hidden, gain, before, grads, weight):
    rows, model_width = hidden.shape
    block = min(256, rows)
    by_rows = pl.BlockSpec((block, model_width), lambda i: (i, 0))
    in_specs = [by_rows, whole((1, model_width)), by_rows] + [by_rows] * len(grads)
    args = [hidden, gain.reshape(1, model_width), before, *grads]
    out_specs = [by_rows]
    out_shape = [jax.ShapeDtypeStruct((rows, model_width), jnp.float32)]
    if weight is not None:
        in_specs.append(whole(weight.shape))
        args.append(weight)
        out_specs.append(by_rows)
        out_shape.append(jax.ShapeDtypeStruct((rows, model_width), jnp.bfloat16))
    out_specs.append(whole((1, model_width)))
    out_shape.append(jax.ShapeDtypeStruct((1, model_width), jnp.float32))
    if weight is not None:
        out_specs.append(pl.BlockSpec((block, weight.shape[0]), lambda i: (i, 0)))
        out_shape.append(jax.ShapeDtypeStruct((rows, weight.shape[0]), jnp.bfloat16))
    return pl.pallas_call(
        functools.partial(norm_back_kernel, len(grads), weight is not None),
        grid=(rows // block,),
        in_specs=in_specs,
        out_specs=out_specs,
        out_shape=out_shape,
        compiler_params=params(),
        cost_estimate=free(),
    )(*args)


ROOT = 0.7978845608028654
CUBE = 0.044715


def hidden_kernel(block, input_ref, grad_ref, inward_ref, outward_ref, active_ref, back_ref):
    rows = input_ref.shape[0]
    for start in range(0, rows, block):
        here = slice(start, start + block)
        before = dot(input_ref[here, :], inward_ref[...], NN)
        grad_active = dot(grad_ref[here, :], outward_ref[...], NT)
        square = before * before
        bent = jnp.tanh(ROOT * before * (1.0 + CUBE * square))
        half = 0.5 * (1.0 + bent)
        active_ref[here, :] = (before * half).astype(jnp.bfloat16)
        slope = half + 0.5 * before * (1.0 - bent * bent) * (
            ROOT + (3.0 * CUBE * ROOT) * square
        )
        back_ref[here, :] = (grad_active * slope).astype(jnp.bfloat16)


def hidden_both(inputs, grads, inward, outward):
    rows, model_width = inputs.shape
    hidden = inward.shape[1]
    block = min(512, hidden)
    by_hidden = pl.BlockSpec((rows, block), lambda i: (0, i))
    return pl.pallas_call(
        functools.partial(hidden_kernel, min(256, rows)),
        grid=(hidden // block,),
        in_specs=[
            whole(inputs.shape),
            whole(grads.shape),
            pl.BlockSpec((model_width, block), lambda i: (0, i)),
            pl.BlockSpec((block, model_width), lambda i: (i, 0)),
        ],
        out_specs=[by_hidden, by_hidden],
        out_shape=[jax.ShapeDtypeStruct((rows, hidden), jnp.bfloat16)] * 2,
        compiler_params=params(),
        cost_estimate=free(),
    )(inputs, grads, inward, outward)


def products_kernel(groups, *refs):
    count = 2 * sum(groups)
    at = 0
    for out_ref, size in zip(refs[count:], groups):
        total = None
        for _ in range(size):
            former, latter = refs[at], refs[at + 1]
            turned = former.shape[1] != latter.shape[0] or latter.shape[0] == out_ref.shape[1]
            part = dot(former[...], latter[...], NT if turned else NN)
            total = part if total is None else total + part
            at += 2
        out_ref[...] = total


def products(*groups):
    rows = groups[0][0][0].shape[0]
    block = min(256, rows)
    in_specs = []
    args = []
    out_specs = []
    out_shape = []
    for group in groups:
        for former, latter in group:
            in_specs += [
                pl.BlockSpec((block, former.shape[1]), lambda i: (i, 0)),
                whole(latter.shape),
            ]
            args += [former, latter]
        inner = former.shape[1]
        width = latter.shape[1] if latter.shape[0] == inner else latter.shape[0]
        out_specs.append(pl.BlockSpec((block, width), lambda i: (i, 0)))
        out_shape.append(jax.ShapeDtypeStruct((rows, width), jnp.float32))
    return pl.pallas_call(
        functools.partial(products_kernel, tuple(len(group) for group in groups)),
        grid=(rows // block,),
        in_specs=in_specs,
        out_specs=out_specs,
        out_shape=out_shape,
        compiler_params=params(),
        cost_estimate=free(),
    )(*args)


TN = (((0,), (0,)), ((), ()))


def bits_call(kernel, bits, args, in_specs, out_specs, out_shape, steps):
    return pl.pallas_call(
        kernel,
        grid_spec=pltpu.PrefetchScalarGridSpec(
            num_scalar_prefetch=1, grid=(steps,), in_specs=in_specs, out_specs=out_specs
        ),
        out_shape=out_shape,
        compiler_params=params(),
        cost_estimate=free(),
    )(bits, *args)


def tiles_kernel(widths, bits_ref, *refs):
    column = 0
    for number, width in enumerate(widths):
        refs[-1][:, column : column + width] = dot(
            refs[2 * number][...], refs[2 * number + 1][...], TN
        )
        column += width


def half_grad(bits, mine, tiles, bit):
    in_specs = []
    args = []
    rows = tiles[0][0].shape[1] // 2
    for left, right in tiles:
        total, width = right.shape
        in_specs += [
            pl.BlockSpec((total, rows), lambda i, b: (0, b[bit] if mine else 1 - b[bit])),
            pl.BlockSpec((total, width), lambda i, b: (0, 0)),
        ]
        args += [left, right]
    widths = tuple(right.shape[1] for _, right in tiles)
    shape = (rows, sum(widths))
    return bits_call(
        functools.partial(tiles_kernel, widths),
        bits,
        args,
        in_specs,
        pl.BlockSpec(shape, lambda i, b: (0, 0)),
        jax.ShapeDtypeStruct(shape, jnp.float32),
        1,
    )


def whole_grads(tiles):
    return jnp.concatenate(
        [
            lax.dot_general(left, right, TN, preferred_element_type=jnp.float32)
            for left, right in tiles
        ],
        axis=1,
    )


def at_half(where, size):
    return pl.ds(pl.multiple_of(where * size, 8), size)


def by_columns(rows, block):
    return pl.BlockSpec((rows, block), lambda i, b: (0, i))


def split_kernel(bit, bits_ref, keep_ref, other_ref, send_ref, rest_ref):
    size = send_ref.shape[0]
    mine = bits_ref[bit]
    away = at_half(1 - mine, size)
    here = at_half(mine, size)
    send_ref[...] = keep_ref[away, :] + other_ref[away, :]
    rest_ref[...] = keep_ref[here, :] + other_ref[here, :]


def split_sum(bits, keep, other, bit):
    rows, columns = keep.shape
    block = columns // 2
    shape = jax.ShapeDtypeStruct((rows // 2, columns), jnp.float32)
    return bits_call(
        functools.partial(split_kernel, bit),
        bits,
        [keep, other],
        [by_columns(rows, block)] * 2,
        [by_columns(rows // 2, block)] * 2,
        [shape] * 2,
        2,
    )


def add_kernel(bits_ref, former, latter, out_ref):
    out_ref[...] = former[...] + latter[...]


def add_two(bits, former, latter):
    rows, columns = former.shape
    steps = 2 if rows > 96 else 1
    part = by_columns(rows, columns // steps)
    return bits_call(
        add_kernel,
        bits,
        [former, latter],
        [part] * 2,
        part,
        jax.ShapeDtypeStruct(former.shape, jnp.float32),
        steps,
    )


def join_kernel(bit, bits_ref, own_ref, other_ref, out_ref):
    size = own_ref.shape[0]
    out_ref[at_half(bits_ref[bit], size), :] = own_ref[...]
    out_ref[at_half(1 - bits_ref[bit], size), :] = other_ref[...]


def join(bits, own, other, bit):
    rows, columns = own.shape
    steps = 3 if rows > 96 else 1
    block = columns // steps
    return bits_call(
        functools.partial(join_kernel, bit),
        bits,
        [own, other],
        [by_columns(rows, block)] * 2,
        by_columns(2 * rows, block),
        jax.ShapeDtypeStruct((2 * rows, columns), jnp.float32),
        steps,
    )


def last_kernel(bit, bits_ref, own_ref, other_ref, *outs):
    size = own_ref.shape[0]
    width = outs[0].shape[1]
    for ref, where in ((own_ref, bits_ref[bit]), (other_ref, 1 - bits_ref[bit])):
        for number in range(3):
            outs[number][at_half(where, size), :] = ref[:, number * width : (number + 1) * width]
        turned = ref[:, 3 * width :].T

        @pl.when(where == 0)
        def _():
            outs[3][:, :size] = turned

        @pl.when(where == 1)
        def _():
            outs[3][:, size:] = turned


def join_four(bits, own, other, bit):
    rows, columns = own.shape
    width = columns // 4
    shapes = [(2 * rows, width)] * 3 + [(width, 2 * rows)]
    return bits_call(
        functools.partial(last_kernel, bit),
        bits,
        [own, other],
        [by_columns(rows, columns)] * 2,
        [pl.BlockSpec(shape, lambda i, b: (0, 0)) for shape in shapes],
        [jax.ShapeDtypeStruct(shape, jnp.float32) for shape in shapes],
        1,
    )


class Order:
    def __init__(self):
        self.last = None

    def after(self, *arrays):
        if self.last is not None:
            arrays = lax.optimization_barrier((*arrays, self.last))[:-1]
        return arrays if len(arrays) > 1 else arrays[0]

    def done(self, array):
        self.last = array
        return array


def core_swap(array):
    return lax.ppermute(array, "tensor", [(0, 1), (1, 0)])


FLIPS = ((1, 2), (2, 1), (4, 12), (8, 4))
KEPT = ((0, 1), (1, 0), (2, 3), (3, 2))
FLAT = ((0, 1, 2, 3), ())
FLAT_WHOLE = ((0, 1), (2, 3))
DEEP = ((2, 3, 0, 1), ())
DEEP_WHOLE = ((2, 3), (0, 1))


def kept_halves():
    chip = lax.axis_index("dp")
    core = lax.axis_index("tensor")
    shifts = jnp.array(KEPT, jnp.int32)
    return (chip >> jnp.where(core == 0, shifts[:, 0], shifts[:, 1])) & 1


def exchange(array, stage):
    pairs = [
        (2 * chip + core, 2 * (chip ^ FLIPS[stage][core]) + core)
        for chip in range(16)
        for core in range(2)
    ]
    return lax.ppermute(array, ("dp", "tensor"), pairs)


def sum_steps(order, bits, tiles, stages, form, result):
    halves, wholes = stages

    def gated():
        left, right = tiles[0]
        return [(order.after(left), right), *tiles[1:]]

    send = order.done(half_grad(bits, False, gated(), halves[0]))
    other = exchange(send, halves[0])
    yield
    rest = order.done(half_grad(bits, True, gated(), halves[0]))
    yield
    for stage in halves[1:]:
        send, rest = split_sum(bits, rest, order.after(other), stage)
        order.done(send)
        other = exchange(send, stage)
        yield
    for stage in wholes:
        rest = order.done(rest + order.after(other))
        other = exchange(rest, stage)
        yield
    own = order.done(rest + order.after(other))
    for stage in halves[:0:-1]:
        other = exchange(own, stage)
        yield
        own = order.done(join(bits, own, order.after(other), stage))
    other = exchange(own, halves[0])
    yield
    if form == "four":
        result.extend(join_four(bits, own, order.after(other), halves[0]))
    else:
        result.append(join(bits, own, order.after(other), halves[0]))
    order.done(result[0])
    yield


def small_steps(order, bits, array, result):
    for stage in FLAT[0]:
        array = order.done(array)
        other = exchange(array, stage)
        yield
        array = array + order.after(other)
    result.append(array)
    yield


def matrix_product(former, latter):
    return jnp.dot(former, latter, preferred_element_type=jnp.float32)


def left_contract(former, latter):
    return jnp.einsum("ti,tj->ij", former, latter, preferred_element_type=jnp.float32)


def right_contract(former, latter):
    return jnp.einsum("ti,ji->tj", former, latter, preferred_element_type=jnp.float32)


ROUTES = {"O": DEEP_WHOLE, "I": FLAT, "C": FLAT, "S": FLAT}
PLAN = (
    "O", "I", "Pga3", "O", "I", "NB3", "CB", "Pgi2", "C", "C", "I", "NB2", "O", "SB", "C",
    "I", "S", "Py3", "C", "I", "Lout", "O", "C", "S", "I", "S", "C", "I", "Penc", "O", "S",
    "Genc", "C", "I", "O", "Pga1", "S", "I", "NB1", "C", "m", "S", "C", "S", "O", "m", "S",
    "I", "S", "m", "C", "m", "S", "m", "O",
)


def body(
    decoder_input,
    encoder_output,
    cotangent,
    target_length,
    source_length,
    identifier_tags,
    distance_bucket,
    self_gain,
    self_query,
    self_attention_key,
    self_value,
    self_output,
    position_table,
    cross_gain,
    cross_query,
    cross_key,
    cross_value,
    cross_output,
    hidden_gain,
    hidden_in,
    hidden_out,
):
    item_count, target, model_width = decoder_input.shape
    source = encoder_output.shape[1]
    low = jnp.bfloat16
    cores = lax.axis_size("tensor")
    devices = lax.axis_size("dp")
    order = Order()
    by_hand = devices == 16 and cores == 2
    bits = kept_halves()

    def both(array):
        return [array, core_swap(array)] if cores == 2 else [lax.psum(array, "tensor")]

    def spread(tiles, stages, form="one"):
        result = []
        if by_hand:
            return sum_steps(order, bits, tiles, stages, form, result), result
        total = lax.psum(whole_grads(tiles), "dp")
        width = total.shape[1] // 4
        if form == "four":
            result += [total[:, i * width : (i + 1) * width] for i in range(3)]
            result.append(total[:, 3 * width :].T)
        else:
            result.append(total)
        return iter(()), result

    decoder_rows = decoder_input.reshape(item_count * target, model_width)
    encoder_rows = encoder_output.reshape(item_count * source, model_width)
    lines = bias_lines(distance_bucket, position_table)
    places = jnp.arange(target, dtype=jnp.int32)
    factor = jnp.where(
        places[None, :] < target_length[:, None], 1.0 + identifier_tags.astype(jnp.float32), 0.0
    )
    grad_third = (cotangent.astype(jnp.float32) * factor[:, :, None]).reshape(
        item_count * target, model_width
    )
    grad_branch = grad_third.astype(low)

    input_one, queries_one, keys_one, values_one = norm_forward(
        [decoder_rows], self_gain, [self_query, self_attention_key, self_value]
    )
    exact_one, logs_one = attend(queries_one, keys_one, values_one, target_length, lines)
    mixed_one = exact_one.astype(low)
    parts = both(matrix_product(mixed_one, self_output))
    first, input_two, queries_two = norm_forward(
        [decoder_rows, *parts], cross_gain, [cross_query]
    )
    keys_two = matrix_product(encoder_rows, cross_key).astype(low)
    values_two = matrix_product(encoder_rows, cross_value).astype(low)
    exact_two, logs_two = attend(queries_two, keys_two, values_two, source_length, None)
    mixed_two = exact_two.astype(low)
    parts = both(matrix_product(mixed_two, cross_output))
    second, input_three = norm_forward([first, *parts], hidden_gain, [])

    active, grad_before = hidden_both(input_three, grad_branch, hidden_in, hidden_out)
    held = {}
    sums = {}

    def products_three():
        (part,) = products([(order.after(grad_before), hidden_in)])
        held["grads_three"] = both(order.done(part))

    def back_three():
        held["second"], held["branch_two"], held["hidden_gain"], held["mixed_two"] = norm_backward(
            second, hidden_gain, order.after(grad_third), held["grads_three"], cross_output
        )
        order.done(held["second"])

    def back_cross():
        held["cross"] = attend_back(
            queries_two,
            keys_two,
            values_two,
            order.after(held["mixed_two"]),
            exact_two,
            logs_two,
            source_length,
            None,
        )
        order.done(held["cross"][0])
        begin(
            "C",
            [
                (input_two, held["cross"][0]),
                (encoder_rows, held["cross"][1]),
                (encoder_rows, held["cross"][2]),
                (held["branch_two"], mixed_two),
            ],
            "four",
        )

    def products_two():
        (part,) = products([(order.after(held["cross"][0]), cross_query)])
        held["grads_two"] = both(order.done(part))

    def back_two():
        held["first"], held["branch_one"], held["cross_gain"], held["mixed_one"] = norm_backward(
            first, cross_gain, order.after(held["second"]), held["grads_two"], self_output
        )
        order.done(held["mixed_one"])

    def back_self():
        held["self"] = attend_back(
            queries_one,
            keys_one,
            values_one,
            order.after(held["mixed_one"]),
            exact_one,
            logs_one,
            target_length,
            lines,
        )
        order.done(held["self"][0])
        begin(
            "S",
            [
                (input_one, held["self"][0]),
                (input_one, held["self"][1]),
                (input_one, held["self"][2]),
                (held["branch_one"], mixed_one),
            ],
            "four",
        )

    def products_one():
        (part,) = products(
            [
                (order.after(held["self"][0]), self_query),
                (held["self"][1], self_attention_key),
                (held["self"][2], self_value),
            ]
        )
        held["grads_one"] = both(order.done(part))

    def back_one():
        grad_decoder, held["self_gain"] = norm_backward(
            decoder_rows, self_gain, order.after(held["first"]), held["grads_one"], None
        )
        order.done(grad_decoder)
        held["decoder"] = grad_decoder.reshape(item_count, target, model_width)

    def products_encoder():
        (part,) = products(
            [(order.after(held["cross"][1]), cross_key), (held["cross"][2], cross_value)]
        )
        held["encoder_parts"] = both(order.done(part))

    def encoder_out():
        parts = order.after(*held["encoder_parts"], order.last)[:-1]
        held["encoder"] = order.done(sum(parts).reshape(item_count, source, model_width))

    def products_out():
        (part,) = products([(order.after(active), hidden_out)])
        held["parts_three"] = both(order.done(part))

    def layer_end():
        third = second + sum(order.after(*held["parts_three"], order.last)[:-1])
        held["layer_out"] = order.done(third.astype(low).reshape(item_count, target, model_width))

    def small_begin():
        flat = jnp.concatenate(
            [
                held["self_gain"].reshape(-1),
                held["cross_gain"].reshape(-1),
                held["hidden_gain"].reshape(-1),
                table_grad(held["self"][3], distance_bucket, position_table.shape[0]).reshape(-1),
            ]
        )
        lanes = 512
        flat = jnp.pad(flat, (0, -flat.shape[0] % (8 * lanes))).reshape(-1, lanes)
        flat = order.after(flat)
        if by_hand:
            sums["m"] = []
            return small_steps(order, bits, flat, sums["m"])
        sums["m"] = [lax.psum(flat, "dp")]
        return iter(())

    running = {}

    def begin(name, tiles, form="one"):
        running[name], sums[name] = spread(tiles, ROUTES[name], form)

    begin("O", [(active, grad_branch)])
    begin("I", [(input_three, grad_before)])
    work = dict(
        Pga3=products_three,
        NB3=back_three,
        CB=back_cross,
        Pgi2=products_two,
        NB2=back_two,
        SB=back_self,
        Pga1=products_one,
        NB1=back_one,
        Penc=products_encoder,
        Genc=encoder_out,
        Py3=products_out,
        Lout=layer_end,
    )
    for name in PLAN:
        if name in work:
            work[name]()
        else:
            if name == "m" and "m" not in running:
                running["m"] = small_begin()
            next(running[name], None)
    flat = sums["m"][0].reshape(-1)
    gains = [flat[i * model_width : (i + 1) * model_width] for i in range(3)]
    table = flat[3 * model_width : 3 * model_width + position_table.size].reshape(
        position_table.shape
    )
    return (
        held["layer_out"],
        held["decoder"],
        held["encoder"],
        gains[0],
        *sums["S"],
        table,
        gains[1],
        *sums["C"],
        gains[2],
        *sums["I"],
        *sums["O"],
    )


def solution(mesh):
    by_item = P("dp", None, None)
    columns = P(None, "tensor")
    rows = P("tensor", None)
    attention = (P(), columns, columns, columns, rows)
    return jax.shard_map(
        body,
        mesh=mesh,
        in_specs=(by_item, by_item, by_item, P("dp"), P("dp"), P("dp", None), P())
        + attention
        + (columns,)
        + attention
        + (P(), columns, rows),
        out_specs=(by_item, by_item, by_item)
        + attention
        + (columns,)
        + attention
        + (P(), columns, rows),
        check_vma=False,
    )
```

```python
import functools

import jax
import jax.numpy as jnp
from jax import lax
from jax.experimental import pallas as pl
from jax.experimental.pallas import tpu as pltpu
from jax.sharding import PartitionSpec as P

EPSILON = 1e-06
MASKED = -1e30
LANES = 128
NT = (((1,), (1,)), ((), ()))
NN = (((1,), (0,)), ((), ()))


def dot(a, b, dims):
    return lax.dot_general(a, b, dims, preferred_element_type=jnp.float32)


def head_lane_masks(rows, width, half):
    lane = lax.broadcasted_iota(jnp.int32, (rows, 2 * width), 1)
    return (lane < width) if half == 0 else (lane >= width)


def only_head(array, half):
    width = array.shape[1] // 2
    keep = head_lane_masks(array.shape[0], width, half)
    return jnp.where(keep, array.astype(jnp.float32), 0.0).astype(jnp.bfloat16)


def with_mark(array, half, mark):
    rows, both = array.shape
    width = both // 2
    lane = lax.broadcasted_iota(jnp.int32, (rows, both), 1)
    keep = (lane < width) if half == 0 else (lane >= width)
    place = width if half == 0 else 0
    other = jnp.where(lane == place, mark, 0.0)
    return jnp.where(keep, array.astype(jnp.float32), other).astype(jnp.bfloat16)


def key_marks(key_ref, limit):
    rows, both = key_ref.shape
    row = lax.broadcasted_iota(jnp.int32, (rows, both), 0)
    mark = jnp.where(row < limit, 0.0, MASKED)
    keys = key_ref[...]
    return [with_mark(keys, half, mark) for half in range(2)]


def diagonal_bias(line):
    wide = jnp.broadcast_to(line, (LANES, line.shape[1]))
    return pltpu.roll(wide, 0, 1, stride=1, stride_axis=0)


def forward_kernel(causal, block, limit_ref, query_ref, key_ref, value_ref, *rest):
    if causal:
        line_ref, out_ref, log_ref, key_scr, value_scr, bias_scr = rest
    else:
        out_ref, log_ref, key_scr, value_scr = rest
    value_scr[...] = value_ref[...].T
    keys = key_marks(key_ref, limit_ref[0])
    for half in range(2):
        key_scr[half] = keys[half]
        if causal:
            bias_scr[half] = diagonal_bias(line_ref[0, half : half + 1, :])
    rows = query_ref.shape[0]
    key_total = key_ref.shape[0]
    width = query_ref.shape[1] // 2
    step = 2 * LANES

    def scores_of(start, half):
        keys_here = min(key_total, start + block) if causal else key_total
        marked = with_mark(query_ref[start : start + block, :], half, 1.0)
        kept = []
        top = None
        for key_at in range(0, keys_here, step):
            scores = dot(key_scr[half, key_at : key_at + step, :], marked, NT)
            if causal:
                lane_at = start - key_at + LANES
                scores = scores + jnp.concatenate(
                    [
                        bias_scr[half, :, lane_at : lane_at + block],
                        bias_scr[half, :, lane_at - LANES : lane_at - LANES + block],
                    ],
                    axis=0,
                )
            kept.append(scores)
            here = jnp.max(scores, axis=0, keepdims=True)
            top = here if top is None else jnp.maximum(top, here)
        return kept, top

    def mix(start, half, kept, top):
        total = None
        for number, scores in enumerate(kept):
            here = slice(number * step, (number + 1) * step)
            raised = jnp.exp(scores - top)
            count = jnp.sum(raised, axis=0, keepdims=True)
            part = dot(
                value_scr[half * width : (half + 1) * width, here],
                raised.astype(jnp.bfloat16),
                NN,
            )
            total, mixed = (count, part) if total is None else (total + count, mixed + part)
        log_ref[0, half : half + 1, start : start + block] = top + jnp.log(total)
        return mixed / total

    units = [(start, half) for start in range(0, rows, block) for half in range(2)]
    outs = []
    waiting = scores_of(*units[0])
    for number, unit in enumerate(units):
        following = scores_of(*units[number + 1]) if number + 1 < len(units) else None
        outs.append(mix(*unit, *waiting))
        waiting = following
        if unit[1] == 1:
            out_ref[unit[0] : unit[0] + block, :] = jnp.concatenate(outs, axis=0).T
            outs = []


def smem():
    return pl.BlockSpec(memory_space=pltpu.SMEM)


def attend(queries, keys, values, limit, lines):
    rows, wide = queries.shape
    key_total = keys.shape[0]
    pairs = wide // LANES
    causal = lines is not None
    block = min(256, rows)
    in_specs = [
        smem(),
        pl.BlockSpec((rows, LANES), lambda p: (0, p)),
        pl.BlockSpec((key_total, LANES), lambda p: (0, p)),
        pl.BlockSpec((key_total, LANES), lambda p: (0, p)),
    ]
    scratch = [
        pltpu.VMEM((2, key_total, LANES), jnp.bfloat16),
        pltpu.VMEM((LANES, key_total), jnp.bfloat16),
    ]
    args = [limit, queries, keys, values]
    if causal:
        in_specs.append(pl.BlockSpec((1, 2, lines.shape[2]), lambda p: (p, 0, 0)))
        scratch.append(pltpu.VMEM((2, LANES, lines.shape[2]), jnp.float32))
        args.append(lines)
    return pl.pallas_call(
        functools.partial(forward_kernel, causal, block),
        grid=(pairs,),
        in_specs=in_specs,
        out_specs=[
            pl.BlockSpec((rows, LANES), lambda p: (0, p)),
            pl.BlockSpec((1, 2, rows), lambda p: (p, 0, 0)),
        ],
        out_shape=[
            jax.ShapeDtypeStruct((rows, wide), jnp.float32),
            jax.ShapeDtypeStruct((pairs, 2, rows), jnp.float32),
        ],
        scratch_shapes=scratch,
        compiler_params=pltpu.CompilerParams(vmem_limit_bytes=32 * 1024 * 1024),
        cost_estimate=free(),
    )(*args)


def backward_kernel(
    causal, block, limit_ref, query_ref, key_ref, value_ref, grad_ref, mixed_ref, log_ref, *rest
):
    if causal:
        line_ref, gq_ref, gk_ref, gv_ref, table_ref, key_scr, key_t_scr, bias_scr, diag_scr, gk_scr, gv_scr = rest
    else:
        gq_ref, gk_ref, gv_ref, key_scr, key_t_scr, gk_scr, gv_scr = rest
    key_t_scr[...] = key_ref[...].T
    keys = key_marks(key_ref, limit_ref[0])
    for half in range(2):
        key_scr[half] = keys[half]
        if causal:
            bias_scr[half] = diagonal_bias(line_ref[0, half : half + 1, :])
            diag_scr[half] = jnp.zeros(diag_scr.shape[1:], jnp.float32)
    gk_scr[...] = jnp.zeros(gk_scr.shape, jnp.float32)
    gv_scr[...] = jnp.zeros(gv_scr.shape, jnp.float32)
    rows = query_ref.shape[0]
    key_total = key_ref.shape[0]
    width = query_ref.shape[1] // 2
    step = 2 * LANES
    def weigh(start, half):
        keys_here = min(key_total, start + block) if causal else key_total
        queries = query_ref[start : start + block, :]
        grads = grad_ref[start : start + block, :]
        product = (grads.astype(jnp.float32) * mixed_ref[start : start + block, :]).T
        inner = jnp.sum(product[half * width : (half + 1) * width], axis=0, keepdims=True)
        marked = with_mark(queries, half, 1.0)
        grads_here = only_head(grads, half)
        log_total = log_ref[0, half : half + 1, start : start + block]
        both = []
        for key_at in range(0, keys_here, step):
            here = slice(key_at, key_at + step)
            scores = dot(key_scr[half, here, :], marked, NT)
            if causal:
                lane_at = start - key_at + LANES
                scores = scores + jnp.concatenate(
                    [
                        bias_scr[half, :, lane_at : lane_at + block],
                        bias_scr[half, :, lane_at - LANES : lane_at - LANES + block],
                    ],
                    axis=0,
                )
            shares = jnp.exp(scores - log_total)
            grad_scores = shares * (dot(value_ref[here, :], grads_here, NT) - inner)
            if causal:
                diag_scr[half, :, lane_at : lane_at + block] += grad_scores[:LANES]
                diag_scr[half, :, lane_at - LANES : lane_at - LANES + block] += grad_scores[LANES:]
            both.append((shares.astype(jnp.bfloat16), grad_scores.astype(jnp.bfloat16)))
        return both, only_head(queries, half), grads_here

    def spread_back(half, both, plain, grads_here):
        total = None
        for number, (shares, grad_scores) in enumerate(both):
            here = slice(number * step, (number + 1) * step)
            gv_scr[here, :] += dot(shares, grads_here, NN)
            gk_scr[here, :] += dot(grad_scores, plain, NN)
            part = dot(key_t_scr[half * width : (half + 1) * width, here], grad_scores, NN)
            total = part if total is None else total + part
        return total

    units = [(start, half) for start in range(0, rows, block) for half in range(2)]
    query_parts = []
    waiting = weigh(*units[0])
    for number, (start, half) in enumerate(units):
        following = weigh(*units[number + 1]) if number + 1 < len(units) else None
        query_parts.append(spread_back(half, *waiting))
        waiting = following
        if half == 1:
            gq_ref[start : start + block, :] = (
                jnp.concatenate(query_parts, axis=0).T.astype(jnp.bfloat16)
            )
            query_parts = []
    gk_ref[...] = gk_scr[...].astype(jnp.bfloat16)
    gv_ref[...] = gv_scr[...].astype(jnp.bfloat16)
    if causal:
        lanes = diag_scr.shape[2]
        down = lax.broadcasted_iota(jnp.int32, (LANES, LANES), 0)
        across = lax.broadcasted_iota(jnp.int32, (LANES, LANES), 1)
        backwards = jnp.where(down + across == LANES - 1, 1.0, 0.0)
        for half in range(2):
            turned = lax.dot_general(
                backwards, diag_scr[half], NN, precision=lax.Precision.HIGHEST
            )
            straight = pltpu.roll(turned, lanes - LANES + 1, 1, stride=1, stride_axis=0)
            table_ref[0, half : half + 1, :] = jnp.sum(straight, axis=0, keepdims=True)


def attend_back(queries, keys, values, grads, mixed, logs, limit, lines):
    rows, wide = queries.shape
    key_total = keys.shape[0]
    pairs = wide // LANES
    causal = lines is not None
    block = min(256, rows)
    tall = pl.BlockSpec((rows, LANES), lambda p: (0, p))
    by_key = pl.BlockSpec((key_total, LANES), lambda p: (0, p))
    in_specs = [
        smem(),
        tall,
        by_key,
        by_key,
        tall,
        tall,
        pl.BlockSpec((1, 2, rows), lambda p: (p, 0, 0)),
    ]
    args = [limit, queries, keys, values, grads, mixed, logs]
    out_specs = [tall, by_key, by_key]
    out_shape = [
        jax.ShapeDtypeStruct((rows, wide), jnp.bfloat16),
        jax.ShapeDtypeStruct((key_total, wide), jnp.bfloat16),
        jax.ShapeDtypeStruct((key_total, wide), jnp.bfloat16),
    ]
    scratch = [
        pltpu.VMEM((2, key_total, LANES), jnp.bfloat16),
        pltpu.VMEM((LANES, key_total), jnp.bfloat16),
    ]
    if causal:
        lanes = lines.shape[2]
        in_specs.append(pl.BlockSpec((1, 2, lanes), lambda p: (p, 0, 0)))
        args.append(lines)
        out_specs.append(pl.BlockSpec((1, 2, lanes), lambda p: (p, 0, 0)))
        out_shape.append(jax.ShapeDtypeStruct((pairs, 2, lanes), jnp.float32))
        scratch += [pltpu.VMEM((2, LANES, lanes), jnp.float32)] * 2
    scratch += [pltpu.VMEM((key_total, LANES), jnp.float32)] * 2
    return pl.pallas_call(
        functools.partial(backward_kernel, causal, block),
        grid=(pairs,),
        in_specs=in_specs,
        out_specs=out_specs,
        out_shape=out_shape,
        scratch_shapes=scratch,
        compiler_params=pltpu.CompilerParams(vmem_limit_bytes=32 * 1024 * 1024),
        cost_estimate=free(),
    )(*args)


def bias_lines(distance_bucket, position_table):
    buckets, heads = position_table.shape
    total = distance_bucket.shape[0]
    hot = distance_bucket[:, None, None] == jnp.arange(buckets)[None, :, None]
    by_distance = jnp.sum(jnp.where(hot, position_table[None], 0.0), axis=1).T
    edge = jnp.full((heads, LANES), MASKED, jnp.float32)
    lines = jnp.concatenate([edge, by_distance, edge], axis=1)
    return lines.reshape(heads // 2, 2, total + 2 * LANES)


def table_grad(lines, distance_bucket, buckets):
    pairs, two, lanes = lines.shape
    by_distance = lines.reshape(pairs * two, lanes)[:, LANES : lanes - LANES]
    hot = distance_bucket[None, :] == jnp.arange(buckets)[:, None]
    return jnp.sum(jnp.where(hot[:, None, :], by_distance[None], 0.0), axis=-1)


def free():
    return pl.CostEstimate(flops=10**11, bytes_accessed=1, transcendentals=1)


def params():
    return pltpu.CompilerParams(vmem_limit_bytes=32 * 1024 * 1024)


def whole(shape):
    zeros = (0,) * len(shape)
    return pl.BlockSpec(shape, lambda i: zeros)


def norm_kernel(terms, products, *refs):
    parts = refs[:terms]
    gain_ref = refs[terms]
    weights = refs[terms + 1 : terms + 1 + products]
    outs = refs[terms + 1 + products :]
    hidden = parts[0][...].astype(jnp.float32)
    if terms > 1:
        hidden = hidden + sum(part[...] for part in parts[1:])
        outs[0][...] = hidden
        outs = outs[1:]
    inverse_rms = lax.rsqrt(jnp.mean(hidden * hidden, axis=-1, keepdims=True) + EPSILON)
    normed = (hidden * inverse_rms * gain_ref[...]).astype(jnp.bfloat16)
    outs[0][...] = normed
    for weight_ref, out_ref in zip(weights, outs[1:]):
        out_ref[...] = dot(normed, weight_ref[...], NN).astype(jnp.bfloat16)


def norm_forward(parts, gain, weights):
    rows, model_width = parts[0].shape
    block = min(256, rows)
    by_rows = pl.BlockSpec((block, model_width), lambda i: (i, 0))
    out_specs = []
    out_shape = []
    if len(parts) > 1:
        out_specs.append(by_rows)
        out_shape.append(jax.ShapeDtypeStruct((rows, model_width), jnp.float32))
    out_specs.append(by_rows)
    out_shape.append(jax.ShapeDtypeStruct((rows, model_width), jnp.bfloat16))
    for weight in weights:
        out_specs.append(pl.BlockSpec((block, weight.shape[1]), lambda i: (i, 0)))
        out_shape.append(jax.ShapeDtypeStruct((rows, weight.shape[1]), jnp.bfloat16))
    return pl.pallas_call(
        functools.partial(norm_kernel, len(parts), len(weights)),
        grid=(rows // block,),
        in_specs=[by_rows] * len(parts)
        + [whole((1, model_width))]
        + [whole(weight.shape) for weight in weights],
        out_specs=out_specs,
        out_shape=out_shape,
        compiler_params=params(),
        cost_estimate=free(),
    )(*parts, gain.reshape(1, model_width), *weights)


def norm_back_kernel(grads, deep, hidden_ref, gain_ref, before_ref, *refs):
    grad_refs = refs[:grads]
    refs = refs[grads:]
    if deep:
        weight_ref, grad_ref, low_ref, gain_grad_ref, back_ref = refs
    else:
        grad_ref, gain_grad_ref = refs
    hidden = hidden_ref[...].astype(jnp.float32)
    grad_normed = sum(ref[...] for ref in grad_refs)
    inverse_rms = lax.rsqrt(jnp.mean(hidden * hidden, axis=-1, keepdims=True) + EPSILON)
    straight = hidden * inverse_rms
    gain_part = jnp.sum(grad_normed * straight, axis=0, keepdims=True)

    @pl.when(pl.program_id(0) == 0)
    def _():
        gain_grad_ref[...] = gain_part

    @pl.when(pl.program_id(0) > 0)
    def _():
        gain_grad_ref[...] += gain_part

    scaled = grad_normed * gain_ref[...]
    inner = jnp.mean(scaled * straight, axis=-1, keepdims=True)
    grad = before_ref[...] + inverse_rms * (scaled - straight * inner)
    grad_ref[...] = grad
    if deep:
        rounded = grad.astype(jnp.bfloat16)
        low_ref[...] = rounded
        back_ref[...] = dot(rounded, weight_ref[...], NT).astype(jnp.bfloat16)


def norm_backward(hidden, gain, before, grads, weight):
    rows, model_width = hidden.shape
    block = min(256, rows)
    by_rows = pl.BlockSpec((block, model_width), lambda i: (i, 0))
    in_specs = [by_rows, whole((1, model_width)), by_rows] + [by_rows] * len(grads)
    args = [hidden, gain.reshape(1, model_width), before, *grads]
    out_specs = [by_rows]
    out_shape = [jax.ShapeDtypeStruct((rows, model_width), jnp.float32)]
    if weight is not None:
        in_specs.append(whole(weight.shape))
        args.append(weight)
        out_specs.append(by_rows)
        out_shape.append(jax.ShapeDtypeStruct((rows, model_width), jnp.bfloat16))
    out_specs.append(whole((1, model_width)))
    out_shape.append(jax.ShapeDtypeStruct((1, model_width), jnp.float32))
    if weight is not None:
        out_specs.append(pl.BlockSpec((block, weight.shape[0]), lambda i: (i, 0)))
        out_shape.append(jax.ShapeDtypeStruct((rows, weight.shape[0]), jnp.bfloat16))
    return pl.pallas_call(
        functools.partial(norm_back_kernel, len(grads), weight is not None),
        grid=(rows // block,),
        in_specs=in_specs,
        out_specs=out_specs,
        out_shape=out_shape,
        compiler_params=params(),
        cost_estimate=free(),
    )(*args)


ROOT = 0.7978845608028654
CUBE = 0.044715


def hidden_kernel(block, input_ref, grad_ref, inward_ref, outward_ref, active_ref, back_ref):
    rows = input_ref.shape[0]
    for start in range(0, rows, block):
        here = slice(start, start + block)
        before = dot(input_ref[here, :], inward_ref[...], NN)
        grad_active = dot(grad_ref[here, :], outward_ref[...], NT)
        square = before * before
        bent = jnp.tanh(ROOT * before * (1.0 + CUBE * square))
        half = 0.5 * (1.0 + bent)
        active_ref[here, :] = (before * half).astype(jnp.bfloat16)
        slope = half + 0.5 * before * (1.0 - bent * bent) * (
            ROOT + (3.0 * CUBE * ROOT) * square
        )
        back_ref[here, :] = (grad_active * slope).astype(jnp.bfloat16)


def hidden_both(inputs, grads, inward, outward):
    rows, model_width = inputs.shape
    hidden = inward.shape[1]
    block = min(512, hidden)
    by_hidden = pl.BlockSpec((rows, block), lambda i: (0, i))
    return pl.pallas_call(
        functools.partial(hidden_kernel, min(256, rows)),
        grid=(hidden // block,),
        in_specs=[
            whole(inputs.shape),
            whole(grads.shape),
            pl.BlockSpec((model_width, block), lambda i: (0, i)),
            pl.BlockSpec((block, model_width), lambda i: (i, 0)),
        ],
        out_specs=[by_hidden, by_hidden],
        out_shape=[jax.ShapeDtypeStruct((rows, hidden), jnp.bfloat16)] * 2,
        compiler_params=params(),
        cost_estimate=free(),
    )(inputs, grads, inward, outward)


def products_kernel(groups, *refs):
    count = 2 * sum(groups)
    at = 0
    for out_ref, size in zip(refs[count:], groups):
        total = None
        for _ in range(size):
            former, latter = refs[at], refs[at + 1]
            turned = former.shape[1] != latter.shape[0] or latter.shape[0] == out_ref.shape[1]
            part = dot(former[...], latter[...], NT if turned else NN)
            total = part if total is None else total + part
            at += 2
        out_ref[...] = total


def products(*groups):
    rows = groups[0][0][0].shape[0]
    block = min(256, rows)
    in_specs = []
    args = []
    out_specs = []
    out_shape = []
    for group in groups:
        for former, latter in group:
            in_specs += [
                pl.BlockSpec((block, former.shape[1]), lambda i: (i, 0)),
                whole(latter.shape),
            ]
            args += [former, latter]
        inner = former.shape[1]
        width = latter.shape[1] if latter.shape[0] == inner else latter.shape[0]
        out_specs.append(pl.BlockSpec((block, width), lambda i: (i, 0)))
        out_shape.append(jax.ShapeDtypeStruct((rows, width), jnp.float32))
    return pl.pallas_call(
        functools.partial(products_kernel, tuple(len(group) for group in groups)),
        grid=(rows // block,),
        in_specs=in_specs,
        out_specs=out_specs,
        out_shape=out_shape,
        compiler_params=params(),
        cost_estimate=free(),
    )(*args)


TN = (((0,), (0,)), ((), ()))


def bits_call(kernel, bits, args, in_specs, out_specs, out_shape, steps):
    return pl.pallas_call(
        kernel,
        grid_spec=pltpu.PrefetchScalarGridSpec(
            num_scalar_prefetch=1, grid=(steps,), in_specs=in_specs, out_specs=out_specs
        ),
        out_shape=out_shape,
        compiler_params=params(),
        cost_estimate=free(),
    )(bits, *args)


def tiles_kernel(widths, bits_ref, *refs):
    column = 0
    for number, width in enumerate(widths):
        refs[-1][:, column : column + width] = dot(
            refs[2 * number][...], refs[2 * number + 1][...], TN
        )
        column += width


def half_grad(bits, mine, tiles, bit):
    in_specs = []
    args = []
    rows = tiles[0][0].shape[1] // 2
    for left, right in tiles:
        total, width = right.shape
        in_specs += [
            pl.BlockSpec((total, rows), lambda i, b: (0, b[bit] if mine else 1 - b[bit])),
            pl.BlockSpec((total, width), lambda i, b: (0, 0)),
        ]
        args += [left, right]
    widths = tuple(right.shape[1] for _, right in tiles)
    shape = (rows, sum(widths))
    return bits_call(
        functools.partial(tiles_kernel, widths),
        bits,
        args,
        in_specs,
        pl.BlockSpec(shape, lambda i, b: (0, 0)),
        jax.ShapeDtypeStruct(shape, jnp.float32),
        1,
    )


def whole_grads(tiles):
    return jnp.concatenate(
        [
            lax.dot_general(left, right, TN, preferred_element_type=jnp.float32)
            for left, right in tiles
        ],
        axis=1,
    )


def at_half(where, size):
    return pl.ds(pl.multiple_of(where * size, 8), size)


def by_columns(rows, block):
    return pl.BlockSpec((rows, block), lambda i, b: (0, i))


def split_kernel(bit, bits_ref, keep_ref, other_ref, send_ref, rest_ref):
    size = send_ref.shape[0]
    mine = bits_ref[bit]
    away = at_half(1 - mine, size)
    here = at_half(mine, size)
    send_ref[...] = keep_ref[away, :] + other_ref[away, :]
    rest_ref[...] = keep_ref[here, :] + other_ref[here, :]


def split_sum(bits, keep, other, bit):
    rows, columns = keep.shape
    block = columns // 2
    shape = jax.ShapeDtypeStruct((rows // 2, columns), jnp.float32)
    return bits_call(
        functools.partial(split_kernel, bit),
        bits,
        [keep, other],
        [by_columns(rows, block)] * 2,
        [by_columns(rows // 2, block)] * 2,
        [shape] * 2,
        2,
    )


def add_kernel(bits_ref, former, latter, out_ref):
    out_ref[...] = former[...] + latter[...]


def add_two(bits, former, latter):
    rows, columns = former.shape
    steps = 2 if rows > 96 else 1
    part = by_columns(rows, columns // steps)
    return bits_call(
        add_kernel,
        bits,
        [former, latter],
        [part] * 2,
        part,
        jax.ShapeDtypeStruct(former.shape, jnp.float32),
        steps,
    )


def join_kernel(bit, bits_ref, own_ref, other_ref, out_ref):
    size = own_ref.shape[0]
    out_ref[at_half(bits_ref[bit], size), :] = own_ref[...]
    out_ref[at_half(1 - bits_ref[bit], size), :] = other_ref[...]


def join(bits, own, other, bit):
    rows, columns = own.shape
    steps = 3 if rows > 96 else 1
    block = columns // steps
    return bits_call(
        functools.partial(join_kernel, bit),
        bits,
        [own, other],
        [by_columns(rows, block)] * 2,
        by_columns(2 * rows, block),
        jax.ShapeDtypeStruct((2 * rows, columns), jnp.float32),
        steps,
    )


def last_kernel(bit, bits_ref, own_ref, other_ref, *outs):
    size = own_ref.shape[0]
    width = outs[0].shape[1]
    for ref, where in ((own_ref, bits_ref[bit]), (other_ref, 1 - bits_ref[bit])):
        for number in range(3):
            outs[number][at_half(where, size), :] = ref[:, number * width : (number + 1) * width]
        turned = ref[:, 3 * width :].T

        @pl.when(where == 0)
        def _():
            outs[3][:, :size] = turned

        @pl.when(where == 1)
        def _():
            outs[3][:, size:] = turned


def join_four(bits, own, other, bit):
    rows, columns = own.shape
    width = columns // 4
    shapes = [(2 * rows, width)] * 3 + [(width, 2 * rows)]
    return bits_call(
        functools.partial(last_kernel, bit),
        bits,
        [own, other],
        [by_columns(rows, columns)] * 2,
        [pl.BlockSpec(shape, lambda i, b: (0, 0)) for shape in shapes],
        [jax.ShapeDtypeStruct(shape, jnp.float32) for shape in shapes],
        1,
    )


class Order:
    def __init__(self):
        self.last = None

    def after(self, *arrays):
        if self.last is not None:
            arrays = lax.optimization_barrier((*arrays, self.last))[:-1]
        return arrays if len(arrays) > 1 else arrays[0]

    def done(self, array):
        self.last = array
        return array


def core_swap(array):
    return lax.ppermute(array, "tensor", [(0, 1), (1, 0)])


FLIPS = ((1, 2), (2, 1), (4, 12), (8, 4))
KEPT = ((0, 1), (1, 0), (2, 3), (3, 2))
FLAT = ((0, 1, 2, 3), ())
FLAT_WHOLE = ((0, 1), (2, 3))
DEEP = ((2, 3, 0, 1), ())
DEEP_WHOLE = ((2, 3), (0, 1))


def kept_halves():
    chip = lax.axis_index("dp")
    core = lax.axis_index("tensor")
    shifts = jnp.array(KEPT, jnp.int32)
    return (chip >> jnp.where(core == 0, shifts[:, 0], shifts[:, 1])) & 1


def exchange(array, stage):
    pairs = [
        (2 * chip + core, 2 * (chip ^ FLIPS[stage][core]) + core)
        for chip in range(16)
        for core in range(2)
    ]
    return lax.ppermute(array, ("dp", "tensor"), pairs)


def sum_steps(order, bits, tiles, stages, form, result):
    halves, wholes = stages

    def gated():
        left, right = tiles[0]
        return [(order.after(left), right), *tiles[1:]]

    send = order.done(half_grad(bits, False, gated(), halves[0]))
    other = exchange(send, halves[0])
    yield
    rest = order.done(half_grad(bits, True, gated(), halves[0]))
    yield
    for stage in halves[1:]:
        send, rest = split_sum(bits, rest, order.after(other), stage)
        order.done(send)
        other = exchange(send, stage)
        yield
    for stage in wholes:
        rest = order.done(rest + order.after(other))
        other = exchange(rest, stage)
        yield
    own = order.done(rest + order.after(other))
    for stage in halves[:0:-1]:
        other = exchange(own, stage)
        yield
        own = order.done(join(bits, own, order.after(other), stage))
    other = exchange(own, halves[0])
    yield
    if form == "four":
        result.extend(join_four(bits, own, order.after(other), halves[0]))
    else:
        result.append(join(bits, own, order.after(other), halves[0]))
    order.done(result[0])
    yield


def small_steps(order, bits, array, result):
    for stage in FLAT[0]:
        array = order.done(array)
        other = exchange(array, stage)
        yield
        array = array + order.after(other)
    result.append(array)
    yield


def matrix_product(former, latter):
    return jnp.dot(former, latter, preferred_element_type=jnp.float32)


def left_contract(former, latter):
    return jnp.einsum("ti,tj->ij", former, latter, preferred_element_type=jnp.float32)


def right_contract(former, latter):
    return jnp.einsum("ti,ji->tj", former, latter, preferred_element_type=jnp.float32)


ROUTES = {"O": DEEP_WHOLE, "I": FLAT, "C": FLAT, "S": FLAT}
PLAN = (
    "Pga3", "O", "I", "O", "I", "NB3", "CB", "Pgi2", "C", "C", "I", "NB2", "O", "SB", "C",
    "I", "S", "Py3", "C", "I", "Lout", "O", "C", "S", "I", "S", "C", "I", "Penc", "O", "S",
    "Genc", "C", "I", "O", "Pga1", "S", "I", "NB1", "C", "m", "S", "C", "m", "S", "m", "O",
    "S", "I", "S", "C", "m", "S", "m", "O",
)


def body(
    decoder_input,
    encoder_output,
    cotangent,
    target_length,
    source_length,
    identifier_tags,
    distance_bucket,
    self_gain,
    self_query,
    self_attention_key,
    self_value,
    self_output,
    position_table,
    cross_gain,
    cross_query,
    cross_key,
    cross_value,
    cross_output,
    hidden_gain,
    hidden_in,
    hidden_out,
):
    item_count, target, model_width = decoder_input.shape
    source = encoder_output.shape[1]
    low = jnp.bfloat16
    cores = lax.axis_size("tensor")
    devices = lax.axis_size("dp")
    order = Order()
    by_hand = devices == 16 and cores == 2
    bits = kept_halves()

    def both(array):
        return [array, core_swap(array)] if cores == 2 else [lax.psum(array, "tensor")]

    def spread(tiles, stages, form="one"):
        result = []
        if by_hand:
            return sum_steps(order, bits, tiles, stages, form, result), result
        total = lax.psum(whole_grads(tiles), "dp")
        width = total.shape[1] // 4
        if form == "four":
            result += [total[:, i * width : (i + 1) * width] for i in range(3)]
            result.append(total[:, 3 * width :].T)
        else:
            result.append(total)
        return iter(()), result

    decoder_rows = decoder_input.reshape(item_count * target, model_width)
    encoder_rows = encoder_output.reshape(item_count * source, model_width)
    lines = bias_lines(distance_bucket, position_table)
    places = jnp.arange(target, dtype=jnp.int32)
    factor = jnp.where(
        places[None, :] < target_length[:, None], 1.0 + identifier_tags.astype(jnp.float32), 0.0
    )
    grad_third = (cotangent.astype(jnp.float32) * factor[:, :, None]).reshape(
        item_count * target, model_width
    )
    grad_branch = grad_third.astype(low)

    input_one, queries_one, keys_one, values_one = norm_forward(
        [decoder_rows], self_gain, [self_query, self_attention_key, self_value]
    )
    exact_one, logs_one = attend(queries_one, keys_one, values_one, target_length, lines)
    mixed_one = exact_one.astype(low)
    parts = both(matrix_product(mixed_one, self_output))
    first, input_two, queries_two = norm_forward(
        [decoder_rows, *parts], cross_gain, [cross_query]
    )
    keys_two = matrix_product(encoder_rows, cross_key).astype(low)
    values_two = matrix_product(encoder_rows, cross_value).astype(low)
    exact_two, logs_two = attend(queries_two, keys_two, values_two, source_length, None)
    mixed_two = exact_two.astype(low)
    parts = both(matrix_product(mixed_two, cross_output))
    second, input_three = norm_forward([first, *parts], hidden_gain, [])

    active, grad_before = hidden_both(input_three, grad_branch, hidden_in, hidden_out)
    held = {}
    sums = {}

    def products_three():
        (part,) = products([(order.after(grad_before), hidden_in)])
        held["grads_three"] = both(order.done(part))

    def back_three():
        held["second"], held["branch_two"], held["hidden_gain"], held["mixed_two"] = norm_backward(
            second, hidden_gain, order.after(grad_third), held["grads_three"], cross_output
        )
        order.done(held["second"])

    def back_cross():
        held["cross"] = attend_back(
            queries_two,
            keys_two,
            values_two,
            order.after(held["mixed_two"]),
            exact_two,
            logs_two,
            source_length,
            None,
        )
        order.done(held["cross"][0])
        begin(
            "C",
            [
                (input_two, held["cross"][0]),
                (encoder_rows, held["cross"][1]),
                (encoder_rows, held["cross"][2]),
                (held["branch_two"], mixed_two),
            ],
            "four",
        )

    def products_two():
        (part,) = products([(order.after(held["cross"][0]), cross_query)])
        held["grads_two"] = both(order.done(part))

    def back_two():
        held["first"], held["branch_one"], held["cross_gain"], held["mixed_one"] = norm_backward(
            first, cross_gain, order.after(held["second"]), held["grads_two"], self_output
        )
        order.done(held["mixed_one"])

    def back_self():
        held["self"] = attend_back(
            queries_one,
            keys_one,
            values_one,
            order.after(held["mixed_one"]),
            exact_one,
            logs_one,
            target_length,
            lines,
        )
        order.done(held["self"][0])
        begin(
            "S",
            [
                (input_one, held["self"][0]),
                (input_one, held["self"][1]),
                (input_one, held["self"][2]),
                (held["branch_one"], mixed_one),
            ],
            "four",
        )

    def products_one():
        (part,) = products(
            [
                (order.after(held["self"][0]), self_query),
                (held["self"][1], self_attention_key),
                (held["self"][2], self_value),
            ]
        )
        held["grads_one"] = both(order.done(part))

    def back_one():
        grad_decoder, held["self_gain"] = norm_backward(
            decoder_rows, self_gain, order.after(held["first"]), held["grads_one"], None
        )
        order.done(grad_decoder)
        held["decoder"] = grad_decoder.reshape(item_count, target, model_width)

    def products_encoder():
        (part,) = products(
            [(order.after(held["cross"][1]), cross_key), (held["cross"][2], cross_value)]
        )
        held["encoder_parts"] = both(order.done(part))

    def encoder_out():
        parts = order.after(*held["encoder_parts"], order.last)[:-1]
        held["encoder"] = order.done(sum(parts).reshape(item_count, source, model_width))

    def products_out():
        (part,) = products([(order.after(active), hidden_out)])
        held["parts_three"] = both(order.done(part))

    def layer_end():
        third = second + sum(order.after(*held["parts_three"], order.last)[:-1])
        held["layer_out"] = order.done(third.astype(low).reshape(item_count, target, model_width))

    def small_begin():
        flat = jnp.concatenate(
            [
                held["self_gain"].reshape(-1),
                held["cross_gain"].reshape(-1),
                held["hidden_gain"].reshape(-1),
                table_grad(held["self"][3], distance_bucket, position_table.shape[0]).reshape(-1),
            ]
        )
        lanes = 512
        flat = jnp.pad(flat, (0, -flat.shape[0] % (8 * lanes))).reshape(-1, lanes)
        flat = order.after(flat)
        if by_hand:
            sums["m"] = []
            return small_steps(order, bits, flat, sums["m"])
        sums["m"] = [lax.psum(flat, "dp")]
        return iter(())

    running = {}

    def begin(name, tiles, form="one"):
        running[name], sums[name] = spread(tiles, ROUTES[name], form)

    begin("O", [(active, grad_branch)])
    begin("I", [(input_three, grad_before)])
    work = dict(
        Pga3=products_three,
        NB3=back_three,
        CB=back_cross,
        Pgi2=products_two,
        NB2=back_two,
        SB=back_self,
        Pga1=products_one,
        NB1=back_one,
        Penc=products_encoder,
        Genc=encoder_out,
        Py3=products_out,
        Lout=layer_end,
    )
    for name in PLAN:
        if name in work:
            work[name]()
        else:
            if name == "m" and "m" not in running:
                running["m"] = small_begin()
            next(running[name], None)
    flat = sums["m"][0].reshape(-1)
    gains = [flat[i * model_width : (i + 1) * model_width] for i in range(3)]
    table = flat[3 * model_width : 3 * model_width + position_table.size].reshape(
        position_table.shape
    )
    return (
        held["layer_out"],
        held["decoder"],
        held["encoder"],
        gains[0],
        *sums["S"],
        table,
        gains[1],
        *sums["C"],
        gains[2],
        *sums["I"],
        *sums["O"],
    )


def solution(mesh):
    by_item = P("dp", None, None)
    columns = P(None, "tensor")
    rows = P("tensor", None)
    attention = (P(), columns, columns, columns, rows)
    return jax.shard_map(
        body,
        mesh=mesh,
        in_specs=(by_item, by_item, by_item, P("dp"), P("dp"), P("dp", None), P())
        + attention
        + (columns,)
        + attention
        + (P(), columns, rows),
        out_specs=(by_item, by_item, by_item)
        + attention
        + (columns,)
        + attention
        + (P(), columns, rows),
        check_vma=False,
    )
```
